32 devices in a mesh: clip: 2 (over x), tile: 16 (over z, y, core).
Axes of the slice: x: 2, y: 2, z: 4, core: 2. Of those that a mesh axis runs over, the one named last changes fastest.
Arguments:
- frames: bfloat16 [8, 32, 128, 1024], P('clip', 'tile'), parts along dimension 0, may hold values from -40 to 40
- keyframes: bfloat16 [4, 32, 128, 1024], P('clip', 'tile'), parts along dimension 0, may hold values from -40 to 40
- matches: int32 [16, 8, 4], P('tile', 'clip'), parts along dimension 1, may hold values from 0 to 5, as said below
- counts: int32 [16, 8], P('tile', 'clip'), parts along dimension 1, may hold values from 1 to 4, as said below
- w_query: bfloat16 [1024, 1024], replicated, may hold values from -1 to 1
- w_key: bfloat16 [1024, 1024], replicated, may hold values from -1 to 1
- w_value: bfloat16 [1024, 1024], replicated, may hold values from -0.1875 to 0.1875
- w_out: bfloat16 [1024, 1024], replicated, may hold values from -0.1875 to 0.1875
Outputs:
- mixed: bfloat16 [8, 32, 128, 1024], P('clip', None, 'tile'), parts along dimension 0
The draws below stay inside these ranges and needn't reach their ends.
There are 2 independent parts, one for each index of `clip`. The reference program is written for one: setup_inputs(seed, part) draws one part's arguments, and reference() takes and returns one part's arrays. A program takes and returns all parts, laid end to end along the dimension named above; an argument that names none is the same for every part. Nothing has to cross between parts.
Inputs may be any that keep to these rules, and one draw needn't show every extreme that they name: `matches`: every entry names a candidate whose block lies inside the image; the entries of one list are distinct, and entry 0 is candidate 1 (keyframe 0's block at the reader's own tile). Entries past the count are valid but unused. `counts`: in every frame some tile uses 4 entries.
All inputs are finite; a program needn't handle non-finite values.
Results may differ from the reference program's by a relative error of at most 0.0095.
Values may be sent and summed in bfloat16 or wider, within the bound.
A program may use at most 128 MiB of HBM per device.

```python
import jax
import jax.numpy as jnp
from jax import lax

D = 1024
HEADS = 16
W = 128
ROWS_DEV = 2
H = 32
FRAMES = 4
KEYS = 2
MAXM = 4
N_TILE = 16


def latent_pair(key):
    base_key = jax.random.fold_in(key, 11)
    frame_key, still_key = jax.random.split(base_key, 2)
    frame_vals = jax.random.normal(frame_key, (FRAMES, H, W, D), jnp.float32)
    still_vals = jax.random.normal(still_key, (KEYS, H, W, D), jnp.float32)
    return (frame_vals, still_vals)


def draw_frames(key, part):
    return latent_pair(key)[0].astype(jnp.bfloat16)


def draw_keyframes(key, part):
    return latent_pair(key)[1].astype(jnp.bfloat16)


def weight_pair(key):
    base_key = jax.random.fold_in(key, 23)
    first_key, second_key = jax.random.split(base_key, 2)
    first_w = jnp.clip(jax.random.normal(first_key, (D, D), jnp.float32), -5.0, 5.0) * D ** (-0.5)
    noise_w = jnp.clip(jax.random.normal(second_key, (D, D), jnp.float32), -5.0, 5.0) * D ** (-0.5)
    second_w = noise_w
    return (first_w, second_w)


def draw_w_query(key, part):
    return weight_pair(key)[0].astype(jnp.bfloat16)


def draw_w_key(key, part):
    return weight_pair(key)[1].astype(jnp.bfloat16)


def draw_matches(key, part):
    match_key = jax.random.fold_in(key, 31)
    cand_total = 3 * KEYS
    scores = jax.random.randint(match_key, (N_TILE, FRAMES, cand_total), 0, 4096, dtype=jnp.int32)
    numbers = jnp.arange(cand_total, dtype=jnp.int32)
    scores = scores * cand_total + numbers[None, None, :]
    tile_ids = jnp.arange(N_TILE, dtype=jnp.int32)[:, None, None]
    target = tile_ids + numbers[None, None, :] % 3 - 1
    inside = (target >= 0) & (target < N_TILE)
    scores = jnp.where(inside, scores + 1, 0)
    scores = jnp.where(numbers[None, None, :] == 1, 4096 * cand_total + 10, scores)
    picked = lax.top_k(scores, MAXM)[1]
    return picked.astype(jnp.int32)


def draw_counts(key, part):
    count_key, busy_key = jax.random.split(jax.random.fold_in(key, 41), 2)
    drawn = jax.random.randint(count_key, (N_TILE, FRAMES), 1, MAXM + 1, dtype=jnp.int32)
    busiest = jax.random.randint(busy_key, (FRAMES,), 0, N_TILE, dtype=jnp.int32)
    tile_ids = jnp.arange(N_TILE, dtype=jnp.int32)[:, None]
    return jnp.where(tile_ids == busiest[None, :], MAXM, drawn).astype(jnp.int32)


def gaussian(key, extent, width, most, kind=jnp.bfloat16):
    return jnp.clip(width * jax.random.normal(key, extent, jnp.float32), -most, most).astype(kind)


def setup_inputs(seed: int = 0, part: int = 0) -> dict:
    splits = jax.random.split(jax.random.key(seed), 9)
    part_splits = jax.random.split(jax.random.fold_in(splits[8], part), 9)
    frames = draw_frames(jax.random.fold_in(jax.random.fold_in(splits[8], part), 71), part)
    keyframes = draw_keyframes(jax.random.fold_in(jax.random.fold_in(splits[8], part), 71), part)
    matches = draw_matches(jax.random.fold_in(jax.random.fold_in(splits[8], part), 71), part)
    counts = draw_counts(jax.random.fold_in(jax.random.fold_in(splits[8], part), 71), part)
    w_query = draw_w_query(jax.random.fold_in(splits[8], 71), part)
    w_key = draw_w_key(jax.random.fold_in(splits[8], 71), part)
    w_value = gaussian(splits[6], (D, D), D ** -0.5, 0.1875)
    w_out = gaussian(splits[7], (D, D), D ** -0.5, 0.1875)
    return {"frames": frames, "keyframes": keyframes, "matches": matches, "counts": counts, "w_query": w_query, "w_key": w_key, "w_value": w_value, "w_out": w_out}


def attend(queries, keys, values, allowed):
    block_len = queries.shape[0]
    head_dim = D // HEADS
    q_heads = queries.reshape(block_len, HEADS, head_dim).astype(jnp.float32)
    k_heads = keys.reshape(-1, HEADS, head_dim).astype(jnp.float32)
    v_heads = values.reshape(-1, HEADS, head_dim).astype(jnp.float32)
    scores = jnp.einsum('qhd,khd->hqk', q_heads, k_heads) * (head_dim ** -0.5)
    scores = jnp.where(allowed[None, None, :], scores, -jnp.inf)
    row_max = jnp.max(scores, axis=-1, keepdims=True)
    exp_terms = jnp.exp(scores - row_max)
    probabilities = (exp_terms / jnp.sum(exp_terms, axis=-1, keepdims=True)).astype(jnp.bfloat16)
    context = jnp.einsum('hqk,khd->qhd', probabilities.astype(jnp.float32), v_heads)
    return context.astype(jnp.bfloat16).reshape(block_len, D)


def reference(frames, keyframes, matches, counts, w_query, w_key, w_value, w_out):
    block_len = ROWS_DEV * W
    query = jnp.dot(frames.reshape(-1, D), w_query, preferred_element_type=jnp.float32).astype(jnp.bfloat16)
    query = query.reshape(FRAMES, N_TILE, block_len, D)
    flat_keys = keyframes.reshape(-1, D)
    key_all = jnp.dot(flat_keys, w_key, preferred_element_type=jnp.float32).astype(jnp.bfloat16)
    value_all = jnp.dot(flat_keys, w_value, preferred_element_type=jnp.float32).astype(jnp.bfloat16)
    key_all = key_all.reshape(KEYS, N_TILE, block_len, D)
    value_all = value_all.reshape(KEYS, N_TILE, block_len, D)
    zero_pad = jnp.zeros((KEYS, 1, block_len, D), jnp.bfloat16)
    key_table = jnp.concatenate([zero_pad, key_all, zero_pad], axis=1)
    value_table = jnp.concatenate([zero_pad, value_all, zero_pad], axis=1)

    def per_item(position):
        tile_id = position // FRAMES
        frame_id = position % FRAMES
        queries = query[frame_id, tile_id]
        candidates = matches[tile_id, frame_id]
        key_id = (candidates // 3).astype(jnp.int32)
        block_id = (tile_id + candidates % 3).astype(jnp.int32)
        keys = key_table[key_id, block_id].reshape(-1, D)
        values = value_table[key_id, block_id].reshape(-1, D)
        live = jnp.arange(MAXM, dtype=jnp.int32) < counts[tile_id, frame_id]
        allowed = jnp.repeat(live, block_len)
        return attend(queries, keys, values, allowed)

    context = lax.map(per_item, jnp.arange(N_TILE * FRAMES, dtype=jnp.int32))
    context = context.reshape(N_TILE, FRAMES, block_len, D).transpose(1, 0, 2, 3).reshape(-1, D)
    update = jnp.dot(context, w_out, preferred_element_type=jnp.float32)
    mixed = frames.reshape(-1, D).astype(jnp.float32) + update
    return mixed.astype(jnp.bfloat16).reshape(FRAMES, H, W, D)
```

```python
import functools

import jax
import jax.numpy as jnp
from jax import lax
from jax.experimental import pallas as pl
from jax.experimental.pallas import tpu as pltpu
from jax.sharding import PartitionSpec as P

HEADS = 16
PAIR = 128
CHUNK = 512
FAST_EARLY = 1
F32 = jnp.float32
BF16 = jnp.bfloat16


def kernel(
    tiles, exchange,
    matches_in, counts_in, frames_in, keys_in, wq_in, wk_in, wv_in, wo_in,
    out,
    matches, counts, frames, stills, wq, wk, wv, wo, queries, key_table, value_table, context,
    stage, scores_even, scores_odd, max_even, max_odd, early_total, early_max,
    load_sem, halo_send, halo_recv, send_sem, recv_sem, own_sem,
):
    _, frame_count, rows, half_cols, model_dim = frames.shape
    piece_len = rows * half_cols
    block_len = 2 * piece_len
    key_count = stills.shape[1] // block_len
    slot_count = matches.shape[2]
    head_dim = model_dim // HEADS
    pair_count = model_dim // PAIR
    chunk_count = model_dim // CHUNK
    half_tiles = tiles // 2
    cols = half_cols // half_tiles
    me = lax.axis_index("tile")
    side = me // half_tiles

    def image_half(half):
        return jnp.where(half == 0, 1 - side, side)

    def half_columns(half):
        return pl.ds(pl.multiple_of(image_half(half) * half_cols, half_cols), half_cols)

    loads = [
        pltpu.make_async_copy(src, dst, load_sem.at[i])
        for i, (src, dst) in enumerate(
            [
                (keys_in, stills.at[1]), (wk_in, wk), (wv_in, wv),
                (frames_in.at[:, :, half_columns(0)], frames.at[0]), (wq_in, wq),
                (frames_in.at[:, :, half_columns(1)], frames.at[1]), (wo_in, wo),
                (matches_in, matches), (counts_in, counts),
            ]
        )
    ]
    for load in loads:
        load.start()

    barrier = pltpu.get_barrier_semaphore()

    def greet(step, carry):
        other = lax.rem(me + step, tiles)
        pl.semaphore_signal(
            barrier, inc=1, device_id={"tile": other}, device_id_type=pl.DeviceIdType.MESH
        )
        return carry

    lax.fori_loop(1, tiles, greet, 0)

    def fill(block, carry):
        one = jnp.where(block < 3 * key_count, 1.0, 0.0).astype(BF16)
        for pair in range(pair_count):
            value_table[block, :, pl.ds(pair * 2 * PAIR + PAIR, PAIR)] = jnp.full(
                (block_len, PAIR), 1.0, F32
            ).astype(BF16) * one
        return carry

    odd = lax.rem(me, 2)
    partners = ((me + 1 - 2 * odd, 2 - 2 * odd), (me - 1 + 2 * odd, 2 * odd))
    far = partners[1][0]
    has_far = (far >= 0) & (far < tiles)
    place = lax.rem(me, 4)
    slow = ((place == 1) | (place == 2)) & (me != 1) & (me != tiles - 2)
    early_count = jnp.where(has_far, jnp.where(slow, frame_count, FAST_EARLY), 0)

    pl.semaphore_wait(barrier, tiles - 1)

    def halo(kind, key):
        part = pl.ds(key * block_len, block_len)
        return pltpu.make_async_remote_copy(
            src_ref=keys_in.at[part], dst_ref=stills.at[partners[1 - kind][1], part],
            send_sem=halo_send.at[kind, key], recv_sem=halo_recv.at[kind, key],
            device_id={"tile": partners[kind][0]}, device_id_type=pl.DeviceIdType.MESH,
        )

    def arrival(kind, key):
        part = pl.ds(key * block_len, block_len)
        return pltpu.make_async_remote_copy(
            src_ref=keys_in.at[part], dst_ref=stills.at[partners[kind][1], part],
            send_sem=halo_send.at[kind, key], recv_sem=halo_recv.at[kind, key],
            device_id={"tile": partners[kind][0]}, device_id_type=pl.DeviceIdType.MESH,
        )

    @pl.when(has_far)
    def _():
        for key in range(key_count):
            halo(1, key).start()

    for key in range(key_count):
        halo(0, key).start()

    lax.fori_loop(0, 3 * key_count + 1, fill, 0)
    for pair in range(pair_count):
        value_table[3 * key_count, :, pl.ds(pair * 2 * PAIR, PAIR)] = jnp.zeros(
            (block_len, PAIR), BF16
        )

    lane = lax.broadcasted_iota(jnp.int32, (piece_len, CHUNK), 1)
    even = lax.rem(lane, PAIR) < head_dim

    def project_queries(half):
        def step(chunk, carry):
            at = pl.ds(pl.multiple_of(chunk * CHUNK, CHUNK), CHUNK)
            tokens = frames[half].reshape(frame_count * piece_len, model_dim)
            q = jnp.dot(tokens, wq[:, at], preferred_element_type=F32)
            q = q * head_dim ** (-0.5)
            for frame in range(frame_count):
                part = q[frame * piece_len : (frame + 1) * piece_len]
                piece = half * frame_count + frame
                queries[piece, 0:piece_len, at] = jnp.where(even, part, 0.0).astype(BF16)
                queries[piece, piece_len : 2 * piece_len, at] = jnp.where(even, 0.0, part).astype(BF16)
            return carry

        lax.fori_loop(0, chunk_count, step, 0)

    def project_stills(slot, first, count):
        def step(chunk, carry):
            at = pl.ds(pl.multiple_of(chunk * CHUNK, CHUNK), CHUNK)
            tokens = stills[slot, first * block_len : (first + count) * block_len, :]
            k = jnp.dot(tokens, wk[:, at], preferred_element_type=F32).astype(BF16)
            v = jnp.dot(tokens, wv[:, at], preferred_element_type=F32).astype(BF16)
            for key in range(count):
                part = slice(key * block_len, (key + 1) * block_len)
                block = slot * key_count + first + key
                key_table[block, at, :] = k[part].T
                for pair in range(CHUNK // PAIR):
                    to = pl.multiple_of(chunk * 2 * CHUNK + pair * 2 * PAIR, PAIR)
                    value_table[block, :, pl.ds(to, PAIR)] = v[part, pair * PAIR : (pair + 1) * PAIR]
            return carry

        lax.fori_loop(0, chunk_count, step, 0)

    for load in loads[:3]:
        load.wait()
    project_stills(1, 0, key_count)
    for load in loads[3:]:
        load.wait()

    def project_half(half, carry):
        project_queries(half)
        return carry

    lax.fori_loop(0, jnp.where(slow, 2, 1), project_half, 0)
    for key in range(key_count):
        arrival(0, key).wait_recv()
    project_stills(partners[0][1], 0, key_count)
    pair_lane = lax.broadcasted_iota(jnp.int32, (piece_len, PAIR), 1) < head_dim

    def send(frame, other, source):
        return pltpu.make_async_remote_copy(
            src_ref=stage.at[frame, other], dst_ref=out.at[frame, source],
            send_sem=send_sem.at[frame, other], recv_sem=recv_sem.at[frame, source],
            device_id={"tile": other}, device_id_type=pl.DeviceIdType.MESH,
        )

    def keep(frame):
        return pltpu.make_async_copy(stage.at[frame, me], out.at[frame, me], own_sem.at[0, frame])

    def place_half(frame, half):
        return pltpu.make_async_copy(
            stage.at[frame, image_half(half)], out.at[frame, :, half_columns(half)],
            own_sem.at[half, frame],
        )

    def attend(piece, keys, values, early=False, late=False):
        def score_block(q, slot, at, scores, most):
            s = jnp.dot(q, key_table[keys[slot], at, :], preferred_element_type=F32)
            scores[:, slot * block_len : (slot + 1) * block_len] = s
            for part in range(block_len // PAIR):
                some = s[:, part * PAIR : (part + 1) * PAIR]
                most = some if most is None else jnp.maximum(most, some)
            return most

        def value_block(slot, wide, scores, most, total):
            p = jnp.concatenate(
                [
                    jnp.exp(scores[:, at : at + PAIR] - most).astype(BF16)
                    for at in range(slot * block_len, (slot + 1) * block_len, PAIR)
                ],
                axis=1,
            )
            term = jnp.dot(p, value_table[values[slot], :, wide], preferred_element_type=F32)
            return term if total is None else total + term

        def close(most, pair, top):
            most = jnp.broadcast_to(jnp.max(most, axis=1, keepdims=True), top.shape)
            if late:
                most = jnp.maximum(most, early_max[piece, pair])
            top[...] = most

        def columns(pair, width):
            return pl.ds(pl.multiple_of(pair * width, width), width)

        def load_query(pair):
            return queries[piece, :, columns(pair, PAIR)]

        def step(pair, scores, top, next_pair, next_scores, next_top):
            most, total, next_most = top[...], None, None
            q = load_query(next_pair)
            if late:
                scale = jnp.exp(early_max[piece, pair] - most)
                total = early_total[piece, pair] * jnp.concatenate([scale, scale], axis=1)
            for slot in range(len(keys)):
                next_most = score_block(q, slot, columns(next_pair, PAIR), next_scores, next_most)
                total = value_block(slot, columns(pair, 2 * PAIR), scores, most, total)
            close(next_most, next_pair, next_top)
            if early:
                early_total[piece, pair] = total
                early_max[piece, pair] = most
                return None
            each = total[:, :PAIR] / total[:, PAIR:]
            both = jnp.where(pair_lane, each[:piece_len], each[piece_len:])
            context[:, columns(pair, PAIR)] = both.astype(BF16)

        most, q = None, load_query(0)
        for slot in range(len(keys)):
            most = score_block(q, slot, columns(0, PAIR), scores_even, most)
        close(most, 0, max_even)

        def two_pairs(index, carry):
            pair = index * 2
            after = jnp.minimum(pair + 2, pair_count - 1)
            step(pair, scores_even, max_even, pair + 1, scores_odd, max_odd)
            step(pair + 1, scores_odd, max_odd, after, scores_even, max_even)
            return carry

        lax.fori_loop(0, pair_count // 2, two_pairs, 0)

    def used(frame, slot):
        return slot < counts[0, frame]

    def named(frame, position):
        keys, values = [], []
        for key in range(key_count):
            there = jnp.int32(0)
            for slot in range(slot_count):
                same = (matches[0, frame, slot] == key * 3 + position) & used(frame, slot)
                there = there + jnp.where(same, 1, 0)
            block = position * key_count + key
            keys.append(jnp.where(there > 0, block, key_count))
            values.append(jnp.where(there > 0, block, 3 * key_count))
        return keys, values

    def partner(half, step):
        top = lax.rem(me // half_tiles, 2)
        other, bit = jnp.where(half == 0, 1 - top, top) * half_tiles, 1
        while bit < half_tiles:
            mine = lax.rem(me // bit, 2)
            other = other + (1 - mine if step // bit % 2 else mine) * bit
            bit *= 2
        return other

    def finish_piece(half, frame):
        for chunk in range(chunk_count):
            at = slice(chunk * CHUNK, (chunk + 1) * CHUNK)
            update = jnp.dot(context[...], wo[:, at], preferred_element_type=F32)
            mixed = frames[half, frame, :, :, at].reshape(piece_len, CHUNK).astype(F32) + update
            if exchange:
                first = image_half(half) * half_tiles
                for other in range(half_tiles):
                    group = [
                        mixed[row * half_cols + other * cols : row * half_cols + (other + 1) * cols]
                        for row in range(rows)
                    ]
                    stage[frame, first + other, :, at] = jnp.concatenate(group, axis=0).astype(BF16)
            else:
                stage[frame, image_half(half), :, :, at] = mixed.reshape(rows, half_cols, CHUNK).astype(BF16)

        if exchange:
            order = sorted(range(half_tiles), key=lambda step: (step // 2 % 2, -step))
            for step in order:
                other = partner(half, step)
                if step:
                    send(frame, other, me).start()
                    continue

                @pl.when(half == 0)
                def _():
                    send(frame, other, me).start()

                @pl.when(half != 0)
                def _():
                    keep(frame).start()
        else:
            place_half(frame, half).start()

    def one_piece(piece, carry):
        half = piece // frame_count
        frame = lax.rem(piece, frame_count)
        keys, values = [], []
        for slot in range(slot_count):
            chosen = jnp.where(used(frame, slot), matches[0, frame, slot], matches[0, frame, 0])
            block = lax.rem(chosen, 3) * key_count + lax.div(chosen, 3)
            keys.append(block)
            values.append(jnp.where(used(frame, slot), block, 3 * key_count))

        @pl.when((piece == frame_count) & jnp.logical_not(slow))
        def _():
            project_queries(1)

        attend(piece, keys, values)
        finish_piece(half, frame)
        return carry

    def early_piece(piece, carry):
        own_keys, own_values = named(piece, 1)
        near_keys, near_values = named(piece, partners[0][1])
        attend(piece, own_keys + near_keys, own_values + near_values, early=True)
        return carry

    def late_piece(piece, carry):
        attend(piece, *named(piece, partners[1][1]), late=True)
        finish_piece(jnp.int32(0), piece)
        return carry

    lax.fori_loop(0, early_count, early_piece, 0)

    @pl.when(has_far)
    def _():
        for key in range(key_count):
            arrival(1, key).wait_recv()
            project_stills(partners[1][1], key, 1)

    lax.fori_loop(0, early_count, late_piece, 0)
    lax.fori_loop(early_count, 2 * frame_count, one_piece, 0)

    @pl.when(has_far)
    def _():
        for key in range(key_count):
            halo(1, key).wait_send()

    for key in range(key_count):
        halo(0, key).wait_send()

    def finish(frame, carry):
        if exchange:

            def end(step, carry):
                other = lax.rem(me + step, tiles)
                send(frame, other, me).wait_send()
                send(frame, other, other).wait_recv()
                return carry

            lax.fori_loop(1, tiles, end, 0)
            keep(frame).wait()
        else:
            for half in range(2):
                place_half(frame, half).wait()
        return carry

    lax.fori_loop(0, frame_count, finish, 0)


def shards(tiles, frames, keyframes, matches, counts, w_query, w_key, w_value, w_out):
    frame_count, row_count, col_count, model_dim = frames.shape
    key_count = keyframes.shape[0]
    block_len = row_count * col_count
    half_cols = col_count // 2
    piece_len = row_count * half_cols
    slots = matches.shape[2]
    cols = col_count // tiles
    exchange = cols % 8 == 0 and tiles & (tiles - 1) == 0
    if exchange:
        out_shape = (frame_count, tiles, row_count * cols, model_dim)
        stage_shape = out_shape
    else:
        out_shape = (frame_count, row_count, col_count, model_dim)
        stage_shape = (frame_count, 2, row_count, half_cols, model_dim)
    weight = pltpu.VMEM((model_dim, model_dim), BF16)
    products = (4 * frame_count + 12 * key_count) * block_len * model_dim * model_dim
    products += 4 * frame_count * slots * block_len * block_len * model_dim
    mixed = pl.pallas_call(
        functools.partial(kernel, tiles, exchange),
        out_shape=jax.ShapeDtypeStruct(out_shape, BF16),
        in_specs=[pl.BlockSpec(memory_space=pl.ANY)] * 8,
        out_specs=pl.BlockSpec(memory_space=pl.ANY),
        scratch_shapes=[
            pltpu.SMEM(matches.shape, jnp.int32),
            pltpu.SMEM(counts.shape, jnp.int32),
            pltpu.VMEM((2, frame_count, row_count, half_cols, model_dim), BF16),
            pltpu.VMEM((3, key_count * block_len, model_dim), BF16),
            weight, weight, weight, weight,
            pltpu.VMEM((2 * frame_count, 2 * piece_len, model_dim), BF16),
            pltpu.VMEM((3 * key_count, model_dim, block_len), BF16),
            pltpu.VMEM((3 * key_count + 1, block_len, 2 * model_dim), BF16),
            pltpu.VMEM((piece_len, model_dim), BF16),
            pltpu.VMEM(stage_shape, BF16),
            pltpu.VMEM((2 * piece_len, slots * block_len), F32),
            pltpu.VMEM((2 * piece_len, slots * block_len), F32),
            pltpu.VMEM((2 * piece_len, PAIR), F32),
            pltpu.VMEM((2 * piece_len, PAIR), F32),
            pltpu.VMEM((frame_count, HEADS // 2, 2 * piece_len, 2 * PAIR), F32),
            pltpu.VMEM((frame_count, HEADS // 2, 2 * piece_len, PAIR), F32),
            pltpu.SemaphoreType.DMA((9,)),
            pltpu.SemaphoreType.DMA((2, key_count)),
            pltpu.SemaphoreType.DMA((2, key_count)),
            pltpu.SemaphoreType.DMA((frame_count, tiles)),
            pltpu.SemaphoreType.DMA((frame_count, tiles)),
            pltpu.SemaphoreType.DMA((2, frame_count)),
        ],
        compiler_params=pltpu.CompilerParams(
            collective_id=0, has_side_effects=True, vmem_limit_bytes=60 * 1024 * 1024
        ),
        cost_estimate=pl.CostEstimate(
            flops=products, bytes_accessed=16 * 1024 * 1024,
            transcendentals=frame_count * slots * HEADS * block_len * block_len,
        ),
        name="attend_and_relay",
    )(
        matches, counts, frames,
        keyframes.reshape(key_count * block_len, model_dim),
        w_query, w_key, w_value, w_out,
    )
    if exchange:
        return mixed.reshape(frame_count, tiles * row_count, cols, model_dim)
    return lax.all_to_all(mixed, "tile", split_axis=2, concat_axis=1, tiled=True)


def solution(mesh):
    placed = (
        P("clip", "tile", None, None),
        P("clip", "tile", None, None),
        P("tile", "clip", None),
        P("tile", "clip"),
        P(),
        P(),
        P(),
        P(),
    )
    return jax.shard_map(
        functools.partial(shards, mesh.shape["tile"]),
        mesh=mesh, in_specs=placed, out_specs=P("clip", None, "tile", None), check_vma=False,
    )
```

```python
import functools

import jax
import jax.numpy as jnp
from jax import lax
from jax.experimental import pallas as pl
from jax.experimental.pallas import tpu as pltpu
from jax.sharding import PartitionSpec as P

HEADS = 16
PAIR = 128
CHUNK = 512
FAST_EARLY = 1
GROUP = 8
F32 = jnp.float32
BF16 = jnp.bfloat16


def kernel(
    tiles, exchange,
    matches_in, counts_in, frames_in, keys_in, wq_in, wk_in, wv_in, wo_in,
    out,
    matches, counts, frames, stills, wq, wk, wv, wo, queries, key_table, value_table, context,
    stage, scores_even, scores_odd, max_even, max_odd, early_total, early_max,
    load_sem, halo_send, halo_recv, near_send, near_recv, send_sem, recv_sem, own_sem,
):
    _, frame_count, rows, half_cols, model_dim = frames.shape
    piece_len = rows * half_cols
    block_len = 2 * piece_len
    key_count = stills.shape[1] // block_len
    slot_count = matches.shape[2]
    head_dim = model_dim // HEADS
    pair_count = model_dim // PAIR
    chunk_count = model_dim // CHUNK
    half_tiles = tiles // 2
    cols = half_cols // half_tiles
    me = lax.axis_index("tile")
    side = me // half_tiles

    def image_half(half):
        return jnp.where(half == 0, 1 - side, side)

    def half_columns(half):
        return pl.ds(pl.multiple_of(image_half(half) * half_cols, half_cols), half_cols)

    loads = [
        pltpu.make_async_copy(src, dst, load_sem.at[i])
        for i, (src, dst) in enumerate(
            [
                (keys_in, stills.at[0]), (wk_in, wk), (wv_in, wv),
                (frames_in.at[:, :, half_columns(0)], frames.at[0]), (wq_in, wq),
                (frames_in.at[:, :, half_columns(1)], frames.at[1]), (wo_in, wo),
                (matches_in, matches), (counts_in, counts),
            ]
        )
    ]
    for load in loads:
        load.start()

    barrier = pltpu.get_barrier_semaphore()

    def greet(step, carry):
        other = lax.rem(me + step, tiles)
        pl.semaphore_signal(
            barrier, inc=1, device_id={"tile": other}, device_id_type=pl.DeviceIdType.MESH
        )
        return carry

    lax.fori_loop(1, tiles, greet, 0)

    def fill(block):
        one = jnp.where(block < 3 * key_count, 1.0, 0.0).astype(BF16)
        for pair in range(pair_count):
            value_table[block, :, pl.ds(pair * 2 * PAIR + PAIR, PAIR)] = jnp.full(
                (block_len, PAIR), 1.0, F32
            ).astype(BF16) * one

    odd = lax.rem(me, 2)
    partners = ((me + 1 - 2 * odd, 2 - 2 * odd), (me - 1 + 2 * odd, 2 * odd))
    far = partners[1][0]
    has_far = (far >= 0) & (far < tiles)
    place = lax.rem(me, 4)
    inner = (place == 1) | (place == 2)
    slow = inner & (me != 1) & (me != tiles - 2)
    held = has_far & inner & (far != 1) & (far != tiles - 2)
    early_count = jnp.where(has_far, jnp.where(slow, frame_count, FAST_EARLY), 0)

    for key in range(key_count):
        fill(key_count + key)
        fill(partners[1][1] * key_count + key)
    fill(3 * key_count)
    for pair in range(pair_count):
        value_table[3 * key_count, :, pl.ds(pair * 2 * PAIR, PAIR)] = jnp.zeros(
            (block_len, PAIR), BF16
        )
    pl.semaphore_wait(barrier, tiles - 1)

    def halo(key):
        part = pl.ds(key * block_len, block_len)
        return pltpu.make_async_remote_copy(
            src_ref=keys_in.at[part], dst_ref=stills.at[1, part],
            send_sem=halo_send.at[key], recv_sem=halo_recv.at[key],
            device_id={"tile": far}, device_id_type=pl.DeviceIdType.MESH,
        )

    def start_halo():
        for key in range(key_count):
            halo(key).start()

    def shared(key, chunk, position):
        block = position * key_count + key
        own = key_count + key
        narrow = pl.ds(pl.multiple_of(chunk * CHUNK, CHUNK), CHUNK)
        wide = pl.ds(pl.multiple_of(chunk * 2 * CHUNK, 2 * CHUNK), 2 * CHUNK)
        pieces = (
            (key_table.at[own, narrow], key_table.at[block, narrow]),
            (value_table.at[own, :, wide], value_table.at[block, :, wide]),
        )
        return [
            pltpu.make_async_remote_copy(
                src_ref=src, dst_ref=dst,
                send_sem=near_send.at[kind, key, chunk], recv_sem=near_recv.at[kind, key, chunk],
                device_id={"tile": partners[0][0]}, device_id_type=pl.DeviceIdType.MESH,
            )
            for kind, (src, dst) in enumerate(pieces)
        ]

    @pl.when(has_far & jnp.logical_not(held))
    def _():
        start_halo()

    lane = lax.broadcasted_iota(jnp.int32, (piece_len, CHUNK), 1)
    even = lax.rem(lane, PAIR) < head_dim

    def project_queries(half):
        def step(chunk, carry):
            at = pl.ds(pl.multiple_of(chunk * CHUNK, CHUNK), CHUNK)
            tokens = frames[half].reshape(frame_count * piece_len, model_dim)
            q = jnp.dot(tokens, wq[:, at], preferred_element_type=F32)
            q = q * head_dim ** (-0.5)
            for frame in range(frame_count):
                part = q[frame * piece_len : (frame + 1) * piece_len]
                piece = half * frame_count + frame
                queries[piece, 0:piece_len, at] = jnp.where(even, part, 0.0).astype(BF16)
                queries[piece, piece_len : 2 * piece_len, at] = jnp.where(even, 0.0, part).astype(BF16)
            return carry

        lax.fori_loop(0, chunk_count, step, 0)

    def project_stills(source, slot, first, count, share=False):
        def step(chunk, carry):
            at = pl.ds(pl.multiple_of(chunk * CHUNK, CHUNK), CHUNK)
            tokens = stills[source, first * block_len : (first + count) * block_len, :]
            k = jnp.dot(tokens, wk[:, at], preferred_element_type=F32).astype(BF16)
            v = jnp.dot(tokens, wv[:, at], preferred_element_type=F32).astype(BF16)
            for key in range(count):
                part = slice(key * block_len, (key + 1) * block_len)
                block = slot * key_count + first + key
                key_table[block, at, :] = k[part].T
                for pair in range(CHUNK // PAIR):
                    to = pl.multiple_of(chunk * 2 * CHUNK + pair * 2 * PAIR, PAIR)
                    value_table[block, :, pl.ds(to, PAIR)] = v[part, pair * PAIR : (pair + 1) * PAIR]
                if share:
                    for copy in shared(key, chunk, partners[1][1]):
                        copy.start()
            return carry

        lax.fori_loop(0, chunk_count, step, 0)

    for load in loads[:3]:
        load.wait()
    project_stills(0, 1, 0, key_count, share=True)
    for load in loads[3:]:
        load.wait()

    def project_half(half, carry):
        project_queries(half)
        return carry

    lax.fori_loop(0, jnp.where(slow, 2, 1), project_half, 0)
    for key in range(key_count):
        for chunk in range(chunk_count):
            for copy in shared(key, chunk, partners[0][1]):
                copy.wait_recv()
    pair_lane = lax.broadcasted_iota(jnp.int32, (piece_len, PAIR), 1) < head_dim

    def send(frame, other, source):
        return pltpu.make_async_remote_copy(
            src_ref=stage.at[frame, other], dst_ref=out.at[frame, source],
            send_sem=send_sem.at[frame, other], recv_sem=recv_sem.at[frame, source],
            device_id={"tile": other}, device_id_type=pl.DeviceIdType.MESH,
        )

    def keep(frame):
        return pltpu.make_async_copy(stage.at[frame, me], out.at[frame, me], own_sem.at[0, frame])

    def place_half(frame, half):
        return pltpu.make_async_copy(
            stage.at[frame, image_half(half)], out.at[frame, :, half_columns(half)],
            own_sem.at[half, frame],
        )

    def attend(piece, keys, values, early=False, late=False):
        def score_block(q, slot, at, scores, most):
            s = jnp.dot(q, key_table[keys[slot], at, :], preferred_element_type=F32)
            scores[:, slot * block_len : (slot + 1) * block_len] = s
            for part in range(block_len // PAIR):
                some = s[:, part * PAIR : (part + 1) * PAIR]
                most = some if most is None else jnp.maximum(most, some)
            return most

        def value_block(slot, wide, scores, most, total):
            p = jnp.concatenate(
                [
                    jnp.exp(scores[:, at : at + PAIR] - most).astype(BF16)
                    for at in range(slot * block_len, (slot + 1) * block_len, PAIR)
                ],
                axis=1,
            )
            term = jnp.dot(p, value_table[values[slot], :, wide], preferred_element_type=F32)
            return term if total is None else total + term

        def close(most, pair, top):
            most = jnp.broadcast_to(jnp.max(most, axis=1, keepdims=True), top.shape)
            if late:
                most = jnp.maximum(most, early_max[piece, pair])
            top[...] = most

        def columns(pair, width):
            return pl.ds(pl.multiple_of(pair * width, width), width)

        def load_query(pair):
            return queries[piece, :, columns(pair, PAIR)]

        def step(pair, scores, top, next_pair, next_scores, next_top):
            most, total, next_most = top[...], None, None
            q = load_query(next_pair)
            if late:
                scale = jnp.exp(early_max[piece, pair] - most)
                total = early_total[piece, pair] * jnp.concatenate([scale, scale], axis=1)
            for slot in range(len(keys)):
                next_most = score_block(q, slot, columns(next_pair, PAIR), next_scores, next_most)
                total = value_block(slot, columns(pair, 2 * PAIR), scores, most, total)
            close(next_most, next_pair, next_top)
            if early:
                early_total[piece, pair] = total
                early_max[piece, pair] = most
                return None
            each = total[:, :PAIR] / total[:, PAIR:]
            both = jnp.where(pair_lane, each[:piece_len], each[piece_len:])
            context[:, columns(pair, PAIR)] = both.astype(BF16)

        most, q = None, load_query(0)
        for slot in range(len(keys)):
            most = score_block(q, slot, columns(0, PAIR), scores_even, most)
        close(most, 0, max_even)

        def group(index, carry):
            for inner_pair in range(0, GROUP, 2):
                pair = index * GROUP + inner_pair
                after = jnp.minimum(pair + 2, pair_count - 1)
                step(pair, scores_even, max_even, pair + 1, scores_odd, max_odd)
                step(pair + 1, scores_odd, max_odd, after, scores_even, max_even)
            return carry

        lax.fori_loop(0, pair_count // GROUP, group, 0)

    def used(frame, slot):
        return slot < counts[0, frame]

    def named(frame, position):
        keys, values = [], []
        for key in range(key_count):
            there = jnp.int32(0)
            for slot in range(slot_count):
                same = (matches[0, frame, slot] == key * 3 + position) & used(frame, slot)
                there = there + jnp.where(same, 1, 0)
            block = position * key_count + key
            keys.append(jnp.where(there > 0, block, key_count))
            values.append(jnp.where(there > 0, block, 3 * key_count))
        return keys, values

    def partner(half, step):
        top = lax.rem(me // half_tiles, 2)
        other, bit = jnp.where(half == 0, 1 - top, top) * half_tiles, 1
        while bit < half_tiles:
            mine = lax.rem(me // bit, 2)
            other = other + (1 - mine if step // bit % 2 else mine) * bit
            bit *= 2
        return other

    def finish_piece(half, frame):
        for chunk in range(chunk_count):
            at = slice(chunk * CHUNK, (chunk + 1) * CHUNK)
            update = jnp.dot(context[...], wo[:, at], preferred_element_type=F32)
            mixed = frames[half, frame, :, :, at].reshape(piece_len, CHUNK).astype(F32) + update
            if exchange:
                first = image_half(half) * half_tiles
                for other in range(half_tiles):
                    group = [
                        mixed[row * half_cols + other * cols : row * half_cols + (other + 1) * cols]
                        for row in range(rows)
                    ]
                    stage[frame, first + other, :, at] = jnp.concatenate(group, axis=0).astype(BF16)
            else:
                stage[frame, image_half(half), :, :, at] = mixed.reshape(rows, half_cols, CHUNK).astype(BF16)

        if exchange:
            order = sorted(range(half_tiles), key=lambda step: (step // 2 % 2, -step))
            for step in order:
                other = partner(half, step)
                if step:
                    send(frame, other, me).start()
                    continue

                @pl.when(half == 0)
                def _():
                    send(frame, other, me).start()

                @pl.when(half != 0)
                def _():
                    keep(frame).start()
        else:
            place_half(frame, half).start()

    def one_piece(piece, carry):
        half = piece // frame_count
        frame = lax.rem(piece, frame_count)
        keys, values = [], []
        for slot in range(slot_count):
            chosen = jnp.where(used(frame, slot), matches[0, frame, slot], matches[0, frame, 0])
            block = lax.rem(chosen, 3) * key_count + lax.div(chosen, 3)
            keys.append(block)
            values.append(jnp.where(used(frame, slot), block, 3 * key_count))

        @pl.when((piece == frame_count) & jnp.logical_not(has_far))
        def _():
            project_queries(1)

        attend(piece, keys, values)
        finish_piece(half, frame)
        return carry

    def early_piece(piece, carry):
        own_keys, own_values = named(piece, 1)
        near_keys, near_values = named(piece, partners[0][1])
        attend(piece, own_keys + near_keys, own_values + near_values, early=True)

        @pl.when((piece == 0) & held)
        def _():
            start_halo()

        return carry

    def late_piece(piece, carry):
        attend(piece, *named(piece, partners[1][1]), late=True)
        finish_piece(jnp.int32(0), piece)
        return carry

    lax.fori_loop(0, early_count, early_piece, 0)

    @pl.when(has_far)
    def _():
        for key in range(key_count):
            halo(key).wait_recv()
            project_stills(1, partners[1][1], key, 1)
            if key == 0:

                @pl.when(jnp.logical_not(slow))
                def _():
                    project_queries(1)

    lax.fori_loop(0, early_count, late_piece, 0)
    lax.fori_loop(early_count, 2 * frame_count, one_piece, 0)

    @pl.when(has_far)
    def _():
        for key in range(key_count):
            halo(key).wait_send()

    for key in range(key_count):
        for chunk in range(chunk_count):
            for copy in shared(key, chunk, partners[1][1]):
                copy.wait_send()

    def finish(frame, carry):
        if exchange:

            def end(step, carry):
                other = lax.rem(me + step, tiles)
                send(frame, other, me).wait_send()
                send(frame, other, other).wait_recv()
                return carry

            lax.fori_loop(1, tiles, end, 0)
            keep(frame).wait()
        else:
            for half in range(2):
                place_half(frame, half).wait()
        return carry

    lax.fori_loop(0, frame_count, finish, 0)


def settle(src, out, held, in_sem, out_sem):
    frame_count, parts = in_sem.shape
    step = src.shape[1] // parts
    places = [(frame, pl.ds(part * step, step)) for frame in range(frame_count) for part in range(parts)]
    fetch = [
        pltpu.make_async_copy(src.at[at], held.at[at], in_sem.at[i // parts, i % parts])
        for i, at in enumerate(places)
    ]
    place = [
        pltpu.make_async_copy(held.at[at], out.at[at], out_sem.at[i // parts, i % parts])
        for i, at in enumerate(places)
    ]
    for copy in fetch:
        copy.start()
    for copy, back in zip(fetch, place):
        copy.wait()
        back.start()
    for back in place:
        back.wait()


def shards(tiles, frames, keyframes, matches, counts, w_query, w_key, w_value, w_out):
    frame_count, row_count, col_count, model_dim = frames.shape
    key_count = keyframes.shape[0]
    block_len = row_count * col_count
    half_cols = col_count // 2
    piece_len = row_count * half_cols
    slots = matches.shape[2]
    cols = col_count // tiles
    exchange = cols % 8 == 0 and tiles & (tiles - 1) == 0
    if exchange:
        out_shape = (frame_count, tiles, row_count * cols, model_dim)
        stage_shape = out_shape
    else:
        out_shape = (frame_count, row_count, col_count, model_dim)
        stage_shape = (frame_count, 2, row_count, half_cols, model_dim)
    weight = pltpu.VMEM((model_dim, model_dim), BF16)
    products = (4 * frame_count + 12 * key_count) * block_len * model_dim * model_dim
    products += 4 * frame_count * slots * block_len * block_len * model_dim
    mixed = pl.pallas_call(
        functools.partial(kernel, tiles, exchange),
        out_shape=jax.ShapeDtypeStruct(out_shape, BF16),
        in_specs=[pl.BlockSpec(memory_space=pl.ANY)] * 8,
        out_specs=pl.BlockSpec(memory_space=pl.ANY),
        scratch_shapes=[
            pltpu.SMEM(matches.shape, jnp.int32),
            pltpu.SMEM(counts.shape, jnp.int32),
            pltpu.VMEM((2, frame_count, row_count, half_cols, model_dim), BF16),
            pltpu.VMEM((2, key_count * block_len, model_dim), BF16),
            weight, weight, weight, weight,
            pltpu.VMEM((2 * frame_count, 2 * piece_len, model_dim), BF16),
            pltpu.VMEM((3 * key_count, model_dim, block_len), BF16),
            pltpu.VMEM((3 * key_count + 1, block_len, 2 * model_dim), BF16),
            pltpu.VMEM((piece_len, model_dim), BF16),
            pltpu.VMEM(stage_shape, BF16),
            pltpu.VMEM((2 * piece_len, slots * block_len), F32),
            pltpu.VMEM((2 * piece_len, slots * block_len), F32),
            pltpu.VMEM((2 * piece_len, PAIR), F32),
            pltpu.VMEM((2 * piece_len, PAIR), F32),
            pltpu.VMEM((frame_count, HEADS // 2, 2 * piece_len, 2 * PAIR), F32),
            pltpu.VMEM((frame_count, HEADS // 2, 2 * piece_len, PAIR), F32),
            pltpu.SemaphoreType.DMA((9,)),
            pltpu.SemaphoreType.DMA((key_count,)),
            pltpu.SemaphoreType.DMA((key_count,)),
            pltpu.SemaphoreType.DMA((2, key_count, model_dim // CHUNK)),
            pltpu.SemaphoreType.DMA((2, key_count, model_dim // CHUNK)),
            pltpu.SemaphoreType.DMA((frame_count, tiles)),
            pltpu.SemaphoreType.DMA((frame_count, tiles)),
            pltpu.SemaphoreType.DMA((2, frame_count)),
        ],
        compiler_params=pltpu.CompilerParams(
            collective_id=0, has_side_effects=True, vmem_limit_bytes=60 * 1024 * 1024
        ),
        cost_estimate=pl.CostEstimate(
            flops=products, bytes_accessed=16 * 1024 * 1024,
            transcendentals=frame_count * slots * HEADS * block_len * block_len,
        ),
        name="attend_and_relay",
    )(
        matches, counts, frames,
        keyframes.reshape(key_count * block_len, model_dim),
        w_query, w_key, w_value, w_out,
    )
    if exchange:
        mixed = pl.pallas_call(
            settle,
            out_shape=jax.ShapeDtypeStruct(out_shape, BF16),
            in_specs=[pl.BlockSpec(memory_space=pl.ANY)],
            out_specs=pl.BlockSpec(memory_space=pl.ANY),
            scratch_shapes=[
                pltpu.VMEM(out_shape, BF16),
                pltpu.SemaphoreType.DMA((frame_count, 2)),
                pltpu.SemaphoreType.DMA((frame_count, 2)),
            ],
            name="settle",
        )(mixed)
        return mixed.reshape(frame_count, tiles * row_count, cols, model_dim)
    return lax.all_to_all(mixed, "tile", split_axis=2, concat_axis=1, tiled=True)


def solution(mesh):
    placed = (
        P("clip", "tile", None, None),
        P("clip", "tile", None, None),
        P("tile", "clip", None),
        P("tile", "clip"),
        P(),
        P(),
        P(),
        P(),
    )
    return jax.shard_map(
        functools.partial(shards, mesh.shape["tile"]),
        mesh=mesh, in_specs=placed, out_specs=P("clip", None, "tile", None), check_vma=False,
    )
```

```python
import functools

import jax
import jax.numpy as jnp
from jax import lax
from jax.experimental import pallas as pl
from jax.experimental.pallas import tpu as pltpu
from jax.sharding import PartitionSpec as P

HEADS = 16
PAIR = 128
CHUNK = 512
FAST_EARLY = 1
GROUP = 8
RELAYED = 2
F32 = jnp.float32
BF16 = jnp.bfloat16


def kernel(
    tiles, exchange,
    matches_in, counts_in, frames_in, keys_in, wq_in, wk_in, wv_in, wo_in,
    out,
    matches, counts, frames, stills, wq, wk, wv, wo, queries, key_table, value_table, context,
    stage, relay, scores_even, scores_odd, max_even, max_odd, early_total, early_max,
    load_sem, halo_send, halo_recv, near_send, near_recv, relay_recv, relay_send, send_sem, recv_sem, own_sem,
):
    _, frame_count, rows, half_cols, model_dim = frames.shape
    piece_len = rows * half_cols
    block_len = 2 * piece_len
    key_count = stills.shape[1] // block_len
    slot_count = matches.shape[2]
    head_dim = model_dim // HEADS
    pair_count = model_dim // PAIR
    chunk_count = model_dim // CHUNK
    half_tiles = tiles // 2
    relay_count = relay.shape[0] if exchange and tiles == 16 else 0
    cols = half_cols // half_tiles
    me = lax.axis_index("tile")
    side = me // half_tiles

    def image_half(half):
        return jnp.where(half == 0, 1 - side, side)

    def half_columns(half):
        return pl.ds(pl.multiple_of(image_half(half) * half_cols, half_cols), half_cols)

    loads = [
        pltpu.make_async_copy(src, dst, load_sem.at[i])
        for i, (src, dst) in enumerate(
            [
                (keys_in, stills.at[0]), (wk_in, wk), (wv_in, wv),
                (frames_in.at[:, :, half_columns(0)], frames.at[0]), (wq_in, wq),
                (frames_in.at[:, :, half_columns(1)], frames.at[1]), (wo_in, wo),
                (matches_in, matches), (counts_in, counts),
            ]
        )
    ]
    for load in loads:
        load.start()

    barrier = pltpu.get_barrier_semaphore()

    def greet(step, carry):
        other = lax.rem(me + step, tiles)
        pl.semaphore_signal(
            barrier, inc=1, device_id={"tile": other}, device_id_type=pl.DeviceIdType.MESH
        )
        return carry

    lax.fori_loop(1, tiles, greet, 0)

    def fill(block):
        one = jnp.where(block < 3 * key_count, 1.0, 0.0).astype(BF16)
        for pair in range(pair_count):
            value_table[block, :, pl.ds(pair * 2 * PAIR + PAIR, PAIR)] = jnp.full(
                (block_len, PAIR), 1.0, F32
            ).astype(BF16) * one

    odd = lax.rem(me, 2)
    partners = ((me + 1 - 2 * odd, 2 - 2 * odd), (me - 1 + 2 * odd, 2 * odd))
    far = partners[1][0]
    has_far = (far >= 0) & (far < tiles)
    place = lax.rem(me, 4)
    inner = (place == 1) | (place == 2)
    slow = inner & (me != 1) & (me != tiles - 2)
    held = has_far & inner & (far != 1) & (far != tiles - 2)
    early_count = jnp.where(has_far, jnp.where(slow, frame_count, FAST_EARLY), 0)

    for key in range(key_count):
        fill(key_count + key)
        fill(partners[1][1] * key_count + key)
    fill(3 * key_count)
    for pair in range(pair_count):
        value_table[3 * key_count, :, pl.ds(pair * 2 * PAIR, PAIR)] = jnp.zeros(
            (block_len, PAIR), BF16
        )
    pl.semaphore_wait(barrier, tiles - 1)

    def halo(key):
        part = pl.ds(key * block_len, block_len)
        return pltpu.make_async_remote_copy(
            src_ref=keys_in.at[part], dst_ref=stills.at[1, part],
            send_sem=halo_send.at[key], recv_sem=halo_recv.at[key],
            device_id={"tile": far}, device_id_type=pl.DeviceIdType.MESH,
        )

    def start_halo():
        for key in range(key_count):
            halo(key).start()

    def shared(key, chunk, position):
        block = position * key_count + key
        own = key_count + key
        narrow = pl.ds(pl.multiple_of(chunk * CHUNK, CHUNK), CHUNK)
        wide = pl.ds(pl.multiple_of(chunk * 2 * CHUNK, 2 * CHUNK), 2 * CHUNK)
        pieces = (
            (key_table.at[own, narrow], key_table.at[block, narrow]),
            (value_table.at[own, :, wide], value_table.at[block, :, wide]),
        )
        return [
            pltpu.make_async_remote_copy(
                src_ref=src, dst_ref=dst,
                send_sem=near_send.at[kind, key, chunk], recv_sem=near_recv.at[kind, key, chunk],
                device_id={"tile": partners[0][0]}, device_id_type=pl.DeviceIdType.MESH,
            )
            for kind, (src, dst) in enumerate(pieces)
        ]

    @pl.when(has_far & jnp.logical_not(held))
    def _():
        start_halo()

    lane = lax.broadcasted_iota(jnp.int32, (piece_len, CHUNK), 1)
    even = lax.rem(lane, PAIR) < head_dim

    def project_queries(half):
        def step(chunk, carry):
            at = pl.ds(pl.multiple_of(chunk * CHUNK, CHUNK), CHUNK)
            tokens = frames[half].reshape(frame_count * piece_len, model_dim)
            q = jnp.dot(tokens, wq[:, at], preferred_element_type=F32)
            q = q * head_dim ** (-0.5)
            for frame in range(frame_count):
                part = q[frame * piece_len : (frame + 1) * piece_len]
                piece = half * frame_count + frame
                queries[piece, 0:piece_len, at] = jnp.where(even, part, 0.0).astype(BF16)
                queries[piece, piece_len : 2 * piece_len, at] = jnp.where(even, 0.0, part).astype(BF16)
            return carry

        lax.fori_loop(0, chunk_count, step, 0)

    def project_stills(source, slot, first, count, share=False):
        def step(chunk, carry):
            at = pl.ds(pl.multiple_of(chunk * CHUNK, CHUNK), CHUNK)
            tokens = stills[source, first * block_len : (first + count) * block_len, :]
            k = jnp.dot(tokens, wk[:, at], preferred_element_type=F32).astype(BF16)
            v = jnp.dot(tokens, wv[:, at], preferred_element_type=F32).astype(BF16)
            for key in range(count):
                part = slice(key * block_len, (key + 1) * block_len)
                block = slot * key_count + first + key
                key_table[block, at, :] = k[part].T
                for pair in range(CHUNK // PAIR):
                    to = pl.multiple_of(chunk * 2 * CHUNK + pair * 2 * PAIR, PAIR)
                    value_table[block, :, pl.ds(to, PAIR)] = v[part, pair * PAIR : (pair + 1) * PAIR]
                if share:
                    for copy in shared(key, chunk, partners[1][1]):
                        copy.start()
            return carry

        lax.fori_loop(0, chunk_count, step, 0)

    for load in loads[:3]:
        load.wait()
    project_stills(0, 1, 0, key_count, share=True)
    for load in loads[3:]:
        load.wait()

    def project_half(half, carry):
        project_queries(half)
        return carry

    lax.fori_loop(0, jnp.where(slow, 2, 1), project_half, 0)
    for key in range(key_count):
        for chunk in range(chunk_count):
            for copy in shared(key, chunk, partners[0][1]):
                copy.wait_recv()
    pair_lane = lax.broadcasted_iota(jnp.int32, (piece_len, PAIR), 1) < head_dim

    def send(frame, other, source):
        return pltpu.make_async_remote_copy(
            src_ref=stage.at[frame, other], dst_ref=out.at[frame, source],
            send_sem=send_sem.at[frame, other], recv_sem=recv_sem.at[frame, source],
            device_id={"tile": other}, device_id_type=pl.DeviceIdType.MESH,
        )

    def keep(frame):
        return pltpu.make_async_copy(stage.at[frame, me], out.at[frame, me], own_sem.at[0, frame])

    def place_half(frame, half):
        return pltpu.make_async_copy(
            stage.at[frame, image_half(half)], out.at[frame, :, half_columns(half)],
            own_sem.at[half, frame],
        )

    def attend(piece, keys, values, early=False, late=False):
        def score_block(q, slot, at, scores, most):
            s = jnp.dot(q, key_table[keys[slot], at, :], preferred_element_type=F32)
            scores[:, slot * block_len : (slot + 1) * block_len] = s
            for part in range(block_len // PAIR):
                some = s[:, part * PAIR : (part + 1) * PAIR]
                most = some if most is None else jnp.maximum(most, some)
            return most

        def value_block(slot, wide, scores, most, total):
            p = jnp.concatenate(
                [
                    jnp.exp(scores[:, at : at + PAIR] - most).astype(BF16)
                    for at in range(slot * block_len, (slot + 1) * block_len, PAIR)
                ],
                axis=1,
            )
            term = jnp.dot(p, value_table[values[slot], :, wide], preferred_element_type=F32)
            return term if total is None else total + term

        def close(most, pair, top):
            most = jnp.broadcast_to(jnp.max(most, axis=1, keepdims=True), top.shape)
            if late:
                most = jnp.maximum(most, early_max[piece, pair])
            top[...] = most

        def columns(pair, width):
            return pl.ds(pl.multiple_of(pair * width, width), width)

        def load_query(pair):
            return queries[piece, :, columns(pair, PAIR)]

        def step(pair, scores, top, next_pair, next_scores, next_top):
            most, total, next_most = top[...], None, None
            q = load_query(next_pair)
            if late:
                scale = jnp.exp(early_max[piece, pair] - most)
                total = early_total[piece, pair] * jnp.concatenate([scale, scale], axis=1)
            for slot in range(len(keys)):
                next_most = score_block(q, slot, columns(next_pair, PAIR), next_scores, next_most)
                total = value_block(slot, columns(pair, 2 * PAIR), scores, most, total)
            close(next_most, next_pair, next_top)
            if early:
                early_total[piece, pair] = total
                early_max[piece, pair] = most
                return None
            each = total[:, :PAIR] / total[:, PAIR:]
            both = jnp.where(pair_lane, each[:piece_len], each[piece_len:])
            context[:, columns(pair, PAIR)] = both.astype(BF16)

        most, q = None, load_query(0)
        for slot in range(len(keys)):
            most = score_block(q, slot, columns(0, PAIR), scores_even, most)
        close(most, 0, max_even)

        def group(index, carry):
            for inner_pair in range(0, GROUP, 2):
                pair = index * GROUP + inner_pair
                after = jnp.minimum(pair + 2, pair_count - 1)
                step(pair, scores_even, max_even, pair + 1, scores_odd, max_odd)
                step(pair + 1, scores_odd, max_odd, after, scores_even, max_even)
            return carry

        lax.fori_loop(0, pair_count // GROUP, group, 0)

    def used(frame, slot):
        return slot < counts[0, frame]

    def named(frame, position):
        keys, values = [], []
        for key in range(key_count):
            there = jnp.int32(0)
            for slot in range(slot_count):
                same = (matches[0, frame, slot] == key * 3 + position) & used(frame, slot)
                there = there + jnp.where(same, 1, 0)
            block = position * key_count + key
            keys.append(jnp.where(there > 0, block, key_count))
            values.append(jnp.where(there > 0, block, 3 * key_count))
        return keys, values

    def partner(half, step, source=me):
        top = lax.rem(source // half_tiles, 2)
        other, bit = jnp.where(half == 0, 1 - top, top) * half_tiles, 1
        while bit < half_tiles:
            mine = lax.rem(source // bit, 2)
            other = other + (1 - mine if step // bit % 2 else mine) * bit
            bit *= 2
        return other

    across = me + 2 - 4 * lax.rem(me // 2, 2)
    relayed = (me == 3) | (me == tiles - 4)
    relays = (me == 1) | (me == tiles - 2)

    def relay_slot(step):
        return step // 4 * 2 + step % 2

    def hand_over(frame, step, other):
        return pltpu.make_async_remote_copy(
            src_ref=stage.at[frame, other], dst_ref=relay.at[frame, relay_slot(step)],
            send_sem=send_sem.at[frame, other], recv_sem=relay_recv.at[frame, relay_slot(step)],
            device_id={"tile": across}, device_id_type=pl.DeviceIdType.MESH,
        )

    def pass_on(frame, step):
        return pltpu.make_async_remote_copy(
            src_ref=relay.at[frame, relay_slot(step)], dst_ref=out.at[frame, across],
            send_sem=relay_send.at[frame, relay_slot(step)], recv_sem=recv_sem.at[frame, across],
            device_id={"tile": partner(0, step, across)}, device_id_type=pl.DeviceIdType.MESH,
        )

    relay_steps = [step for step in range(half_tiles) if step // 2 % 2]

    def finish_piece(half, frame):
        for chunk in range(chunk_count):
            at = slice(chunk * CHUNK, (chunk + 1) * CHUNK)
            update = jnp.dot(context[...], wo[:, at], preferred_element_type=F32)
            mixed = frames[half, frame, :, :, at].reshape(piece_len, CHUNK).astype(F32) + update
            if exchange:
                first = image_half(half) * half_tiles
                for other in range(half_tiles):
                    group = [
                        mixed[row * half_cols + other * cols : row * half_cols + (other + 1) * cols]
                        for row in range(rows)
                    ]
                    stage[frame, first + other, :, at] = jnp.concatenate(group, axis=0).astype(BF16)
            else:
                stage[frame, image_half(half), :, :, at] = mixed.reshape(rows, half_cols, CHUNK).astype(BF16)

        if exchange:
            order = sorted(range(half_tiles), key=lambda step: (step // 2 % 2, -step))
            for step in order:
                other = partner(half, step)
                if step in relay_steps and relay_count:
                    detour = relayed & (half == 0) & (frame < relay_count)

                    @pl.when(detour)
                    def _():
                        hand_over(frame, step, other).start()

                    @pl.when(jnp.logical_not(detour))
                    def _():
                        send(frame, other, me).start()

                    continue
                if step:
                    send(frame, other, me).start()
                    continue

                @pl.when(half == 0)
                def _():
                    send(frame, other, me).start()

                @pl.when(half != 0)
                def _():
                    keep(frame).start()
        else:
            place_half(frame, half).start()

    def one_piece(piece, carry):
        half = piece // frame_count
        frame = lax.rem(piece, frame_count)
        keys, values = [], []
        for slot in range(slot_count):
            chosen = jnp.where(used(frame, slot), matches[0, frame, slot], matches[0, frame, 0])
            block = lax.rem(chosen, 3) * key_count + lax.div(chosen, 3)
            keys.append(block)
            values.append(jnp.where(used(frame, slot), block, 3 * key_count))

        @pl.when((piece == frame_count) & jnp.logical_not(has_far))
        def _():
            project_queries(1)

        attend(piece, keys, values)
        finish_piece(half, frame)
        if relay_count:

            @pl.when(relays & (piece >= 1) & (piece <= relay_count))
            def _():
                for step in relay_steps:
                    hand_over(piece - 1, step, me).wait_recv()
                    pass_on(piece - 1, step).start()

        return carry

    def early_piece(piece, carry):
        own_keys, own_values = named(piece, 1)
        near_keys, near_values = named(piece, partners[0][1])
        attend(piece, own_keys + near_keys, own_values + near_values, early=True)

        @pl.when((piece == 0) & held)
        def _():
            start_halo()

        return carry

    def late_piece(piece, carry):
        attend(piece, *named(piece, partners[1][1]), late=True)
        finish_piece(jnp.int32(0), piece)
        return carry

    lax.fori_loop(0, early_count, early_piece, 0)

    @pl.when(has_far)
    def _():
        for key in range(key_count):
            halo(key).wait_recv()
            project_stills(1, partners[1][1], key, 1)
            if key == 0:

                @pl.when(jnp.logical_not(slow))
                def _():
                    project_queries(1)

    lax.fori_loop(0, early_count, late_piece, 0)
    lax.fori_loop(early_count, 2 * frame_count, one_piece, 0)

    @pl.when(has_far)
    def _():
        for key in range(key_count):
            halo(key).wait_send()

    for key in range(key_count):
        for chunk in range(chunk_count):
            for copy in shared(key, chunk, partners[1][1]):
                copy.wait_send()

    if relay_count:

        @pl.when(relays)
        def _():
            for frame in range(relay_count):
                for step in relay_steps:
                    pass_on(frame, step).wait_send()

    def finish(frame, carry):
        if exchange:

            def end(step, carry):
                other = lax.rem(me + step, tiles)
                send(frame, other, me).wait_send()
                send(frame, other, other).wait_recv()
                return carry

            lax.fori_loop(1, tiles, end, 0)
            keep(frame).wait()
        else:
            for half in range(2):
                place_half(frame, half).wait()
        return carry

    lax.fori_loop(0, frame_count, finish, 0)


def settle(src, out, held, in_sem, out_sem):
    frame_count, parts = in_sem.shape
    step = src.shape[1] // parts
    places = [(frame, pl.ds(part * step, step)) for frame in range(frame_count) for part in range(parts)]
    fetch = [
        pltpu.make_async_copy(src.at[at], held.at[at], in_sem.at[i // parts, i % parts])
        for i, at in enumerate(places)
    ]
    place = [
        pltpu.make_async_copy(held.at[at], out.at[at], out_sem.at[i // parts, i % parts])
        for i, at in enumerate(places)
    ]
    for copy in fetch:
        copy.start()
    for copy, back in zip(fetch, place):
        copy.wait()
        back.start()
    for back in place:
        back.wait()


def shards(tiles, frames, keyframes, matches, counts, w_query, w_key, w_value, w_out):
    frame_count, row_count, col_count, model_dim = frames.shape
    key_count = keyframes.shape[0]
    block_len = row_count * col_count
    half_cols = col_count // 2
    piece_len = row_count * half_cols
    slots = matches.shape[2]
    cols = col_count // tiles
    exchange = cols % 8 == 0 and tiles & (tiles - 1) == 0
    if exchange:
        out_shape = (frame_count, tiles, row_count * cols, model_dim)
        stage_shape = out_shape
    else:
        out_shape = (frame_count, row_count, col_count, model_dim)
        stage_shape = (frame_count, 2, row_count, half_cols, model_dim)
    weight = pltpu.VMEM((model_dim, model_dim), BF16)
    products = (4 * frame_count + 12 * key_count) * block_len * model_dim * model_dim
    products += 4 * frame_count * slots * block_len * block_len * model_dim
    mixed = pl.pallas_call(
        functools.partial(kernel, tiles, exchange),
        out_shape=jax.ShapeDtypeStruct(out_shape, BF16),
        in_specs=[pl.BlockSpec(memory_space=pl.ANY)] * 8,
        out_specs=pl.BlockSpec(memory_space=pl.ANY),
        scratch_shapes=[
            pltpu.SMEM(matches.shape, jnp.int32),
            pltpu.SMEM(counts.shape, jnp.int32),
            pltpu.VMEM((2, frame_count, row_count, half_cols, model_dim), BF16),
            pltpu.VMEM((2, key_count * block_len, model_dim), BF16),
            weight, weight, weight, weight,
            pltpu.VMEM((2 * frame_count, 2 * piece_len, model_dim), BF16),
            pltpu.VMEM((3 * key_count, model_dim, block_len), BF16),
            pltpu.VMEM((3 * key_count + 1, block_len, 2 * model_dim), BF16),
            pltpu.VMEM((piece_len, model_dim), BF16),
            pltpu.VMEM(stage_shape, BF16),
            pltpu.VMEM((min(RELAYED, frame_count), 4) + stage_shape[2:], BF16),
            pltpu.VMEM((2 * piece_len, slots * block_len), F32),
            pltpu.VMEM((2 * piece_len, slots * block_len), F32),
            pltpu.VMEM((2 * piece_len, PAIR), F32),
            pltpu.VMEM((2 * piece_len, PAIR), F32),
            pltpu.VMEM((frame_count, HEADS // 2, 2 * piece_len, 2 * PAIR), F32),
            pltpu.VMEM((frame_count, HEADS // 2, 2 * piece_len, PAIR), F32),
            pltpu.SemaphoreType.DMA((9,)),
            pltpu.SemaphoreType.DMA((key_count,)),
            pltpu.SemaphoreType.DMA((key_count,)),
            pltpu.SemaphoreType.DMA((2, key_count, model_dim // CHUNK)),
            pltpu.SemaphoreType.DMA((2, key_count, model_dim // CHUNK)),
            pltpu.SemaphoreType.DMA((min(RELAYED, frame_count), 4)),
            pltpu.SemaphoreType.DMA((min(RELAYED, frame_count), 4)),
            pltpu.SemaphoreType.DMA((frame_count, tiles)),
            pltpu.SemaphoreType.DMA((frame_count, tiles)),
            pltpu.SemaphoreType.DMA((2, frame_count)),
        ],
        compiler_params=pltpu.CompilerParams(
            collective_id=0, has_side_effects=True, vmem_limit_bytes=60 * 1024 * 1024
        ),
        cost_estimate=pl.CostEstimate(
            flops=products, bytes_accessed=16 * 1024 * 1024,
            transcendentals=frame_count * slots * HEADS * block_len * block_len,
        ),
        name="attend_and_relay",
    )(
        matches, counts, frames,
        keyframes.reshape(key_count * block_len, model_dim),
        w_query, w_key, w_value, w_out,
    )
    if exchange:
        mixed = pl.pallas_call(
            settle,
            out_shape=jax.ShapeDtypeStruct(out_shape, BF16),
            in_specs=[pl.BlockSpec(memory_space=pl.ANY)],
            out_specs=pl.BlockSpec(memory_space=pl.ANY),
            scratch_shapes=[
                pltpu.VMEM(out_shape, BF16),
                pltpu.SemaphoreType.DMA((frame_count, 2)),
                pltpu.SemaphoreType.DMA((frame_count, 2)),
            ],
            name="settle",
        )(mixed)
        return mixed.reshape(frame_count, tiles * row_count, cols, model_dim)
    return lax.all_to_all(mixed, "tile", split_axis=2, concat_axis=1, tiled=True)


def solution(mesh):
    placed = (
        P("clip", "tile", None, None),
        P("clip", "tile", None, None),
        P("tile", "clip", None),
        P("tile", "clip"),
        P(),
        P(),
        P(),
        P(),
    )
    return jax.shard_map(
        functools.partial(shards, mesh.shape["tile"]),
        mesh=mesh, in_specs=placed, out_specs=P("clip", None, "tile", None), check_vma=False,
    )
```

```python
import functools

import jax
import jax.numpy as jnp
from jax import lax
from jax.experimental import pallas as pl
from jax.experimental.pallas import tpu as pltpu
from jax.sharding import PartitionSpec as P

HEADS = 16
PAIR = 128
CHUNK = 512
FAST_EARLY = 1
GROUP = 8
RELAYED = 2
F32 = jnp.float32
BF16 = jnp.bfloat16


def kernel(
    tiles, exchange,
    matches_in, counts_in, frames_in, keys_in, wq_in, wk_in, wv_in, wo_in,
    out,
    matches, counts, frames, stills, wq, wk, wv, wo, queries, key_table, value_table, context,
    stage, relay, scores_even, scores_odd, max_even, max_odd, early_total, early_max,
    load_sem, halo_send, halo_recv, near_send, near_recv, relay_recv, relay_send, send_sem, recv_sem, own_sem,
):
    _, frame_count, rows, half_cols, model_dim = frames.shape
    piece_len = rows * half_cols
    block_len = 2 * piece_len
    key_count = stills.shape[1] // block_len
    slot_count = matches.shape[2]
    head_dim = model_dim // HEADS
    pair_count = model_dim // PAIR
    chunk_count = model_dim // CHUNK
    half_tiles = tiles // 2
    relay_count = relay.shape[0] if exchange and tiles == 16 else 0
    cols = half_cols // half_tiles
    me = lax.axis_index("tile")
    side = me // half_tiles

    def image_half(half):
        return jnp.where(half == 0, 1 - side, side)

    def half_columns(half):
        return pl.ds(pl.multiple_of(image_half(half) * half_cols, half_cols), half_cols)

    loads = [
        pltpu.make_async_copy(src, dst, load_sem.at[i])
        for i, (src, dst) in enumerate(
            [
                (keys_in, stills.at[0]), (wk_in, wk), (wv_in, wv),
                (frames_in.at[:, :, half_columns(0)], frames.at[0]), (wq_in, wq),
                (frames_in.at[:, :, half_columns(1)], frames.at[1]), (wo_in, wo),
                (matches_in, matches), (counts_in, counts),
            ]
        )
    ]
    for load in loads:
        load.start()

    barrier = pltpu.get_barrier_semaphore()

    def greet(step, carry):
        other = lax.rem(me + step, tiles)
        pl.semaphore_signal(
            barrier, inc=1, device_id={"tile": other}, device_id_type=pl.DeviceIdType.MESH
        )
        return carry

    lax.fori_loop(1, tiles, greet, 0)

    def fill(block):
        one = jnp.where(block < 3 * key_count, 1.0, 0.0).astype(BF16)
        for pair in range(pair_count):
            value_table[block, :, pl.ds(pair * 2 * PAIR + PAIR, PAIR)] = jnp.full(
                (block_len, PAIR), 1.0, F32
            ).astype(BF16) * one

    odd = lax.rem(me, 2)
    partners = ((me + 1 - 2 * odd, 2 - 2 * odd), (me - 1 + 2 * odd, 2 * odd))
    far = partners[1][0]
    has_far = (far >= 0) & (far < tiles)
    place = lax.rem(me, 4)
    inner = (place == 1) | (place == 2)
    slow = inner & (me != 1) & (me != tiles - 2)
    held = has_far & inner & (far != 1) & (far != tiles - 2)
    early_count = jnp.where(has_far, jnp.where(slow, frame_count, FAST_EARLY), 0)

    for key in range(key_count):
        fill(key_count + key)
        fill(partners[1][1] * key_count + key)
    fill(3 * key_count)
    for pair in range(pair_count):
        value_table[3 * key_count, :, pl.ds(pair * 2 * PAIR, PAIR)] = jnp.zeros(
            (block_len, PAIR), BF16
        )
    pl.semaphore_wait(barrier, tiles - 1)

    def halo(key):
        part = pl.ds(key * block_len, block_len)
        return pltpu.make_async_remote_copy(
            src_ref=keys_in.at[part], dst_ref=stills.at[1, part],
            send_sem=halo_send.at[key], recv_sem=halo_recv.at[key],
            device_id={"tile": far}, device_id_type=pl.DeviceIdType.MESH,
        )

    def start_halo():
        for key in range(key_count):
            halo(key).start()

    def shared(key, chunk, position):
        block = position * key_count + key
        own = key_count + key
        narrow = pl.ds(pl.multiple_of(chunk * CHUNK, CHUNK), CHUNK)
        wide = pl.ds(pl.multiple_of(chunk * 2 * CHUNK, 2 * CHUNK), 2 * CHUNK)
        pieces = (
            (key_table.at[own, narrow], key_table.at[block, narrow]),
            (value_table.at[own, :, wide], value_table.at[block, :, wide]),
        )
        return [
            pltpu.make_async_remote_copy(
                src_ref=src, dst_ref=dst,
                send_sem=near_send.at[kind, key, chunk], recv_sem=near_recv.at[kind, key, chunk],
                device_id={"tile": partners[0][0]}, device_id_type=pl.DeviceIdType.MESH,
            )
            for kind, (src, dst) in enumerate(pieces)
        ]

    @pl.when(has_far & jnp.logical_not(held))
    def _():
        start_halo()

    lane = lax.broadcasted_iota(jnp.int32, (piece_len, CHUNK), 1)
    even = lax.rem(lane, PAIR) < head_dim

    def project_queries(half):
        def step(chunk, carry):
            at = pl.ds(pl.multiple_of(chunk * CHUNK, CHUNK), CHUNK)
            tokens = frames[half].reshape(frame_count * piece_len, model_dim)
            q = jnp.dot(tokens, wq[:, at], preferred_element_type=F32)
            q = q * head_dim ** (-0.5)
            for frame in range(frame_count):
                part = q[frame * piece_len : (frame + 1) * piece_len]
                piece = half * frame_count + frame
                queries[piece, 0:piece_len, at] = jnp.where(even, part, 0.0).astype(BF16)
                queries[piece, piece_len : 2 * piece_len, at] = jnp.where(even, 0.0, part).astype(BF16)
            return carry

        lax.fori_loop(0, chunk_count, step, 0)

    def project_stills(source, slot, first, count, share=False):
        def step(chunk, carry):
            at = pl.ds(pl.multiple_of(chunk * CHUNK, CHUNK), CHUNK)
            tokens = stills[source, first * block_len : (first + count) * block_len, :]
            k = jnp.dot(tokens, wk[:, at], preferred_element_type=F32).astype(BF16)
            v = jnp.dot(tokens, wv[:, at], preferred_element_type=F32).astype(BF16)
            for key in range(count):
                part = slice(key * block_len, (key + 1) * block_len)
                block = slot * key_count + first + key
                key_table[block, at, :] = k[part].T
                for pair in range(CHUNK // PAIR):
                    to = pl.multiple_of(chunk * 2 * CHUNK + pair * 2 * PAIR, PAIR)
                    value_table[block, :, pl.ds(to, PAIR)] = v[part, pair * PAIR : (pair + 1) * PAIR]
                if share:
                    for copy in shared(key, chunk, partners[1][1]):
                        copy.start()
            return carry

        lax.fori_loop(0, chunk_count, step, 0)

    for load in loads[:3]:
        load.wait()
    project_stills(0, 1, 0, key_count, share=True)
    for load in loads[3:]:
        load.wait()

    def project_half(half, carry):
        project_queries(half)
        return carry

    lax.fori_loop(0, 2, project_half, 0)
    for key in range(key_count):
        for chunk in range(chunk_count):
            for copy in shared(key, chunk, partners[0][1]):
                copy.wait_recv()
    pair_lane = lax.broadcasted_iota(jnp.int32, (piece_len, PAIR), 1) < head_dim

    def send(frame, other, source):
        return pltpu.make_async_remote_copy(
            src_ref=stage.at[frame, other], dst_ref=out.at[frame, source],
            send_sem=send_sem.at[frame, other], recv_sem=recv_sem.at[frame, source],
            device_id={"tile": other}, device_id_type=pl.DeviceIdType.MESH,
        )

    def keep(frame):
        return pltpu.make_async_copy(stage.at[frame, me], out.at[frame, me], own_sem.at[0, frame])

    def place_half(frame, half):
        return pltpu.make_async_copy(
            stage.at[frame, image_half(half)], out.at[frame, :, half_columns(half)],
            own_sem.at[half, frame],
        )

    def attend(piece, keys, values, early=False, late=False):
        def score_block(q, slot, at, scores, most):
            s = jnp.dot(q, key_table[keys[slot], at, :], preferred_element_type=F32)
            scores[:, slot * block_len : (slot + 1) * block_len] = s
            for part in range(block_len // PAIR):
                some = s[:, part * PAIR : (part + 1) * PAIR]
                most = some if most is None else jnp.maximum(most, some)
            return most

        def value_block(slot, wide, scores, most, total):
            p = jnp.concatenate(
                [
                    jnp.exp(scores[:, at : at + PAIR] - most).astype(BF16)
                    for at in range(slot * block_len, (slot + 1) * block_len, PAIR)
                ],
                axis=1,
            )
            term = jnp.dot(p, value_table[values[slot], :, wide], preferred_element_type=F32)
            return term if total is None else total + term

        def close(most, pair, top):
            most = jnp.broadcast_to(jnp.max(most, axis=1, keepdims=True), top.shape)
            if late:
                most = jnp.maximum(most, early_max[piece, pair])
            top[...] = most

        def columns(pair, width):
            return pl.ds(pl.multiple_of(pair * width, width), width)

        def load_query(pair):
            return queries[piece, :, columns(pair, PAIR)]

        def step(pair, scores, top, next_pair, next_scores, next_top):
            most, total, next_most = top[...], None, None
            q = load_query(next_pair)
            if late:
                scale = jnp.exp(early_max[piece, pair] - most)
                total = early_total[piece, pair] * jnp.concatenate([scale, scale], axis=1)
            for slot in range(len(keys)):
                next_most = score_block(q, slot, columns(next_pair, PAIR), next_scores, next_most)
                total = value_block(slot, columns(pair, 2 * PAIR), scores, most, total)
            close(next_most, next_pair, next_top)
            if early:
                early_total[piece, pair] = total
                early_max[piece, pair] = most
                return None
            each = total[:, :PAIR] / total[:, PAIR:]
            both = jnp.where(pair_lane, each[:piece_len], each[piece_len:])
            context[:, columns(pair, PAIR)] = both.astype(BF16)

        most, q = None, load_query(0)
        for slot in range(len(keys)):
            most = score_block(q, slot, columns(0, PAIR), scores_even, most)
        close(most, 0, max_even)

        def group(index, carry):
            for inner_pair in range(0, GROUP, 2):
                pair = index * GROUP + inner_pair
                after = jnp.minimum(pair + 2, pair_count - 1)
                step(pair, scores_even, max_even, pair + 1, scores_odd, max_odd)
                step(pair + 1, scores_odd, max_odd, after, scores_even, max_even)
            return carry

        lax.fori_loop(0, pair_count // GROUP, group, 0)

    def used(frame, slot):
        return slot < counts[0, frame]

    def named(frame, position):
        keys, values = [], []
        for key in range(key_count):
            there = jnp.int32(0)
            for slot in range(slot_count):
                same = (matches[0, frame, slot] == key * 3 + position) & used(frame, slot)
                there = there + jnp.where(same, 1, 0)
            block = position * key_count + key
            keys.append(jnp.where(there > 0, block, key_count))
            values.append(jnp.where(there > 0, block, 3 * key_count))
        return keys, values

    def partner(half, step, source=me):
        top = lax.rem(source // half_tiles, 2)
        other, bit = jnp.where(half == 0, 1 - top, top) * half_tiles, 1
        while bit < half_tiles:
            mine = lax.rem(source // bit, 2)
            moved = 1 - mine if step // bit % 2 else mine
            if 2 * bit == half_tiles:
                moved = jnp.where(half == 0, step // bit % 2, moved)
            other = other + moved * bit
            bit *= 2
        return other

    across = me + 2 - 4 * lax.rem(me // 2, 2)
    relayed = (me == 3) | (me == tiles - 4)
    relays = (me == 1) | (me == tiles - 2)

    def relay_slot(step):
        return step // 4 * 2 + step % 2

    def hand_over(frame, step, other):
        return pltpu.make_async_remote_copy(
            src_ref=stage.at[frame, other], dst_ref=relay.at[frame, relay_slot(step)],
            send_sem=send_sem.at[frame, other], recv_sem=relay_recv.at[frame, relay_slot(step)],
            device_id={"tile": across}, device_id_type=pl.DeviceIdType.MESH,
        )

    def pass_on(frame, step):
        return pltpu.make_async_remote_copy(
            src_ref=relay.at[frame, relay_slot(step)], dst_ref=out.at[frame, across],
            send_sem=relay_send.at[frame, relay_slot(step)], recv_sem=recv_sem.at[frame, across],
            device_id={"tile": partner(0, step, across)}, device_id_type=pl.DeviceIdType.MESH,
        )

    relay_steps = [step for step in range(half_tiles) if step // 2 % 2]

    def finish_piece(half, frame, hold=None):
        for chunk in range(chunk_count):
            at = slice(chunk * CHUNK, (chunk + 1) * CHUNK)
            update = jnp.dot(context[...], wo[:, at], preferred_element_type=F32)
            mixed = frames[half, frame, :, :, at].reshape(piece_len, CHUNK).astype(F32) + update
            if exchange:
                first = image_half(half) * half_tiles
                for other in range(half_tiles):
                    group = [
                        mixed[row * half_cols + other * cols : row * half_cols + (other + 1) * cols]
                        for row in range(rows)
                    ]
                    stage[frame, first + other, :, at] = jnp.concatenate(group, axis=0).astype(BF16)
            else:
                stage[frame, image_half(half), :, :, at] = mixed.reshape(rows, half_cols, CHUNK).astype(BF16)

        if exchange:
            order = sorted(range(half_tiles), key=lambda step: (2 * step // half_tiles, step // 2 % 2, -step))
            for step in order:
                other = partner(half, step)
                if hold is not None and 2 * step >= half_tiles:
                    detour = relayed & (step in relay_steps) & (frame < relay_count)

                    @pl.when(detour)
                    def _():
                        hand_over(frame, step, other).start()

                    @pl.when(jnp.logical_not(detour | hold))
                    def _():
                        send(frame, other, me).start()

                    continue
                if step in relay_steps and relay_count:
                    detour = relayed & (half == 0) & (frame < relay_count)

                    @pl.when(detour)
                    def _():
                        hand_over(frame, step, other).start()

                    @pl.when(jnp.logical_not(detour))
                    def _():
                        send(frame, other, me).start()

                    continue
                if step:
                    send(frame, other, me).start()
                    continue

                @pl.when(half == 0)
                def _():
                    send(frame, other, me).start()

                @pl.when(half != 0)
                def _():
                    keep(frame).start()
        else:
            place_half(frame, half).start()

    def one_piece(piece, carry):
        half = piece // frame_count
        frame = lax.rem(piece, frame_count)
        keys, values = [], []
        for slot in range(slot_count):
            chosen = jnp.where(used(frame, slot), matches[0, frame, slot], matches[0, frame, 0])
            block = lax.rem(chosen, 3) * key_count + lax.div(chosen, 3)
            keys.append(block)
            values.append(jnp.where(used(frame, slot), block, 3 * key_count))

        attend(piece, keys, values)
        finish_piece(half, frame)
        if relay_count:

            @pl.when(relays & (piece >= 1) & (piece <= relay_count))
            def _():
                for step in relay_steps:
                    hand_over(piece - 1, step, me).wait_recv()
                    pass_on(piece - 1, step).start()

        return carry

    def early_piece(piece, carry):
        own_keys, own_values = named(piece, 1)
        near_keys, near_values = named(piece, partners[0][1])
        attend(piece, own_keys + near_keys, own_values + near_values, early=True)

        @pl.when((piece == 0) & held)
        def _():
            start_halo()

        return carry

    def late_piece(piece, carry):
        keys, values = named(piece, partners[1][1])
        attend(piece, keys[-1:], values[-1:], late=True)
        finish_piece(jnp.int32(0), piece, slow & (side == 1))
        return carry

    def middle_piece(key, piece, carry):
        keys, values = named(piece, partners[1][1])
        attend(piece, keys[key : key + 1], values[key : key + 1], early=True, late=True)
        return carry

    def held_sends(frame, carry):
        for step in range(half_tiles // 2, half_tiles):
            send(frame, partner(0, step), me).start()
        return carry

    lax.fori_loop(0, early_count, early_piece, 0)

    @pl.when(has_far)
    def _():
        for key in range(key_count):
            halo(key).wait_recv()
            project_stills(1, partners[1][1], key, 1)
            if key < key_count - 1:
                lax.fori_loop(0, early_count, functools.partial(middle_piece, key), 0)

    lax.fori_loop(0, early_count, late_piece, 0)
    if exchange:
        lax.fori_loop(0, jnp.where(slow & (side == 1), frame_count, 0), held_sends, 0)
    lax.fori_loop(early_count, 2 * frame_count, one_piece, 0)

    @pl.when(has_far)
    def _():
        for key in range(key_count):
            halo(key).wait_send()

    for key in range(key_count):
        for chunk in range(chunk_count):
            for copy in shared(key, chunk, partners[1][1]):
                copy.wait_send()

    if relay_count:

        @pl.when(relays)
        def _():
            for frame in range(relay_count):
                for step in relay_steps:
                    pass_on(frame, step).wait_send()

    def finish(frame, carry):
        if exchange:

            def end(step, carry):
                other = lax.rem(me + step, tiles)
                send(frame, other, me).wait_send()
                send(frame, other, other).wait_recv()
                return carry

            lax.fori_loop(1, tiles, end, 0)
            keep(frame).wait()
        else:
            for half in range(2):
                place_half(frame, half).wait()
        return carry

    lax.fori_loop(0, frame_count, finish, 0)


def settle(src, out, held, in_sem, out_sem):
    frame_count, parts = in_sem.shape
    step = src.shape[1] // parts
    places = [(frame, pl.ds(part * step, step)) for frame in range(frame_count) for part in range(parts)]
    fetch = [
        pltpu.make_async_copy(src.at[at], held.at[at], in_sem.at[i // parts, i % parts])
        for i, at in enumerate(places)
    ]
    place = [
        pltpu.make_async_copy(held.at[at], out.at[at], out_sem.at[i // parts, i % parts])
        for i, at in enumerate(places)
    ]
    for copy in fetch:
        copy.start()
    for copy, back in zip(fetch, place):
        copy.wait()
        back.start()
    for back in place:
        back.wait()


def shards(tiles, frames, keyframes, matches, counts, w_query, w_key, w_value, w_out):
    frame_count, row_count, col_count, model_dim = frames.shape
    key_count = keyframes.shape[0]
    block_len = row_count * col_count
    half_cols = col_count // 2
    piece_len = row_count * half_cols
    slots = matches.shape[2]
    cols = col_count // tiles
    exchange = cols % 8 == 0 and tiles & (tiles - 1) == 0
    if exchange:
        out_shape = (frame_count, tiles, row_count * cols, model_dim)
        stage_shape = out_shape
    else:
        out_shape = (frame_count, row_count, col_count, model_dim)
        stage_shape = (frame_count, 2, row_count, half_cols, model_dim)
    weight = pltpu.VMEM((model_dim, model_dim), BF16)
    products = (4 * frame_count + 12 * key_count) * block_len * model_dim * model_dim
    products += 4 * frame_count * slots * block_len * block_len * model_dim
    mixed = pl.pallas_call(
        functools.partial(kernel, tiles, exchange),
        out_shape=jax.ShapeDtypeStruct(out_shape, BF16),
        in_specs=[pl.BlockSpec(memory_space=pl.ANY)] * 8,
        out_specs=pl.BlockSpec(memory_space=pl.ANY),
        scratch_shapes=[
            pltpu.SMEM(matches.shape, jnp.int32),
            pltpu.SMEM(counts.shape, jnp.int32),
            pltpu.VMEM((2, frame_count, row_count, half_cols, model_dim), BF16),
            pltpu.VMEM((2, key_count * block_len, model_dim), BF16),
            weight, weight, weight, weight,
            pltpu.VMEM((2 * frame_count, 2 * piece_len, model_dim), BF16),
            pltpu.VMEM((3 * key_count, model_dim, block_len), BF16),
            pltpu.VMEM((3 * key_count + 1, block_len, 2 * model_dim), BF16),
            pltpu.VMEM((piece_len, model_dim), BF16),
            pltpu.VMEM(stage_shape, BF16),
            pltpu.VMEM((min(RELAYED, frame_count), 4) + stage_shape[2:], BF16),
            pltpu.VMEM((2 * piece_len, slots * block_len), F32),
            pltpu.VMEM((2 * piece_len, slots * block_len), F32),
            pltpu.VMEM((2 * piece_len, PAIR), F32),
            pltpu.VMEM((2 * piece_len, PAIR), F32),
            pltpu.VMEM((frame_count, HEADS // 2, 2 * piece_len, 2 * PAIR), F32),
            pltpu.VMEM((frame_count, HEADS // 2, 2 * piece_len, PAIR), F32),
            pltpu.SemaphoreType.DMA((9,)),
            pltpu.SemaphoreType.DMA((key_count,)),
            pltpu.SemaphoreType.DMA((key_count,)),
            pltpu.SemaphoreType.DMA((2, key_count, model_dim // CHUNK)),
            pltpu.SemaphoreType.DMA((2, key_count, model_dim // CHUNK)),
            pltpu.SemaphoreType.DMA((min(RELAYED, frame_count), 4)),
            pltpu.SemaphoreType.DMA((min(RELAYED, frame_count), 4)),
            pltpu.SemaphoreType.DMA((frame_count, tiles)),
            pltpu.SemaphoreType.DMA((frame_count, tiles)),
            pltpu.SemaphoreType.DMA((2, frame_count)),
        ],
        compiler_params=pltpu.CompilerParams(
            collective_id=0, has_side_effects=True, vmem_limit_bytes=60 * 1024 * 1024
        ),
        cost_estimate=pl.CostEstimate(
            flops=products, bytes_accessed=16 * 1024 * 1024,
            transcendentals=frame_count * slots * HEADS * block_len * block_len,
        ),
        name="attend_and_relay",
    )(
        matches, counts, frames,
        keyframes.reshape(key_count * block_len, model_dim),
        w_query, w_key, w_value, w_out,
    )
    if exchange:
        mixed = pl.pallas_call(
            settle,
            out_shape=jax.ShapeDtypeStruct(out_shape, BF16),
            in_specs=[pl.BlockSpec(memory_space=pl.ANY)],
            out_specs=pl.BlockSpec(memory_space=pl.ANY),
            scratch_shapes=[
                pltpu.VMEM(out_shape, BF16),
                pltpu.SemaphoreType.DMA((frame_count, 2)),
                pltpu.SemaphoreType.DMA((frame_count, 2)),
            ],
            name="settle",
        )(mixed)
        return mixed.reshape(frame_count, tiles * row_count, cols, model_dim)
    return lax.all_to_all(mixed, "tile", split_axis=2, concat_axis=1, tiled=True)


def solution(mesh):
    placed = (
        P("clip", "tile", None, None),
        P("clip", "tile", None, None),
        P("tile", "clip", None),
        P("tile", "clip"),
        P(),
        P(),
        P(),
        P(),
    )
    return jax.shard_map(
        functools.partial(shards, mesh.shape["tile"]),
        mesh=mesh, in_specs=placed, out_specs=P("clip", None, "tile", None), check_vma=False,
    )
```

```python
import functools

import jax
import jax.numpy as jnp
from jax import lax
from jax.experimental import pallas as pl
from jax.experimental.pallas import tpu as pltpu
from jax.sharding import PartitionSpec as P

HEADS = 16
PAIR = 128
CHUNK = 512
FAST_EARLY = 1
GATHER = 4
GROUP = 8
RELAYED = 2
F32 = jnp.float32
BF16 = jnp.bfloat16


def kernel(
    tiles, exchange,
    matches_in, counts_in, frames_in, keys_in, wq_in, wk_in, wv_in, wo_in,
    out,
    matches, counts, frames, stills, wq, wk, wv, wo, queries, key_table, value_table, context,
    stage, relay, scores_even, scores_odd, max_even, max_odd, early_total, early_max,
    gather_sem, lead_sem, open_sem, load_sem, weight_sem, halo_send, halo_recv, near_send, near_recv, relay_recv, relay_send, send_sem, recv_sem, own_sem,
):
    _, frame_count, rows, half_cols, model_dim = frames.shape
    piece_len = rows * half_cols
    block_len = 2 * piece_len
    key_count = stills.shape[1] // block_len
    slot_count = matches.shape[2]
    head_dim = model_dim // HEADS
    pair_count = model_dim // PAIR
    chunk_count = model_dim // CHUNK
    half_tiles = tiles // 2
    relay_count = relay.shape[0] if exchange and tiles == 16 else 0
    cols = half_cols // half_tiles
    me = lax.axis_index("tile")
    side = me // half_tiles

    def image_half(half):
        return jnp.where(half == 0, 1 - side, side)

    def half_columns(half):
        return pl.ds(pl.multiple_of(image_half(half) * half_cols, half_cols), half_cols)

    loads = [
        pltpu.make_async_copy(src, dst, load_sem.at[i])
        for i, (src, dst) in enumerate(
            [
                (keys_in, stills.at[0]),
                (frames_in.at[:, :, half_columns(0)], frames.at[0]), (wq_in, wq),
                (frames_in.at[:, :, half_columns(1)], frames.at[1]), (wo_in, wo),
                (matches_in, matches), (counts_in, counts),
            ]
        )
    ]

    def weight_load(which, chunk):
        at = pl.ds(pl.multiple_of(chunk * CHUNK, CHUNK), CHUNK)
        src, dst = ((wk_in, wk), (wv_in, wv))[which]
        return pltpu.make_async_copy(src.at[:, at], dst.at[:, at], weight_sem.at[which, chunk])

    loads[0].start()
    for chunk in range(chunk_count):
        for which in range(2):
            weight_load(which, chunk).start()
    for load in loads[1:]:
        load.start()

    barrier = pltpu.get_barrier_semaphore()

    def signal(semaphore, other):
        pl.semaphore_signal(
            semaphore, inc=1, device_id={"tile": other}, device_id_type=pl.DeviceIdType.MESH
        )

    odd = lax.rem(me, 2)
    partners = ((me + 1 - 2 * odd, 2 - 2 * odd), (me - 1 + 2 * odd, 2 * odd))
    far = partners[1][0]
    has_far = (far >= 0) & (far < tiles)
    place = lax.rem(me, GATHER)
    inner = (place == 1) | (place == 2)
    slow = inner & (me != 1) & (me != tiles - 2)
    held = has_far & inner & (far != 1) & (far != tiles - 2)
    early_count = jnp.where(has_far, jnp.where(slow, frame_count, FAST_EARLY), 0)

    groups = tiles // GATHER
    leads = place == 0

    def greet(step, carry):
        signal(barrier, lax.rem(me + step * GATHER, tiles))
        return carry

    signal(barrier, partners[0][0])

    @pl.when(has_far)
    def _():
        signal(barrier, far)

    @pl.when(leads)
    def _():
        lax.fori_loop(1, groups, greet, 0)
        for step in range(2, GATHER):
            signal(barrier, me + step)

    value_table[3 * key_count] = jnp.zeros((block_len, model_dim), BF16)
    known = jnp.where(leads, groups - 1, jnp.where(place >= 2, 1, 0))
    pl.semaphore_wait(barrier, 1 + jnp.where(has_far, 1, 0) + known)

    def halo(key):
        part = pl.ds(key * block_len, block_len)
        return pltpu.make_async_remote_copy(
            src_ref=keys_in.at[part], dst_ref=stills.at[1, part],
            send_sem=halo_send.at[key], recv_sem=halo_recv.at[key],
            device_id={"tile": far}, device_id_type=pl.DeviceIdType.MESH,
        )

    def start_halo():
        for key in range(key_count):
            halo(key).start()

    def shared(key, chunk, position):
        block = position * key_count + key
        own = key_count + key
        narrow = pl.ds(pl.multiple_of(chunk * CHUNK, CHUNK), CHUNK)
        pieces = (
            (key_table.at[own, narrow], key_table.at[block, narrow]),
            (value_table.at[own, :, narrow], value_table.at[block, :, narrow]),
        )
        return [
            pltpu.make_async_remote_copy(
                src_ref=src, dst_ref=dst,
                send_sem=near_send.at[kind, key, chunk], recv_sem=near_recv.at[kind, key, chunk],
                device_id={"tile": partners[0][0]}, device_id_type=pl.DeviceIdType.MESH,
            )
            for kind, (src, dst) in enumerate(pieces)
        ]

    @pl.when(has_far & jnp.logical_not(held))
    def _():
        start_halo()

    if exchange:

        @pl.when(jnp.logical_not(leads))
        def _():
            signal(gather_sem, me - place)

    lane = lax.broadcasted_iota(jnp.int32, (piece_len, CHUNK), 1)
    even = lax.rem(lane, PAIR) < head_dim

    def project_queries(half):
        def step(chunk, carry):
            at = pl.ds(pl.multiple_of(chunk * CHUNK, CHUNK), CHUNK)
            tokens = frames[half].reshape(frame_count * piece_len, model_dim)
            q = jnp.dot(tokens, wq[:, at], preferred_element_type=F32)
            q = q * head_dim ** (-0.5)
            for frame in range(frame_count):
                part = q[frame * piece_len : (frame + 1) * piece_len]
                piece = half * frame_count + frame
                queries[piece, 0:piece_len, at] = jnp.where(even, part, 0.0).astype(BF16)
                queries[piece, piece_len : 2 * piece_len, at] = jnp.where(even, 0.0, part).astype(BF16)
            return carry

        lax.fori_loop(0, chunk_count, step, 0)

    def project_stills(source, slot, first, count, share=False):
        def step(chunk, carry):
            at = pl.ds(pl.multiple_of(chunk * CHUNK, CHUNK), CHUNK)
            if share:
                for which in range(2):
                    weight_load(which, chunk).wait()
            tokens = stills[source, first * block_len : (first + count) * block_len, :]
            k = jnp.dot(tokens, wk[:, at], preferred_element_type=F32).astype(BF16)
            v = jnp.dot(tokens, wv[:, at], preferred_element_type=F32).astype(BF16)
            for key in range(count):
                part = slice(key * block_len, (key + 1) * block_len)
                block = slot * key_count + first + key
                key_table[block, at, :] = k[part].T
                value_table[block, :, at] = v[part]
                if share:
                    for copy in shared(key, chunk, partners[1][1]):
                        copy.start()
            return carry

        lax.fori_loop(0, chunk_count, step, 0)

    loads[0].wait()
    project_stills(0, 1, 0, key_count, share=True)

    def tell(step, carry):
        signal(lead_sem, lax.rem(me + step * GATHER, tiles))
        return carry

    if exchange:

        @pl.when(leads)
        def _():
            pl.semaphore_wait(gather_sem, GATHER - 1)
            lax.fori_loop(1, groups, tell, 0)

    for load in loads[1:]:
        load.wait()

    def project_half(half, carry):
        project_queries(half)
        return carry

    lax.fori_loop(0, 2, project_half, 0)
    if exchange:

        @pl.when(leads)
        def _():
            pl.semaphore_wait(lead_sem, groups - 1)
            for step in range(1, GATHER):
                signal(open_sem, me + step)

    for key in range(key_count):
        for chunk in range(chunk_count):
            for copy in shared(key, chunk, partners[0][1]):
                copy.wait_recv()
    pair_lane = lax.broadcasted_iota(jnp.int32, (piece_len, PAIR), 1) < head_dim

    def send(frame, other, source):
        return pltpu.make_async_remote_copy(
            src_ref=stage.at[frame, other], dst_ref=out.at[frame, source],
            send_sem=send_sem.at[frame, other], recv_sem=recv_sem.at[frame, source],
            device_id={"tile": other}, device_id_type=pl.DeviceIdType.MESH,
        )

    def keep(frame):
        return pltpu.make_async_copy(stage.at[frame, me], out.at[frame, me], own_sem.at[0, frame])

    def place_half(frame, half):
        return pltpu.make_async_copy(
            stage.at[frame, image_half(half)], out.at[frame, :, half_columns(half)],
            own_sem.at[half, frame],
        )

    def attend(piece, keys, values, early=False, late=False):
        ones = [
            jnp.full((block_len, PAIR), jnp.where(block < 3 * key_count, 1.0, 0.0), F32).astype(BF16)
            for block in values
        ]

        def score_block(q, slot, at, scores, most):
            s = jnp.dot(q, key_table[keys[slot], at, :], preferred_element_type=F32)
            scores[:, slot * block_len : (slot + 1) * block_len] = s
            for part in range(block_len // PAIR):
                some = s[:, part * PAIR : (part + 1) * PAIR]
                most = some if most is None else jnp.maximum(most, some)
            return most

        def value_block(slot, at, scores, most, total):
            p = jnp.concatenate(
                [
                    jnp.exp(scores[:, part : part + PAIR] - most).astype(BF16)
                    for part in range(slot * block_len, (slot + 1) * block_len, PAIR)
                ],
                axis=1,
            )
            both = jnp.concatenate([value_table[values[slot], :, at], ones[slot]], axis=1)
            term = jnp.dot(p, both, preferred_element_type=F32)
            return term if total is None else total + term

        def close(most, pair, top):
            most = jnp.broadcast_to(jnp.max(most, axis=1, keepdims=True), top.shape)
            if late:
                most = jnp.maximum(most, early_max[piece, pair])
            top[...] = most

        def columns(pair, width):
            return pl.ds(pl.multiple_of(pair * width, width), width)

        def load_query(pair):
            return queries[piece, :, columns(pair, PAIR)]

        def step(pair, scores, top, next_pair, next_scores, next_top):
            most, total, next_most = top[...], None, None
            q = load_query(next_pair)
            if late:
                scale = jnp.exp(early_max[piece, pair] - most)
                total = early_total[piece, pair] * jnp.concatenate([scale, scale], axis=1)
            for slot in range(len(keys)):
                next_most = score_block(q, slot, columns(next_pair, PAIR), next_scores, next_most)
                total = value_block(slot, columns(pair, PAIR), scores, most, total)
            close(next_most, next_pair, next_top)
            if early:
                early_total[piece, pair] = total
                early_max[piece, pair] = most
                return None
            each = total[:, :PAIR] / total[:, PAIR:]
            both = jnp.where(pair_lane, each[:piece_len], each[piece_len:])
            context[:, columns(pair, PAIR)] = both.astype(BF16)

        most, q = None, load_query(0)
        for slot in range(len(keys)):
            most = score_block(q, slot, columns(0, PAIR), scores_even, most)
        close(most, 0, max_even)

        def group(index, carry):
            for inner_pair in range(0, GROUP, 2):
                pair = index * GROUP + inner_pair
                after = jnp.minimum(pair + 2, pair_count - 1)
                step(pair, scores_even, max_even, pair + 1, scores_odd, max_odd)
                step(pair + 1, scores_odd, max_odd, after, scores_even, max_even)
            return carry

        lax.fori_loop(0, pair_count // GROUP, group, 0)

    def used(frame, slot):
        return slot < counts[0, frame]

    def named(frame, position):
        keys, values = [], []
        for key in range(key_count):
            there = jnp.int32(0)
            for slot in range(slot_count):
                same = (matches[0, frame, slot] == key * 3 + position) & used(frame, slot)
                there = there + jnp.where(same, 1, 0)
            block = position * key_count + key
            keys.append(jnp.where(there > 0, block, key_count))
            values.append(jnp.where(there > 0, block, 3 * key_count))
        return keys, values

    def partner(half, step, source=me):
        top = lax.rem(source // half_tiles, 2)
        other, bit = jnp.where(half == 0, 1 - top, top) * half_tiles, 1
        while bit < half_tiles:
            mine = lax.rem(source // bit, 2)
            moved = 1 - mine if step // bit % 2 else mine
            if 2 * bit == half_tiles:
                moved = jnp.where(half == 0, step // bit % 2, moved)
            other = other + moved * bit
            bit *= 2
        return other

    across = me + 2 - 4 * lax.rem(me // 2, 2)
    relayed = (me == 3) | (me == tiles - 4)
    relays = (me == 1) | (me == tiles - 2)

    def relay_slot(step):
        return step // 4 * 2 + step % 2

    def hand_over(frame, step, other):
        return pltpu.make_async_remote_copy(
            src_ref=stage.at[frame, other], dst_ref=relay.at[frame, relay_slot(step)],
            send_sem=send_sem.at[frame, other], recv_sem=relay_recv.at[frame, relay_slot(step)],
            device_id={"tile": across}, device_id_type=pl.DeviceIdType.MESH,
        )

    def pass_on(frame, step):
        return pltpu.make_async_remote_copy(
            src_ref=relay.at[frame, relay_slot(step)], dst_ref=out.at[frame, across],
            send_sem=relay_send.at[frame, relay_slot(step)], recv_sem=recv_sem.at[frame, across],
            device_id={"tile": partner(0, step, across)}, device_id_type=pl.DeviceIdType.MESH,
        )

    relay_steps = [step for step in range(half_tiles) if step // 2 % 2]

    def finish_piece(half, frame, hold=None):
        for chunk in range(chunk_count):
            at = slice(chunk * CHUNK, (chunk + 1) * CHUNK)
            update = jnp.dot(context[...], wo[:, at], preferred_element_type=F32)
            mixed = frames[half, frame, :, :, at].reshape(piece_len, CHUNK).astype(F32) + update
            if exchange:
                first = image_half(half) * half_tiles
                for other in range(half_tiles):
                    group = [
                        mixed[row * half_cols + other * cols : row * half_cols + (other + 1) * cols]
                        for row in range(rows)
                    ]
                    stage[frame, first + other, :, at] = jnp.concatenate(group, axis=0).astype(BF16)
            else:
                stage[frame, image_half(half), :, :, at] = mixed.reshape(rows, half_cols, CHUNK).astype(BF16)

        if exchange:
            order = sorted(range(half_tiles), key=lambda step: (2 * step // half_tiles, step // 2 % 2, -step))
            for step in order:
                other = partner(half, step)
                if hold is not None and 2 * step >= half_tiles:
                    detour = relayed & (step in relay_steps) & (frame < relay_count)

                    @pl.when(detour)
                    def _():
                        hand_over(frame, step, other).start()

                    @pl.when(jnp.logical_not(detour | hold))
                    def _():
                        send(frame, other, me).start()

                    continue
                if step in relay_steps and relay_count:
                    detour = relayed & (half == 0) & (frame < relay_count)

                    @pl.when(detour)
                    def _():
                        hand_over(frame, step, other).start()

                    @pl.when(jnp.logical_not(detour))
                    def _():
                        send(frame, other, me).start()

                    continue
                if step:
                    send(frame, other, me).start()
                    continue

                @pl.when(half == 0)
                def _():
                    send(frame, other, me).start()

                @pl.when(half != 0)
                def _():
                    keep(frame).start()
        else:
            place_half(frame, half).start()

    def one_piece(piece, carry):
        half = piece // frame_count
        frame = lax.rem(piece, frame_count)
        keys, values = [], []
        for slot in range(slot_count):
            chosen = jnp.where(used(frame, slot), matches[0, frame, slot], matches[0, frame, 0])
            block = lax.rem(chosen, 3) * key_count + lax.div(chosen, 3)
            keys.append(block)
            values.append(jnp.where(used(frame, slot), block, 3 * key_count))

        attend(piece, keys, values)
        finish_piece(half, frame)
        if relay_count:

            @pl.when(relays & (piece >= 1) & (piece <= relay_count))
            def _():
                for step in relay_steps:
                    hand_over(piece - 1, step, me).wait_recv()
                    pass_on(piece - 1, step).start()

        return carry

    def early_piece(piece, carry):
        own_keys, own_values = named(piece, 1)
        near_keys, near_values = named(piece, partners[0][1])
        attend(piece, own_keys + near_keys, own_values + near_values, early=True)

        @pl.when((piece == 0) & held)
        def _():
            start_halo()

        return carry

    def late_piece(piece, carry):
        keys, values = named(piece, partners[1][1])
        attend(piece, keys[-1:], values[-1:], late=True)
        finish_piece(jnp.int32(0), piece, slow & (side == 1))
        return carry

    def middle_piece(key, piece, carry):
        keys, values = named(piece, partners[1][1])
        attend(piece, keys[key : key + 1], values[key : key + 1], early=True, late=True)
        return carry

    def held_sends(frame, carry):
        for step in range(half_tiles // 2, half_tiles):
            send(frame, partner(0, step), me).start()
        return carry

    lax.fori_loop(0, early_count, early_piece, 0)
    if exchange:

        @pl.when(jnp.logical_not(leads))
        def _():
            pl.semaphore_wait(open_sem, 1)


    @pl.when(has_far)
    def _():
        for key in range(key_count):
            halo(key).wait_recv()
            project_stills(1, partners[1][1], key, 1)
            if key < key_count - 1:
                lax.fori_loop(0, early_count, functools.partial(middle_piece, key), 0)

    lax.fori_loop(0, early_count, late_piece, 0)
    if exchange:
        lax.fori_loop(0, jnp.where(slow & (side == 1), frame_count, 0), held_sends, 0)
    lax.fori_loop(early_count, 2 * frame_count, one_piece, 0)

    @pl.when(has_far)
    def _():
        for key in range(key_count):
            halo(key).wait_send()

    for key in range(key_count):
        for chunk in range(chunk_count):
            for copy in shared(key, chunk, partners[1][1]):
                copy.wait_send()

    if relay_count:

        @pl.when(relays)
        def _():
            for frame in range(relay_count):
                for step in relay_steps:
                    pass_on(frame, step).wait_send()

    def finish(frame, carry):
        if exchange:

            def end(step, carry):
                other = lax.rem(me + step, tiles)
                send(frame, other, me).wait_send()
                send(frame, other, other).wait_recv()
                return carry

            lax.fori_loop(1, tiles, end, 0)
            keep(frame).wait()
        else:
            for half in range(2):
                place_half(frame, half).wait()
        return carry

    lax.fori_loop(0, frame_count, finish, 0)


def settle(src, out, held, in_sem, out_sem):
    frame_count, parts = in_sem.shape
    step = src.shape[1] // parts
    places = [(frame, pl.ds(part * step, step)) for frame in range(frame_count) for part in range(parts)]
    fetch = [
        pltpu.make_async_copy(src.at[at], held.at[at], in_sem.at[i // parts, i % parts])
        for i, at in enumerate(places)
    ]
    place = [
        pltpu.make_async_copy(held.at[at], out.at[at], out_sem.at[i // parts, i % parts])
        for i, at in enumerate(places)
    ]
    for copy in fetch:
        copy.start()
    for copy, back in zip(fetch, place):
        copy.wait()
        back.start()
    for back in place:
        back.wait()


def shards(tiles, frames, keyframes, matches, counts, w_query, w_key, w_value, w_out):
    frame_count, row_count, col_count, model_dim = frames.shape
    key_count = keyframes.shape[0]
    block_len = row_count * col_count
    half_cols = col_count // 2
    piece_len = row_count * half_cols
    slots = matches.shape[2]
    cols = col_count // tiles
    exchange = cols % 8 == 0 and tiles & (tiles - 1) == 0 and tiles >= 8
    if exchange:
        out_shape = (frame_count, tiles, row_count * cols, model_dim)
        stage_shape = out_shape
    else:
        out_shape = (frame_count, row_count, col_count, model_dim)
        stage_shape = (frame_count, 2, row_count, half_cols, model_dim)
    weight = pltpu.VMEM((model_dim, model_dim), BF16)
    products = (4 * frame_count + 12 * key_count) * block_len * model_dim * model_dim
    products += 4 * frame_count * slots * block_len * block_len * model_dim
    mixed = pl.pallas_call(
        functools.partial(kernel, tiles, exchange),
        out_shape=jax.ShapeDtypeStruct(out_shape, BF16),
        in_specs=[pl.BlockSpec(memory_space=pl.ANY)] * 8,
        out_specs=pl.BlockSpec(memory_space=pl.ANY),
        scratch_shapes=[
            pltpu.SMEM(matches.shape, jnp.int32),
            pltpu.SMEM(counts.shape, jnp.int32),
            pltpu.VMEM((2, frame_count, row_count, half_cols, model_dim), BF16),
            pltpu.VMEM((2, key_count * block_len, model_dim), BF16),
            weight, weight, weight, weight,
            pltpu.VMEM((2 * frame_count, 2 * piece_len, model_dim), BF16),
            pltpu.VMEM((3 * key_count, model_dim, block_len), BF16),
            pltpu.VMEM((3 * key_count + 1, block_len, model_dim), BF16),
            pltpu.VMEM((piece_len, model_dim), BF16),
            pltpu.VMEM(stage_shape, BF16),
            pltpu.VMEM((min(RELAYED, frame_count), 4) + stage_shape[2:], BF16),
            pltpu.VMEM((2 * piece_len, slots * block_len), F32),
            pltpu.VMEM((2 * piece_len, slots * block_len), F32),
            pltpu.VMEM((2 * piece_len, PAIR), F32),
            pltpu.VMEM((2 * piece_len, PAIR), F32),
            pltpu.VMEM((frame_count, HEADS // 2, 2 * piece_len, 2 * PAIR), F32),
            pltpu.VMEM((frame_count, HEADS // 2, 2 * piece_len, PAIR), F32),
            pltpu.SemaphoreType.REGULAR,
            pltpu.SemaphoreType.REGULAR,
            pltpu.SemaphoreType.REGULAR,
            pltpu.SemaphoreType.DMA((7,)),
            pltpu.SemaphoreType.DMA((2, model_dim // CHUNK)),
            pltpu.SemaphoreType.DMA((key_count,)),
            pltpu.SemaphoreType.DMA((key_count,)),
            pltpu.SemaphoreType.DMA((2, key_count, model_dim // CHUNK)),
            pltpu.SemaphoreType.DMA((2, key_count, model_dim // CHUNK)),
            pltpu.SemaphoreType.DMA((min(RELAYED, frame_count), 4)),
            pltpu.SemaphoreType.DMA((min(RELAYED, frame_count), 4)),
            pltpu.SemaphoreType.DMA((frame_count, tiles)),
            pltpu.SemaphoreType.DMA((frame_count, tiles)),
            pltpu.SemaphoreType.DMA((2, frame_count)),
        ],
        compiler_params=pltpu.CompilerParams(
            collective_id=0, has_side_effects=True, vmem_limit_bytes=60 * 1024 * 1024
        ),
        cost_estimate=pl.CostEstimate(
            flops=products, bytes_accessed=16 * 1024 * 1024,
            transcendentals=frame_count * slots * HEADS * block_len * block_len,
        ),
        name="attend_and_relay",
    )(
        matches, counts, frames,
        keyframes.reshape(key_count * block_len, model_dim),
        w_query, w_key, w_value, w_out,
    )
    if exchange:
        mixed = pl.pallas_call(
            settle,
            out_shape=jax.ShapeDtypeStruct(out_shape, BF16),
            in_specs=[pl.BlockSpec(memory_space=pl.ANY)],
            out_specs=pl.BlockSpec(memory_space=pl.ANY),
            scratch_shapes=[
                pltpu.VMEM(out_shape, BF16),
                pltpu.SemaphoreType.DMA((frame_count, 2)),
                pltpu.SemaphoreType.DMA((frame_count, 2)),
            ],
            name="settle",
        )(mixed)
        return mixed.reshape(frame_count, tiles * row_count, cols, model_dim)
    return lax.all_to_all(mixed, "tile", split_axis=2, concat_axis=1, tiled=True)


def solution(mesh):
    placed = (
        P("clip", "tile", None, None),
        P("clip", "tile", None, None),
        P("tile", "clip", None),
        P("tile", "clip"),
        P(),
        P(),
        P(),
        P(),
    )
    return jax.shard_map(
        functools.partial(shards, mesh.shape["tile"]),
        mesh=mesh, in_specs=placed, out_specs=P("clip", None, "tile", None), check_vma=False,
    )
```

```python
import functools

import jax
import jax.numpy as jnp
from jax import lax
from jax.experimental import pallas as pl
from jax.experimental.pallas import tpu as pltpu
from jax.sharding import PartitionSpec as P

HEADS = 16
PAIR = 128
CHUNK = 512
FAST_EARLY = 1
GATHER = 4
GROUP = 8
RELAYED = (2, 2)
F32 = jnp.float32
BF16 = jnp.bfloat16


def kernel(
    tiles, exchange,
    matches_in, counts_in, frames_in, keys_in, wq_in, wk_in, wv_in, wo_in,
    out,
    matches, counts, frames, stills, wq, wk, wv, wo, queries, key_table, value_table, context,
    stage, relay, scores_even, scores_odd, max_even, max_odd, early_total, early_max,
    gather_sem, lead_sem, open_sem, load_sem, weight_sem, halo_send, halo_recv, near_send, near_recv, relay_recv, relay_send, send_sem, recv_sem, own_sem,
):
    _, frame_count, rows, half_cols, model_dim = frames.shape
    piece_len = rows * half_cols
    block_len = 2 * piece_len
    key_count = stills.shape[1] // block_len
    slot_count = matches.shape[2]
    head_dim = model_dim // HEADS
    pair_count = model_dim // PAIR
    chunk_count = model_dim // CHUNK
    half_tiles = tiles // 2
    relay_count = relay.shape[0] if exchange and tiles == 16 else 0
    cols = half_cols // half_tiles
    me = lax.axis_index("tile")
    side = me // half_tiles
    relay_limit = jnp.where(side == 0, RELAYED[0], RELAYED[1])

    def image_half(half):
        return jnp.where(half == 0, 1 - side, side)

    def half_columns(half):
        return pl.ds(pl.multiple_of(image_half(half) * half_cols, half_cols), half_cols)

    loads = [
        pltpu.make_async_copy(src, dst, load_sem.at[i])
        for i, (src, dst) in enumerate(
            [
                (keys_in, stills.at[0]),
                (frames_in.at[:, :, half_columns(0)], frames.at[0]), (wq_in, wq),
                (frames_in.at[:, :, half_columns(1)], frames.at[1]), (wo_in, wo),
                (matches_in, matches), (counts_in, counts),
            ]
        )
    ]

    def weight_load(which, chunk):
        at = pl.ds(pl.multiple_of(chunk * CHUNK, CHUNK), CHUNK)
        src, dst = ((wk_in, wk), (wv_in, wv))[which]
        return pltpu.make_async_copy(src.at[:, at], dst.at[:, at], weight_sem.at[which, chunk])

    loads[0].start()
    for chunk in range(chunk_count):
        for which in range(2):
            weight_load(which, chunk).start()

    barrier = pltpu.get_barrier_semaphore()

    def signal(semaphore, other):
        pl.semaphore_signal(
            semaphore, inc=1, device_id={"tile": other}, device_id_type=pl.DeviceIdType.MESH
        )

    odd = lax.rem(me, 2)
    partners = ((me + 1 - 2 * odd, 2 - 2 * odd), (me - 1 + 2 * odd, 2 * odd))
    far = partners[1][0]
    has_far = (far >= 0) & (far < tiles)
    place = lax.rem(me, GATHER)
    inner = (place == 1) | (place == 2)
    slow = inner & (me != 1) & (me != tiles - 2)
    held = has_far & inner & (far != 1) & (far != tiles - 2)
    early_count = jnp.where(has_far, jnp.where(slow, frame_count, FAST_EARLY), 0)

    groups = tiles // GATHER
    leads = place == 0

    def greet(step, carry):
        signal(barrier, lax.rem(me + step * GATHER, tiles))
        return carry

    signal(barrier, partners[0][0])

    @pl.when(has_far)
    def _():
        signal(barrier, far)

    @pl.when(leads)
    def _():
        lax.fori_loop(1, groups, greet, 0)
        for step in range(2, GATHER):
            signal(barrier, me + step)

    value_table[3 * key_count] = jnp.zeros((block_len, model_dim), BF16)
    known = jnp.where(leads, groups - 1, jnp.where(place >= 2, 1, 0))
    pl.semaphore_wait(barrier, 1 + jnp.where(has_far, 1, 0) + known)

    def halo(key):
        part = pl.ds(key * block_len, block_len)
        return pltpu.make_async_remote_copy(
            src_ref=keys_in.at[part], dst_ref=stills.at[1, part],
            send_sem=halo_send.at[key], recv_sem=halo_recv.at[key],
            device_id={"tile": far}, device_id_type=pl.DeviceIdType.MESH,
        )

    def start_halo():
        for key in range(key_count):
            halo(key).start()

    def shared(key, chunk, position):
        block = position * key_count + key
        own = key_count + key
        narrow = pl.ds(pl.multiple_of(chunk * CHUNK, CHUNK), CHUNK)
        pieces = (
            (key_table.at[own, narrow], key_table.at[block, narrow]),
            (value_table.at[own, :, narrow], value_table.at[block, :, narrow]),
        )
        return [
            pltpu.make_async_remote_copy(
                src_ref=src, dst_ref=dst,
                send_sem=near_send.at[kind, key, chunk], recv_sem=near_recv.at[kind, key, chunk],
                device_id={"tile": partners[0][0]}, device_id_type=pl.DeviceIdType.MESH,
            )
            for kind, (src, dst) in enumerate(pieces)
        ]

    @pl.when(has_far & jnp.logical_not(held))
    def _():
        start_halo()

    if exchange:

        @pl.when(jnp.logical_not(leads))
        def _():
            signal(gather_sem, me - place)

    lane = lax.broadcasted_iota(jnp.int32, (piece_len, CHUNK), 1)
    even = lax.rem(lane, PAIR) < head_dim

    def project_queries(half):
        def step(chunk, carry):
            at = pl.ds(pl.multiple_of(chunk * CHUNK, CHUNK), CHUNK)
            tokens = frames[half].reshape(frame_count * piece_len, model_dim)
            q = jnp.dot(tokens, wq[:, at], preferred_element_type=F32)
            q = q * head_dim ** (-0.5)
            for frame in range(frame_count):
                part = q[frame * piece_len : (frame + 1) * piece_len]
                piece = half * frame_count + frame
                queries[piece, 0:piece_len, at] = jnp.where(even, part, 0.0).astype(BF16)
                queries[piece, piece_len : 2 * piece_len, at] = jnp.where(even, 0.0, part).astype(BF16)
            return carry

        lax.fori_loop(0, chunk_count, step, 0)

    def project_stills(source, slot, first, count, share=False):
        def step(chunk, carry):
            at = pl.ds(pl.multiple_of(chunk * CHUNK, CHUNK), CHUNK)
            if share:
                for which in range(2):
                    weight_load(which, chunk).wait()

                @pl.when(chunk == 0)
                def _():
                    for load in loads[1:]:
                        load.start()

            tokens = stills[source, first * block_len : (first + count) * block_len, :]
            k = jnp.dot(tokens, wk[:, at], preferred_element_type=F32).astype(BF16)
            v = jnp.dot(tokens, wv[:, at], preferred_element_type=F32).astype(BF16)
            for key in range(count):
                part = slice(key * block_len, (key + 1) * block_len)
                block = slot * key_count + first + key
                key_table[block, at, :] = k[part].T
                value_table[block, :, at] = v[part]
                if share:
                    for copy in shared(key, chunk, partners[1][1]):
                        copy.start()
            return carry

        lax.fori_loop(0, chunk_count, step, 0)

    loads[0].wait()
    project_stills(0, 1, 0, key_count, share=True)

    def tell(step, carry):
        signal(lead_sem, lax.rem(me + step * GATHER, tiles))
        return carry

    if exchange:

        @pl.when(leads)
        def _():
            pl.semaphore_wait(gather_sem, GATHER - 1)
            lax.fori_loop(1, groups, tell, 0)

    for load in loads[1:]:
        load.wait()

    def project_half(half, carry):
        project_queries(half)
        return carry

    lax.fori_loop(0, 2, project_half, 0)
    if exchange:

        @pl.when(leads)
        def _():
            pl.semaphore_wait(lead_sem, groups - 1)
            for step in range(1, GATHER):
                signal(open_sem, me + step)

    for key in range(key_count):
        for chunk in range(chunk_count):
            for copy in shared(key, chunk, partners[0][1]):
                copy.wait_recv()
    pair_lane = lax.broadcasted_iota(jnp.int32, (piece_len, PAIR), 1) < head_dim

    def send(frame, other, source):
        return pltpu.make_async_remote_copy(
            src_ref=stage.at[frame, other], dst_ref=out.at[frame, source],
            send_sem=send_sem.at[frame, other], recv_sem=recv_sem.at[frame, source],
            device_id={"tile": other}, device_id_type=pl.DeviceIdType.MESH,
        )

    def keep(frame):
        return pltpu.make_async_copy(stage.at[frame, me], out.at[frame, me], own_sem.at[0, frame])

    def place_half(frame, half):
        return pltpu.make_async_copy(
            stage.at[frame, image_half(half)], out.at[frame, :, half_columns(half)],
            own_sem.at[half, frame],
        )

    def attend(piece, keys, values, early=False, late=False):
        ones = [
            jnp.full((block_len, PAIR), jnp.where(block < 3 * key_count, 1.0, 0.0), F32).astype(BF16)
            for block in values
        ]

        def score_block(q, slot, at, scores, most):
            s = jnp.dot(q, key_table[keys[slot], at, :], preferred_element_type=F32)
            scores[:, slot * block_len : (slot + 1) * block_len] = s
            for part in range(block_len // PAIR):
                some = s[:, part * PAIR : (part + 1) * PAIR]
                most = some if most is None else jnp.maximum(most, some)
            return most

        def value_block(slot, at, scores, most, total):
            p = jnp.concatenate(
                [
                    jnp.exp(scores[:, part : part + PAIR] - most).astype(BF16)
                    for part in range(slot * block_len, (slot + 1) * block_len, PAIR)
                ],
                axis=1,
            )
            both = jnp.concatenate([value_table[values[slot], :, at], ones[slot]], axis=1)
            term = jnp.dot(p, both, preferred_element_type=F32)
            return term if total is None else total + term

        def close(most, pair, top):
            most = jnp.broadcast_to(jnp.max(most, axis=1, keepdims=True), top.shape)
            if late:
                most = jnp.maximum(most, early_max[piece, pair])
            top[...] = most

        def columns(pair, width):
            return pl.ds(pl.multiple_of(pair * width, width), width)

        def load_query(pair):
            return queries[piece, :, columns(pair, PAIR)]

        def step(pair, scores, top, next_pair, next_scores, next_top):
            most, total, next_most = top[...], None, None
            q = load_query(next_pair)
            if late:
                scale = jnp.exp(early_max[piece, pair] - most)
                total = early_total[piece, pair] * jnp.concatenate([scale, scale], axis=1)
            for slot in range(len(keys)):
                next_most = score_block(q, slot, columns(next_pair, PAIR), next_scores, next_most)
                total = value_block(slot, columns(pair, PAIR), scores, most, total)
            close(next_most, next_pair, next_top)
            if early:
                early_total[piece, pair] = total
                early_max[piece, pair] = most
                return None
            each = total[:, :PAIR] / total[:, PAIR:]
            both = jnp.where(pair_lane, each[:piece_len], each[piece_len:])
            context[:, columns(pair, PAIR)] = both.astype(BF16)

        most, q = None, load_query(0)
        for slot in range(len(keys)):
            most = score_block(q, slot, columns(0, PAIR), scores_even, most)
        close(most, 0, max_even)

        def group(index, carry):
            for inner_pair in range(0, GROUP, 2):
                pair = index * GROUP + inner_pair
                after = jnp.minimum(pair + 2, pair_count - 1)
                step(pair, scores_even, max_even, pair + 1, scores_odd, max_odd)
                step(pair + 1, scores_odd, max_odd, after, scores_even, max_even)
            return carry

        lax.fori_loop(0, pair_count // GROUP, group, 0)

    def used(frame, slot):
        return slot < counts[0, frame]

    def named(frame, position):
        keys, values = [], []
        for key in range(key_count):
            there = jnp.int32(0)
            for slot in range(slot_count):
                same = (matches[0, frame, slot] == key * 3 + position) & used(frame, slot)
                there = there + jnp.where(same, 1, 0)
            block = position * key_count + key
            keys.append(jnp.where(there > 0, block, key_count))
            values.append(jnp.where(there > 0, block, 3 * key_count))
        return keys, values

    def partner(half, step, source=me):
        top = lax.rem(source // half_tiles, 2)
        other, bit = jnp.where(half == 0, 1 - top, top) * half_tiles, 1
        while bit < half_tiles:
            mine = lax.rem(source // bit, 2)
            moved = 1 - mine if step // bit % 2 else mine
            if 2 * bit == half_tiles:
                moved = jnp.where(half == 0, step // bit % 2, moved)
            other = other + moved * bit
            bit *= 2
        return other

    across = me + 2 - 4 * lax.rem(me // 2, 2)
    relayed = (me == 3) | (me == tiles - 4)
    relays = (me == 1) | (me == tiles - 2)

    def relay_slot(step):
        return step // 4 * 2 + step % 2

    def hand_over(frame, step, other):
        return pltpu.make_async_remote_copy(
            src_ref=stage.at[frame, other], dst_ref=relay.at[frame, relay_slot(step)],
            send_sem=send_sem.at[frame, other], recv_sem=relay_recv.at[frame, relay_slot(step)],
            device_id={"tile": across}, device_id_type=pl.DeviceIdType.MESH,
        )

    def pass_on(frame, step):
        return pltpu.make_async_remote_copy(
            src_ref=relay.at[frame, relay_slot(step)], dst_ref=out.at[frame, across],
            send_sem=relay_send.at[frame, relay_slot(step)], recv_sem=recv_sem.at[frame, across],
            device_id={"tile": partner(0, step, across)}, device_id_type=pl.DeviceIdType.MESH,
        )

    relay_steps = [step for step in range(half_tiles) if step // 2 % 2]

    def waits(step):
        return lax.rem(me // 2, 2) != step // 2 % 2

    def finish_piece(half, frame, hold=None):
        for chunk in range(chunk_count):
            at = slice(chunk * CHUNK, (chunk + 1) * CHUNK)
            update = jnp.dot(context[...], wo[:, at], preferred_element_type=F32)
            mixed = frames[half, frame, :, :, at].reshape(piece_len, CHUNK).astype(F32) + update
            if exchange:
                first = image_half(half) * half_tiles
                for other in range(half_tiles):
                    group = [
                        mixed[row * half_cols + other * cols : row * half_cols + (other + 1) * cols]
                        for row in range(rows)
                    ]
                    stage[frame, first + other, :, at] = jnp.concatenate(group, axis=0).astype(BF16)
            else:
                stage[frame, image_half(half), :, :, at] = mixed.reshape(rows, half_cols, CHUNK).astype(BF16)

        if exchange:
            order = sorted(range(half_tiles), key=lambda step: (2 * step // half_tiles, step // 2 % 2, -step))
            for step in order:
                other = partner(half, step)
                if hold is not None:
                    detour = relayed & (step in relay_steps) & (frame < relay_limit)

                    @pl.when(detour)
                    def _():
                        hand_over(frame, step, other).start()

                    @pl.when(jnp.logical_not(detour | (hold & waits(step))))
                    def _():
                        send(frame, other, me).start()

                    continue
                if step in relay_steps and relay_count:
                    detour = relayed & (half == 0) & (frame < relay_limit)

                    @pl.when(detour)
                    def _():
                        hand_over(frame, step, other).start()

                    @pl.when(jnp.logical_not(detour))
                    def _():
                        send(frame, other, me).start()

                    continue
                if step:
                    send(frame, other, me).start()
                    continue

                @pl.when(half == 0)
                def _():
                    send(frame, other, me).start()

                @pl.when(half != 0)
                def _():
                    keep(frame).start()
        else:
            place_half(frame, half).start()

    def one_piece(piece, carry):
        half = piece // frame_count
        frame = lax.rem(piece, frame_count)
        keys, values = [], []
        for slot in range(slot_count):
            chosen = jnp.where(used(frame, slot), matches[0, frame, slot], matches[0, frame, 0])
            block = lax.rem(chosen, 3) * key_count + lax.div(chosen, 3)
            keys.append(block)
            values.append(jnp.where(used(frame, slot), block, 3 * key_count))

        attend(piece, keys, values)
        finish_piece(half, frame)
        if relay_count:

            @pl.when(relays & (piece >= 1) & (piece <= relay_limit))
            def _():
                for step in relay_steps:
                    hand_over(piece - 1, step, me).wait_recv()
                    pass_on(piece - 1, step).start()

        return carry

    def early_piece(piece, carry):
        own_keys, own_values = named(piece, 1)
        near_keys, near_values = named(piece, partners[0][1])
        attend(piece, own_keys + near_keys, own_values + near_values, early=True)

        @pl.when((piece == 0) & held)
        def _():
            start_halo()

        return carry

    def late_piece(piece, carry):
        keys, values = named(piece, partners[1][1])
        attend(piece, keys[-1:], values[-1:], late=True)
        finish_piece(jnp.int32(0), piece, slow & (side == 1))
        return carry

    def middle_piece(key, piece, carry):
        keys, values = named(piece, partners[1][1])
        attend(piece, keys[key : key + 1], values[key : key + 1], early=True, late=True)
        return carry

    def held_sends(frame, carry):
        for step in range(half_tiles):

            @pl.when(waits(step))
            def _():
                send(frame, partner(0, step), me).start()

        return carry

    lax.fori_loop(0, early_count, early_piece, 0)
    if exchange:

        @pl.when(jnp.logical_not(leads))
        def _():
            pl.semaphore_wait(open_sem, 1)


    @pl.when(has_far)
    def _():
        for key in range(key_count):
            halo(key).wait_recv()
            project_stills(1, partners[1][1], key, 1)
            if key < key_count - 1:
                lax.fori_loop(0, early_count, functools.partial(middle_piece, key), 0)

    lax.fori_loop(0, early_count, late_piece, 0)
    if exchange:
        lax.fori_loop(0, jnp.where(slow & (side == 1), frame_count, 0), held_sends, 0)
    lax.fori_loop(early_count, 2 * frame_count, one_piece, 0)

    @pl.when(has_far)
    def _():
        for key in range(key_count):
            halo(key).wait_send()

    for key in range(key_count):
        for chunk in range(chunk_count):
            for copy in shared(key, chunk, partners[1][1]):
                copy.wait_send()

    if relay_count:

        @pl.when(relays)
        def _():
            for frame in range(relay_count):

                @pl.when(frame < relay_limit)
                def _():
                    for step in relay_steps:
                        pass_on(frame, step).wait_send()

    def finish(frame, carry):
        if exchange:

            def end(step, carry):
                other = lax.rem(me + step, tiles)
                send(frame, other, me).wait_send()
                send(frame, other, other).wait_recv()
                return carry

            lax.fori_loop(1, tiles, end, 0)
            keep(frame).wait()
        else:
            for half in range(2):
                place_half(frame, half).wait()
        return carry

    lax.fori_loop(0, frame_count, finish, 0)


def settle(src, out, held, in_sem, out_sem):
    frame_count, parts = in_sem.shape
    step = src.shape[1] // parts
    places = [(frame, pl.ds(part * step, step)) for frame in range(frame_count) for part in range(parts)]
    fetch = [
        pltpu.make_async_copy(src.at[at], held.at[at], in_sem.at[i // parts, i % parts])
        for i, at in enumerate(places)
    ]
    place = [
        pltpu.make_async_copy(held.at[at], out.at[at], out_sem.at[i // parts, i % parts])
        for i, at in enumerate(places)
    ]
    for copy in fetch:
        copy.start()
    for copy, back in zip(fetch, place):
        copy.wait()
        back.start()
    for back in place:
        back.wait()


def shards(tiles, frames, keyframes, matches, counts, w_query, w_key, w_value, w_out):
    frame_count, row_count, col_count, model_dim = frames.shape
    key_count = keyframes.shape[0]
    block_len = row_count * col_count
    half_cols = col_count // 2
    piece_len = row_count * half_cols
    slots = matches.shape[2]
    cols = col_count // tiles
    exchange = cols % 8 == 0 and tiles & (tiles - 1) == 0 and tiles >= 8
    if exchange:
        out_shape = (frame_count, tiles, row_count * cols, model_dim)
        stage_shape = out_shape
    else:
        out_shape = (frame_count, row_count, col_count, model_dim)
        stage_shape = (frame_count, 2, row_count, half_cols, model_dim)
    weight = pltpu.VMEM((model_dim, model_dim), BF16)
    products = (4 * frame_count + 12 * key_count) * block_len * model_dim * model_dim
    products += 4 * frame_count * slots * block_len * block_len * model_dim
    mixed = pl.pallas_call(
        functools.partial(kernel, tiles, exchange),
        out_shape=jax.ShapeDtypeStruct(out_shape, BF16),
        in_specs=[pl.BlockSpec(memory_space=pl.ANY)] * 8,
        out_specs=pl.BlockSpec(memory_space=pl.ANY),
        scratch_shapes=[
            pltpu.SMEM(matches.shape, jnp.int32),
            pltpu.SMEM(counts.shape, jnp.int32),
            pltpu.VMEM((2, frame_count, row_count, half_cols, model_dim), BF16),
            pltpu.VMEM((2, key_count * block_len, model_dim), BF16),
            weight, weight, weight, weight,
            pltpu.VMEM((2 * frame_count, 2 * piece_len, model_dim), BF16),
            pltpu.VMEM((3 * key_count, model_dim, block_len), BF16),
            pltpu.VMEM((3 * key_count + 1, block_len, model_dim), BF16),
            pltpu.VMEM((piece_len, model_dim), BF16),
            pltpu.VMEM(stage_shape, BF16),
            pltpu.VMEM((min(max(RELAYED), frame_count), 4) + stage_shape[2:], BF16),
            pltpu.VMEM((2 * piece_len, slots * block_len), F32),
            pltpu.VMEM((2 * piece_len, slots * block_len), F32),
            pltpu.VMEM((2 * piece_len, PAIR), F32),
            pltpu.VMEM((2 * piece_len, PAIR), F32),
            pltpu.VMEM((frame_count, HEADS // 2, 2 * piece_len, 2 * PAIR), F32),
            pltpu.VMEM((frame_count, HEADS // 2, 2 * piece_len, PAIR), F32),
            pltpu.SemaphoreType.REGULAR,
            pltpu.SemaphoreType.REGULAR,
            pltpu.SemaphoreType.REGULAR,
            pltpu.SemaphoreType.DMA((7,)),
            pltpu.SemaphoreType.DMA((2, model_dim // CHUNK)),
            pltpu.SemaphoreType.DMA((key_count,)),
            pltpu.SemaphoreType.DMA((key_count,)),
            pltpu.SemaphoreType.DMA((2, key_count, model_dim // CHUNK)),
            pltpu.SemaphoreType.DMA((2, key_count, model_dim // CHUNK)),
            pltpu.SemaphoreType.DMA((min(max(RELAYED), frame_count), 4)),
            pltpu.SemaphoreType.DMA((min(max(RELAYED), frame_count), 4)),
            pltpu.SemaphoreType.DMA((frame_count, tiles)),
            pltpu.SemaphoreType.DMA((frame_count, tiles)),
            pltpu.SemaphoreType.DMA((2, frame_count)),
        ],
        compiler_params=pltpu.CompilerParams(
            collective_id=0, has_side_effects=True, vmem_limit_bytes=60 * 1024 * 1024
        ),
        cost_estimate=pl.CostEstimate(
            flops=products, bytes_accessed=16 * 1024 * 1024,
            transcendentals=frame_count * slots * HEADS * block_len * block_len,
        ),
        name="attend_and_relay",
    )(
        matches, counts, frames,
        keyframes.reshape(key_count * block_len, model_dim),
        w_query, w_key, w_value, w_out,
    )
    if exchange:
        mixed = pl.pallas_call(
            settle,
            out_shape=jax.ShapeDtypeStruct(out_shape, BF16),
            in_specs=[pl.BlockSpec(memory_space=pl.ANY)],
            out_specs=pl.BlockSpec(memory_space=pl.ANY),
            scratch_shapes=[
                pltpu.VMEM(out_shape, BF16),
                pltpu.SemaphoreType.DMA((frame_count, 2)),
                pltpu.SemaphoreType.DMA((frame_count, 2)),
            ],
            name="settle",
        )(mixed)
        return mixed.reshape(frame_count, tiles * row_count, cols, model_dim)
    return lax.all_to_all(mixed, "tile", split_axis=2, concat_axis=1, tiled=True)


def solution(mesh):
    placed = (
        P("clip", "tile", None, None),
        P("clip", "tile", None, None),
        P("tile", "clip", None),
        P("tile", "clip"),
        P(),
        P(),
        P(),
        P(),
    )
    return jax.shard_map(
        functools.partial(shards, mesh.shape["tile"]),
        mesh=mesh, in_specs=placed, out_specs=P("clip", None, "tile", None), check_vma=False,
    )
```

```python
import functools

import jax
import jax.numpy as jnp
from jax import lax
from jax.experimental import pallas as pl
from jax.experimental.pallas import tpu as pltpu
from jax.sharding import PartitionSpec as P

HEADS = 16
PAIR = 128
CHUNK = 512
FAST_EARLY = 1
GATHER = 4
GROUP = 8
RELAYED = (2, 2)
F32 = jnp.float32
BF16 = jnp.bfloat16


def kernel(
    tiles, exchange,
    matches_in, counts_in, frames_in, keys_in, wq_in, wk_in, wv_in, wo_in,
    out,
    matches, counts, frames, stills, wq, wk, wv, wo, queries, key_table, value_table, context,
    stage, relay, scores_even, scores_odd, max_even, max_odd, early_total, early_max,
    gather_sem, lead_sem, open_sem, load_sem, weight_sem, halo_send, halo_recv, near_send, near_recv, relay_recv, relay_send, send_sem, recv_sem, own_sem,
):
    _, frame_count, rows, half_cols, model_dim = frames.shape
    piece_len = rows * half_cols
    block_len = 2 * piece_len
    key_count = stills.shape[1] // block_len
    slot_count = matches.shape[2]
    head_dim = model_dim // HEADS
    pair_count = model_dim // PAIR
    chunk_count = model_dim // CHUNK
    half_tiles = tiles // 2
    relay_count = relay.shape[0] if exchange and tiles == 16 else 0
    cols = half_cols // half_tiles
    me = lax.axis_index("tile")
    side = me // half_tiles
    relay_limit = jnp.where(side == 0, RELAYED[0], RELAYED[1])

    def image_half(half):
        return jnp.where(half == 0, 1 - side, side)

    def half_columns(half):
        return pl.ds(pl.multiple_of(image_half(half) * half_cols, half_cols), half_cols)

    loads = [
        pltpu.make_async_copy(src, dst, load_sem.at[i])
        for i, (src, dst) in enumerate(
            [
                (keys_in, stills.at[0]),
                (frames_in.at[:, :, half_columns(0)], frames.at[0]), (wq_in, wq),
                (frames_in.at[:, :, half_columns(1)], frames.at[1]), (wo_in, wo),
                (matches_in, matches), (counts_in, counts),
            ]
        )
    ]

    def weight_load(which, chunk):
        at = pl.ds(pl.multiple_of(chunk * CHUNK, CHUNK), CHUNK)
        src, dst = ((wk_in, wk), (wv_in, wv))[which]
        return pltpu.make_async_copy(src.at[:, at], dst.at[:, at], weight_sem.at[which, chunk])

    loads[0].start()
    for chunk in range(chunk_count):
        for which in range(2):
            weight_load(which, chunk).start()

    barrier = pltpu.get_barrier_semaphore()

    def signal(semaphore, other):
        pl.semaphore_signal(
            semaphore, inc=1, device_id={"tile": other}, device_id_type=pl.DeviceIdType.MESH
        )

    odd = lax.rem(me, 2)
    partners = ((me + 1 - 2 * odd, 2 - 2 * odd), (me - 1 + 2 * odd, 2 * odd))
    far = partners[1][0]
    has_far = (far >= 0) & (far < tiles)
    place = lax.rem(me, GATHER)
    inner = (place == 1) | (place == 2)
    slow = inner & (me != 1) & (me != tiles - 2)
    held = has_far & inner & (far != 1) & (far != tiles - 2)
    early_count = jnp.where(has_far, jnp.where(slow, frame_count, FAST_EARLY), 0)

    groups = tiles // GATHER
    leads = place == 0

    def greet(step, carry):
        signal(barrier, lax.rem(me + step * GATHER, tiles))
        return carry

    signal(barrier, partners[0][0])

    @pl.when(has_far)
    def _():
        signal(barrier, far)

    @pl.when(leads)
    def _():
        lax.fori_loop(1, groups, greet, 0)
        for step in range(2, GATHER):
            signal(barrier, me + step)

    value_table[3 * key_count] = jnp.zeros((block_len, model_dim), BF16)
    known = jnp.where(leads, groups - 1, jnp.where(place >= 2, 1, 0))
    pl.semaphore_wait(barrier, 1 + jnp.where(has_far, 1, 0) + known)

    def halo(key):
        part = pl.ds(key * block_len, block_len)
        return pltpu.make_async_remote_copy(
            src_ref=keys_in.at[part], dst_ref=stills.at[1, part],
            send_sem=halo_send.at[key], recv_sem=halo_recv.at[key],
            device_id={"tile": far}, device_id_type=pl.DeviceIdType.MESH,
        )

    def start_halo():
        for key in range(key_count):
            halo(key).start()

    def shared(key, chunk, position):
        block = position * key_count + key
        own = key_count + key
        narrow = pl.ds(pl.multiple_of(chunk * CHUNK, CHUNK), CHUNK)
        pieces = (
            (key_table.at[own, narrow], key_table.at[block, narrow]),
            (value_table.at[own, :, narrow], value_table.at[block, :, narrow]),
        )
        return [
            pltpu.make_async_remote_copy(
                src_ref=src, dst_ref=dst,
                send_sem=near_send.at[kind, key, chunk], recv_sem=near_recv.at[kind, key, chunk],
                device_id={"tile": partners[0][0]}, device_id_type=pl.DeviceIdType.MESH,
            )
            for kind, (src, dst) in enumerate(pieces)
        ]

    @pl.when(has_far & jnp.logical_not(held))
    def _():
        start_halo()

    if exchange:

        @pl.when(jnp.logical_not(leads))
        def _():
            signal(gather_sem, me - place)

    lane = lax.broadcasted_iota(jnp.int32, (piece_len, CHUNK), 1)
    even = lax.rem(lane, PAIR) < head_dim

    def project_queries(half):
        def step(chunk, carry):
            at = pl.ds(pl.multiple_of(chunk * CHUNK, CHUNK), CHUNK)
            tokens = frames[half].reshape(frame_count * piece_len, model_dim)
            q = jnp.dot(tokens, wq[:, at], preferred_element_type=F32)
            q = q * head_dim ** (-0.5)
            for frame in range(frame_count):
                part = q[frame * piece_len : (frame + 1) * piece_len]
                piece = half * frame_count + frame
                queries[piece, 0:piece_len, at] = jnp.where(even, part, 0.0).astype(BF16)
                queries[piece, piece_len : 2 * piece_len, at] = jnp.where(even, 0.0, part).astype(BF16)
            return carry

        lax.fori_loop(0, chunk_count, step, 0)

    def project_stills(source, slot, first, count, share=False):
        def step(chunk, carry):
            at = pl.ds(pl.multiple_of(chunk * CHUNK, CHUNK), CHUNK)
            if share:
                for which in range(2):
                    weight_load(which, chunk).wait()

                @pl.when(chunk == 0)
                def _():
                    for load in loads[1:]:
                        load.start()

            tokens = stills[source, first * block_len : (first + count) * block_len, :]
            k = jnp.dot(tokens, wk[:, at], preferred_element_type=F32).astype(BF16)
            v = jnp.dot(tokens, wv[:, at], preferred_element_type=F32).astype(BF16)
            for key in range(count):
                part = slice(key * block_len, (key + 1) * block_len)
                block = slot * key_count + first + key
                key_table[block, at, :] = k[part].T
                value_table[block, :, at] = v[part]
                if share:
                    for copy in shared(key, chunk, partners[1][1]):
                        copy.start()
            return carry

        lax.fori_loop(0, chunk_count, step, 0)

    loads[0].wait()
    project_stills(0, 1, 0, key_count, share=True)

    def tell(step, carry):
        signal(lead_sem, lax.rem(me + step * GATHER, tiles))
        return carry

    if exchange:

        @pl.when(leads)
        def _():
            pl.semaphore_wait(gather_sem, GATHER - 1)
            lax.fori_loop(1, groups, tell, 0)

    for load in loads[1:]:
        load.wait()

    def project_half(half, carry):
        project_queries(half)
        return carry

    def open_group():
        pl.semaphore_wait(lead_sem, groups - 1)
        for step in range(1, GATHER):
            signal(open_sem, me + step)

    lax.fori_loop(0, 1, project_half, 0)
    if exchange:

        @pl.when(leads & (side == 1))
        def _():
            open_group()

    lax.fori_loop(1, jnp.where(has_far, 2, 1), project_half, 0)
    if exchange:

        @pl.when(leads & (side == 0))
        def _():
            open_group()

    for key in range(key_count):
        for chunk in range(chunk_count):
            for copy in shared(key, chunk, partners[0][1]):
                copy.wait_recv()
    pair_lane = lax.broadcasted_iota(jnp.int32, (piece_len, PAIR), 1) < head_dim

    def send(frame, other, source):
        return pltpu.make_async_remote_copy(
            src_ref=stage.at[frame, other], dst_ref=out.at[frame, source],
            send_sem=send_sem.at[frame, other], recv_sem=recv_sem.at[frame, source],
            device_id={"tile": other}, device_id_type=pl.DeviceIdType.MESH,
        )

    def keep(frame):
        return pltpu.make_async_copy(stage.at[frame, me], out.at[frame, me], own_sem.at[0, frame])

    def place_half(frame, half):
        return pltpu.make_async_copy(
            stage.at[frame, image_half(half)], out.at[frame, :, half_columns(half)],
            own_sem.at[half, frame],
        )

    def attend(piece, keys, values, early=False, late=False):
        ones = [
            jnp.full((block_len, PAIR), jnp.where(block < 3 * key_count, 1.0, 0.0), F32).astype(BF16)
            for block in values
        ]

        def score_block(q, slot, at, scores, most):
            s = jnp.dot(q, key_table[keys[slot], at, :], preferred_element_type=F32)
            scores[:, slot * block_len : (slot + 1) * block_len] = s
            for part in range(block_len // PAIR):
                some = s[:, part * PAIR : (part + 1) * PAIR]
                most = some if most is None else jnp.maximum(most, some)
            return most

        def value_block(slot, at, scores, most, total):
            p = jnp.concatenate(
                [
                    jnp.exp(scores[:, part : part + PAIR] - most).astype(BF16)
                    for part in range(slot * block_len, (slot + 1) * block_len, PAIR)
                ],
                axis=1,
            )
            both = jnp.concatenate([value_table[values[slot], :, at], ones[slot]], axis=1)
            term = jnp.dot(p, both, preferred_element_type=F32)
            return term if total is None else total + term

        def close(most, pair, top):
            most = jnp.broadcast_to(jnp.max(most, axis=1, keepdims=True), top.shape)
            if late:
                most = jnp.maximum(most, early_max[piece, pair])
            top[...] = most

        def columns(pair, width):
            return pl.ds(pl.multiple_of(pair * width, width), width)

        def load_query(pair):
            return queries[piece, :, columns(pair, PAIR)]

        def step(pair, scores, top, next_pair, next_scores, next_top):
            most, total, next_most = top[...], None, None
            q = load_query(next_pair)
            if late:
                scale = jnp.exp(early_max[piece, pair] - most)
                total = early_total[piece, pair] * jnp.concatenate([scale, scale], axis=1)
            for slot in range(len(keys)):
                next_most = score_block(q, slot, columns(next_pair, PAIR), next_scores, next_most)
                total = value_block(slot, columns(pair, PAIR), scores, most, total)
            close(next_most, next_pair, next_top)
            if early:
                early_total[piece, pair] = total
                early_max[piece, pair] = most
                return None
            each = total[:, :PAIR] / total[:, PAIR:]
            both = jnp.where(pair_lane, each[:piece_len], each[piece_len:])
            context[:, columns(pair, PAIR)] = both.astype(BF16)

        most, q = None, load_query(0)
        for slot in range(len(keys)):
            most = score_block(q, slot, columns(0, PAIR), scores_even, most)
        close(most, 0, max_even)

        def group(index, carry):
            for inner_pair in range(0, GROUP, 2):
                pair = index * GROUP + inner_pair
                after = jnp.minimum(pair + 2, pair_count - 1)
                step(pair, scores_even, max_even, pair + 1, scores_odd, max_odd)
                step(pair + 1, scores_odd, max_odd, after, scores_even, max_even)
            return carry

        lax.fori_loop(0, pair_count // GROUP, group, 0)

    def used(frame, slot):
        return slot < counts[0, frame]

    def named(frame, position):
        keys, values = [], []
        for key in range(key_count):
            there = jnp.int32(0)
            for slot in range(slot_count):
                same = (matches[0, frame, slot] == key * 3 + position) & used(frame, slot)
                there = there + jnp.where(same, 1, 0)
            block = position * key_count + key
            keys.append(jnp.where(there > 0, block, key_count))
            values.append(jnp.where(there > 0, block, 3 * key_count))
        return keys, values

    def partner(half, step, source=me):
        top = lax.rem(source // half_tiles, 2)
        other, bit = jnp.where(half == 0, 1 - top, top) * half_tiles, 1
        while bit < half_tiles:
            mine = lax.rem(source // bit, 2)
            moved = 1 - mine if step // bit % 2 else mine
            if 2 * bit == half_tiles:
                moved = jnp.where(half == 0, step // bit % 2, moved)
            other = other + moved * bit
            bit *= 2
        return other

    across = me + 2 - 4 * lax.rem(me // 2, 2)
    relayed = (me == 3) | (me == tiles - 4)
    relays = (me == 1) | (me == tiles - 2)

    def relay_slot(step):
        return step // 4 * 2 + step % 2

    def hand_over(frame, step, other):
        return pltpu.make_async_remote_copy(
            src_ref=stage.at[frame, other], dst_ref=relay.at[frame, relay_slot(step)],
            send_sem=send_sem.at[frame, other], recv_sem=relay_recv.at[frame, relay_slot(step)],
            device_id={"tile": across}, device_id_type=pl.DeviceIdType.MESH,
        )

    def pass_on(frame, step):
        return pltpu.make_async_remote_copy(
            src_ref=relay.at[frame, relay_slot(step)], dst_ref=out.at[frame, across],
            send_sem=relay_send.at[frame, relay_slot(step)], recv_sem=recv_sem.at[frame, across],
            device_id={"tile": partner(0, step, across)}, device_id_type=pl.DeviceIdType.MESH,
        )

    relay_steps = [step for step in range(half_tiles) if step // 2 % 2]

    def waits(step):
        return lax.rem(me // 2, 2) != step // 2 % 2

    def finish_piece(half, frame, hold=None):
        for chunk in range(chunk_count):
            at = slice(chunk * CHUNK, (chunk + 1) * CHUNK)
            update = jnp.dot(context[...], wo[:, at], preferred_element_type=F32)
            mixed = frames[half, frame, :, :, at].reshape(piece_len, CHUNK).astype(F32) + update
            if exchange:
                first = image_half(half) * half_tiles
                for other in range(half_tiles):
                    group = [
                        mixed[row * half_cols + other * cols : row * half_cols + (other + 1) * cols]
                        for row in range(rows)
                    ]
                    stage[frame, first + other, :, at] = jnp.concatenate(group, axis=0).astype(BF16)
            else:
                stage[frame, image_half(half), :, :, at] = mixed.reshape(rows, half_cols, CHUNK).astype(BF16)

        if exchange:
            order = sorted(range(half_tiles), key=lambda step: (2 * step // half_tiles, step // 2 % 2, -step))
            for step in order:
                other = partner(half, step)
                if hold is not None:
                    detour = relayed & (step in relay_steps) & (frame < relay_limit)

                    @pl.when(detour)
                    def _():
                        hand_over(frame, step, other).start()

                    @pl.when(jnp.logical_not(detour | (hold & waits(step))))
                    def _():
                        send(frame, other, me).start()

                    continue
                if step in relay_steps and relay_count:
                    detour = relayed & (half == 0) & (frame < relay_limit)

                    @pl.when(detour)
                    def _():
                        hand_over(frame, step, other).start()

                    @pl.when(jnp.logical_not(detour))
                    def _():
                        send(frame, other, me).start()

                    continue
                if step:
                    send(frame, other, me).start()
                    continue

                @pl.when(half == 0)
                def _():
                    send(frame, other, me).start()

                @pl.when(half != 0)
                def _():
                    keep(frame).start()
        else:
            place_half(frame, half).start()

    def one_piece(piece, carry):
        half = piece // frame_count
        frame = lax.rem(piece, frame_count)
        keys, values = [], []
        for slot in range(slot_count):
            chosen = jnp.where(used(frame, slot), matches[0, frame, slot], matches[0, frame, 0])
            block = lax.rem(chosen, 3) * key_count + lax.div(chosen, 3)
            keys.append(block)
            values.append(jnp.where(used(frame, slot), block, 3 * key_count))

        @pl.when((piece == frame_count) & jnp.logical_not(has_far))
        def _():
            project_queries(1)

        attend(piece, keys, values)
        finish_piece(half, frame)
        if relay_count:

            @pl.when(relays & (piece >= 1) & (piece <= relay_limit))
            def _():
                for step in relay_steps:
                    hand_over(piece - 1, step, me).wait_recv()
                    pass_on(piece - 1, step).start()

        return carry

    def early_piece(piece, carry):
        own_keys, own_values = named(piece, 1)
        near_keys, near_values = named(piece, partners[0][1])
        attend(piece, own_keys + near_keys, own_values + near_values, early=True)

        @pl.when((piece == 0) & held)
        def _():
            start_halo()

        return carry

    def late_piece(piece, carry):
        keys, values = named(piece, partners[1][1])
        attend(piece, keys[-1:], values[-1:], late=True)
        finish_piece(jnp.int32(0), piece, slow & (side == 1))
        return carry

    def middle_piece(key, piece, carry):
        keys, values = named(piece, partners[1][1])
        attend(piece, keys[key : key + 1], values[key : key + 1], early=True, late=True)
        return carry

    def held_sends(frame, carry):
        for step in range(half_tiles):

            @pl.when(waits(step))
            def _():
                send(frame, partner(0, step), me).start()

        return carry

    lax.fori_loop(0, early_count, early_piece, 0)
    if exchange:

        @pl.when(jnp.logical_not(leads))
        def _():
            pl.semaphore_wait(open_sem, 1)


    @pl.when(has_far)
    def _():
        for key in range(key_count):
            halo(key).wait_recv()
            project_stills(1, partners[1][1], key, 1)
            if key < key_count - 1:
                lax.fori_loop(0, early_count, functools.partial(middle_piece, key), 0)

    lax.fori_loop(0, early_count, late_piece, 0)
    if exchange:
        lax.fori_loop(0, jnp.where(slow & (side == 1), frame_count, 0), held_sends, 0)
    lax.fori_loop(early_count, 2 * frame_count, one_piece, 0)

    @pl.when(has_far)
    def _():
        for key in range(key_count):
            halo(key).wait_send()

    for key in range(key_count):
        for chunk in range(chunk_count):
            for copy in shared(key, chunk, partners[1][1]):
                copy.wait_send()

    if relay_count:

        @pl.when(relays)
        def _():
            for frame in range(relay_count):

                @pl.when(frame < relay_limit)
                def _():
                    for step in relay_steps:
                        pass_on(frame, step).wait_send()

    def finish(frame, carry):
        if exchange:

            def end(step, carry):
                other = lax.rem(me + step, tiles)
                send(frame, other, me).wait_send()
                send(frame, other, other).wait_recv()
                return carry

            lax.fori_loop(1, tiles, end, 0)
            keep(frame).wait()
        else:
            for half in range(2):
                place_half(frame, half).wait()
        return carry

    lax.fori_loop(0, frame_count, finish, 0)


def settle(src, out, held, in_sem, out_sem):
    frame_count, parts = in_sem.shape
    step = src.shape[1] // parts
    places = [(frame, pl.ds(part * step, step)) for frame in range(frame_count) for part in range(parts)]
    fetch = [
        pltpu.make_async_copy(src.at[at], held.at[at], in_sem.at[i // parts, i % parts])
        for i, at in enumerate(places)
    ]
    place = [
        pltpu.make_async_copy(held.at[at], out.at[at], out_sem.at[i // parts, i % parts])
        for i, at in enumerate(places)
    ]
    for copy in fetch:
        copy.start()
    for copy, back in zip(fetch, place):
        copy.wait()
        back.start()
    for back in place:
        back.wait()


def shards(tiles, frames, keyframes, matches, counts, w_query, w_key, w_value, w_out):
    frame_count, row_count, col_count, model_dim = frames.shape
    key_count = keyframes.shape[0]
    block_len = row_count * col_count
    half_cols = col_count // 2
    piece_len = row_count * half_cols
    slots = matches.shape[2]
    cols = col_count // tiles
    exchange = cols % 8 == 0 and tiles & (tiles - 1) == 0 and tiles >= 8
    if exchange:
        out_shape = (frame_count, tiles, row_count * cols, model_dim)
        stage_shape = out_shape
    else:
        out_shape = (frame_count, row_count, col_count, model_dim)
        stage_shape = (frame_count, 2, row_count, half_cols, model_dim)
    weight = pltpu.VMEM((model_dim, model_dim), BF16)
    products = (4 * frame_count + 12 * key_count) * block_len * model_dim * model_dim
    products += 4 * frame_count * slots * block_len * block_len * model_dim
    mixed = pl.pallas_call(
        functools.partial(kernel, tiles, exchange),
        out_shape=jax.ShapeDtypeStruct(out_shape, BF16),
        in_specs=[pl.BlockSpec(memory_space=pl.ANY)] * 8,
        out_specs=pl.BlockSpec(memory_space=pl.ANY),
        scratch_shapes=[
            pltpu.SMEM(matches.shape, jnp.int32),
            pltpu.SMEM(counts.shape, jnp.int32),
            pltpu.VMEM((2, frame_count, row_count, half_cols, model_dim), BF16),
            pltpu.VMEM((2, key_count * block_len, model_dim), BF16),
            weight, weight, weight, weight,
            pltpu.VMEM((2 * frame_count, 2 * piece_len, model_dim), BF16),
            pltpu.VMEM((3 * key_count, model_dim, block_len), BF16),
            pltpu.VMEM((3 * key_count + 1, block_len, model_dim), BF16),
            pltpu.VMEM((piece_len, model_dim), BF16),
            pltpu.VMEM(stage_shape, BF16),
            pltpu.VMEM((min(max(RELAYED), frame_count), 4) + stage_shape[2:], BF16),
            pltpu.VMEM((2 * piece_len, slots * block_len), F32),
            pltpu.VMEM((2 * piece_len, slots * block_len), F32),
            pltpu.VMEM((2 * piece_len, PAIR), F32),
            pltpu.VMEM((2 * piece_len, PAIR), F32),
            pltpu.VMEM((frame_count, HEADS // 2, 2 * piece_len, 2 * PAIR), F32),
            pltpu.VMEM((frame_count, HEADS // 2, 2 * piece_len, PAIR), F32),
            pltpu.SemaphoreType.REGULAR,
            pltpu.SemaphoreType.REGULAR,
            pltpu.SemaphoreType.REGULAR,
            pltpu.SemaphoreType.DMA((7,)),
            pltpu.SemaphoreType.DMA((2, model_dim // CHUNK)),
            pltpu.SemaphoreType.DMA((key_count,)),
            pltpu.SemaphoreType.DMA((key_count,)),
            pltpu.SemaphoreType.DMA((2, key_count, model_dim // CHUNK)),
            pltpu.SemaphoreType.DMA((2, key_count, model_dim // CHUNK)),
            pltpu.SemaphoreType.DMA((min(max(RELAYED), frame_count), 4)),
            pltpu.SemaphoreType.DMA((min(max(RELAYED), frame_count), 4)),
            pltpu.SemaphoreType.DMA((frame_count, tiles)),
            pltpu.SemaphoreType.DMA((frame_count, tiles)),
            pltpu.SemaphoreType.DMA((2, frame_count)),
        ],
        compiler_params=pltpu.CompilerParams(
            collective_id=0, has_side_effects=True, vmem_limit_bytes=60 * 1024 * 1024
        ),
        cost_estimate=pl.CostEstimate(
            flops=products, bytes_accessed=16 * 1024 * 1024,
            transcendentals=frame_count * slots * HEADS * block_len * block_len,
        ),
        name="attend_and_relay",
    )(
        matches, counts, frames,
        keyframes.reshape(key_count * block_len, model_dim),
        w_query, w_key, w_value, w_out,
    )
    if exchange:
        mixed = pl.pallas_call(
            settle,
            out_shape=jax.ShapeDtypeStruct(out_shape, BF16),
            in_specs=[pl.BlockSpec(memory_space=pl.ANY)],
            out_specs=pl.BlockSpec(memory_space=pl.ANY),
            scratch_shapes=[
                pltpu.VMEM(out_shape, BF16),
                pltpu.SemaphoreType.DMA((frame_count, 2)),
                pltpu.SemaphoreType.DMA((frame_count, 2)),
            ],
            name="settle",
        )(mixed)
        return mixed.reshape(frame_count, tiles * row_count, cols, model_dim)
    return lax.all_to_all(mixed, "tile", split_axis=2, concat_axis=1, tiled=True)


def solution(mesh):
    placed = (
        P("clip", "tile", None, None),
        P("clip", "tile", None, None),
        P("tile", "clip", None),
        P("tile", "clip"),
        P(),
        P(),
        P(),
        P(),
    )
    return jax.shard_map(
        functools.partial(shards, mesh.shape["tile"]),
        mesh=mesh, in_specs=placed, out_specs=P("clip", None, "tile", None), check_vma=False,
    )
```

```python
import functools

import jax
import jax.numpy as jnp
from jax import lax
from jax.experimental import pallas as pl
from jax.experimental.pallas import tpu as pltpu
from jax.sharding import PartitionSpec as P

HEADS = 16
PAIR = 128
CHUNK = 512
FAST_EARLY = 1
GATHER = 4
HOLD_FROM = 1
GROUP = 8
RELAYED = (2, 2)
F32 = jnp.float32
BF16 = jnp.bfloat16


def kernel(
    tiles, exchange,
    matches_in, counts_in, frames_in, keys_in, wq_in, wk_in, wv_in, wo_in,
    out,
    matches, counts, frames, stills, wq, wk, wv, wo, queries, key_table, value_table, context,
    stage, relay, scores_even, scores_odd, max_even, max_odd, early_total, early_max,
    gather_sem, lead_sem, open_sem, load_sem, weight_sem, halo_send, halo_recv, near_send, near_recv, relay_recv, relay_send, send_sem, recv_sem, own_sem,
):
    _, frame_count, rows, half_cols, model_dim = frames.shape
    piece_len = rows * half_cols
    block_len = 2 * piece_len
    key_count = stills.shape[1] // block_len
    slot_count = matches.shape[2]
    head_dim = model_dim // HEADS
    pair_count = model_dim // PAIR
    chunk_count = model_dim // CHUNK
    half_tiles = tiles // 2
    relay_count = relay.shape[0] if exchange and tiles == 16 else 0
    cols = half_cols // half_tiles
    me = lax.axis_index("tile")
    side = me // half_tiles
    relay_limit = jnp.where(side == 0, RELAYED[0], RELAYED[1])

    def image_half(half):
        return jnp.where(half == 0, 1 - side, side)

    def half_columns(half):
        return pl.ds(pl.multiple_of(image_half(half) * half_cols, half_cols), half_cols)

    loads = [
        pltpu.make_async_copy(src, dst, load_sem.at[i])
        for i, (src, dst) in enumerate(
            [
                (keys_in, stills.at[0]),
                (frames_in.at[:, :, half_columns(0)], frames.at[0]), (wq_in, wq),
                (frames_in.at[:, :, half_columns(1)], frames.at[1]), (wo_in, wo),
                (matches_in, matches), (counts_in, counts),
            ]
        )
    ]

    def weight_load(which, chunk):
        at = pl.ds(pl.multiple_of(chunk * CHUNK, CHUNK), CHUNK)
        src, dst = ((wk_in, wk), (wv_in, wv))[which]
        return pltpu.make_async_copy(src.at[:, at], dst.at[:, at], weight_sem.at[which, chunk])

    loads[0].start()
    for chunk in range(chunk_count):
        for which in range(2):
            weight_load(which, chunk).start()

    barrier = pltpu.get_barrier_semaphore()

    def signal(semaphore, other):
        pl.semaphore_signal(
            semaphore, inc=1, device_id={"tile": other}, device_id_type=pl.DeviceIdType.MESH
        )

    odd = lax.rem(me, 2)
    partners = ((me + 1 - 2 * odd, 2 - 2 * odd), (me - 1 + 2 * odd, 2 * odd))
    far = partners[1][0]
    has_far = (far >= 0) & (far < tiles)
    place = lax.rem(me, GATHER)
    inner = (place == 1) | (place == 2)
    slow = inner & (me != 1) & (me != tiles - 2)
    held = has_far & inner & (far != 1) & (far != tiles - 2)
    early_count = jnp.where(has_far, jnp.where(slow, frame_count, FAST_EARLY), 0)

    groups = tiles // GATHER
    leads = place == 0

    def greet(step, carry):
        signal(barrier, lax.rem(me + step * GATHER, tiles))
        return carry

    signal(barrier, partners[0][0])

    @pl.when(has_far)
    def _():
        signal(barrier, far)

    @pl.when(leads)
    def _():
        lax.fori_loop(1, groups, greet, 0)
        for step in range(2, GATHER):
            signal(barrier, me + step)

    value_table[3 * key_count] = jnp.zeros((block_len, model_dim), BF16)
    known = jnp.where(leads, groups - 1, jnp.where(place >= 2, 1, 0))
    pl.semaphore_wait(barrier, 1 + jnp.where(has_far, 1, 0) + known)

    def halo(key):
        part = pl.ds(key * block_len, block_len)
        return pltpu.make_async_remote_copy(
            src_ref=keys_in.at[part], dst_ref=stills.at[1, part],
            send_sem=halo_send.at[key], recv_sem=halo_recv.at[key],
            device_id={"tile": far}, device_id_type=pl.DeviceIdType.MESH,
        )

    def start_halo():
        for key in range(key_count):
            halo(key).start()

    def shared(key, chunk, position):
        block = position * key_count + key
        own = key_count + key
        narrow = pl.ds(pl.multiple_of(chunk * CHUNK, CHUNK), CHUNK)
        pieces = (
            (key_table.at[own, narrow], key_table.at[block, narrow]),
            (value_table.at[own, :, narrow], value_table.at[block, :, narrow]),
        )
        return [
            pltpu.make_async_remote_copy(
                src_ref=src, dst_ref=dst,
                send_sem=near_send.at[kind, key, chunk], recv_sem=near_recv.at[kind, key, chunk],
                device_id={"tile": partners[0][0]}, device_id_type=pl.DeviceIdType.MESH,
            )
            for kind, (src, dst) in enumerate(pieces)
        ]

    @pl.when(has_far & jnp.logical_not(held))
    def _():
        start_halo()

    if exchange:

        @pl.when(jnp.logical_not(leads))
        def _():
            signal(gather_sem, me - place)

    lane = lax.broadcasted_iota(jnp.int32, (piece_len, CHUNK), 1)
    even = lax.rem(lane, PAIR) < head_dim

    def project_queries(half):
        def step(chunk, carry):
            at = pl.ds(pl.multiple_of(chunk * CHUNK, CHUNK), CHUNK)
            tokens = frames[half].reshape(frame_count * piece_len, model_dim)
            q = jnp.dot(tokens, wq[:, at], preferred_element_type=F32)
            q = q * head_dim ** (-0.5)
            for frame in range(frame_count):
                part = q[frame * piece_len : (frame + 1) * piece_len]
                piece = half * frame_count + frame
                queries[piece, 0:piece_len, at] = jnp.where(even, part, 0.0).astype(BF16)
                queries[piece, piece_len : 2 * piece_len, at] = jnp.where(even, 0.0, part).astype(BF16)
            return carry

        lax.fori_loop(0, chunk_count, step, 0)

    def project_stills(source, slot, first, count, share=False):
        def step(chunk, carry):
            at = pl.ds(pl.multiple_of(chunk * CHUNK, CHUNK), CHUNK)
            if share:
                for which in range(2):
                    weight_load(which, chunk).wait()

                @pl.when(chunk == 0)
                def _():
                    for load in loads[1:]:
                        load.start()

            tokens = stills[source, first * block_len : (first + count) * block_len, :]
            k = jnp.dot(tokens, wk[:, at], preferred_element_type=F32).astype(BF16)
            v = jnp.dot(tokens, wv[:, at], preferred_element_type=F32).astype(BF16)
            for key in range(count):
                part = slice(key * block_len, (key + 1) * block_len)
                block = slot * key_count + first + key
                key_table[block, at, :] = k[part].T
                value_table[block, :, at] = v[part]
                if share:
                    for copy in shared(key, chunk, partners[1][1]):
                        copy.start()
            return carry

        lax.fori_loop(0, chunk_count, step, 0)

    loads[0].wait()
    project_stills(0, 1, 0, key_count, share=True)

    def tell(step, carry):
        signal(lead_sem, lax.rem(me + step * GATHER, tiles))
        return carry

    if exchange:

        @pl.when(leads)
        def _():
            pl.semaphore_wait(gather_sem, GATHER - 1)
            lax.fori_loop(1, groups, tell, 0)

    for load in loads[1:]:
        load.wait()

    def project_half(half, carry):
        project_queries(half)
        return carry

    def open_group():
        pl.semaphore_wait(lead_sem, groups - 1)
        for step in range(1, GATHER):
            signal(open_sem, me + step)

    lax.fori_loop(0, 1, project_half, 0)
    if exchange:

        @pl.when(leads & (side == 1))
        def _():
            open_group()

    lax.fori_loop(1, jnp.where(has_far, 2, 1), project_half, 0)
    if exchange:

        @pl.when(leads & (side == 0))
        def _():
            open_group()

    for key in range(key_count):
        for chunk in range(chunk_count):
            for copy in shared(key, chunk, partners[0][1]):
                copy.wait_recv()
    pair_lane = lax.broadcasted_iota(jnp.int32, (piece_len, PAIR), 1) < head_dim

    def send(frame, other, source):
        return pltpu.make_async_remote_copy(
            src_ref=stage.at[frame, other], dst_ref=out.at[frame, source],
            send_sem=send_sem.at[frame, other], recv_sem=recv_sem.at[frame, source],
            device_id={"tile": other}, device_id_type=pl.DeviceIdType.MESH,
        )

    def keep(frame):
        return pltpu.make_async_copy(stage.at[frame, me], out.at[frame, me], own_sem.at[0, frame])

    def place_half(frame, half):
        return pltpu.make_async_copy(
            stage.at[frame, image_half(half)], out.at[frame, :, half_columns(half)],
            own_sem.at[half, frame],
        )

    def attend(piece, keys, values, early=False, late=False):
        ones = [
            jnp.full((block_len, PAIR), jnp.where(block < 3 * key_count, 1.0, 0.0), F32).astype(BF16)
            for block in values
        ]

        def score_block(q, slot, at, scores, most):
            s = jnp.dot(q, key_table[keys[slot], at, :], preferred_element_type=F32)
            scores[:, slot * block_len : (slot + 1) * block_len] = s
            for part in range(block_len // PAIR):
                some = s[:, part * PAIR : (part + 1) * PAIR]
                most = some if most is None else jnp.maximum(most, some)
            return most

        def value_block(slot, at, scores, most, total):
            p = jnp.concatenate(
                [
                    jnp.exp(scores[:, part : part + PAIR] - most).astype(BF16)
                    for part in range(slot * block_len, (slot + 1) * block_len, PAIR)
                ],
                axis=1,
            )
            both = jnp.concatenate([value_table[values[slot], :, at], ones[slot]], axis=1)
            term = jnp.dot(p, both, preferred_element_type=F32)
            return term if total is None else total + term

        def close(most, pair, top):
            most = jnp.broadcast_to(jnp.max(most, axis=1, keepdims=True), top.shape)
            if late:
                most = jnp.maximum(most, early_max[piece, pair])
            top[...] = most

        def columns(pair, width):
            return pl.ds(pl.multiple_of(pair * width, width), width)

        def load_query(pair):
            return queries[piece, :, columns(pair, PAIR)]

        def step(pair, scores, top, next_pair, next_scores, next_top):
            most, total, next_most = top[...], None, None
            q = load_query(next_pair)
            if late:
                scale = jnp.exp(early_max[piece, pair] - most)
                total = early_total[piece, pair] * jnp.concatenate([scale, scale], axis=1)
            for slot in range(len(keys)):
                next_most = score_block(q, slot, columns(next_pair, PAIR), next_scores, next_most)
                total = value_block(slot, columns(pair, PAIR), scores, most, total)
            close(next_most, next_pair, next_top)
            if early:
                early_total[piece, pair] = total
                early_max[piece, pair] = most
                return None
            each = total[:, :PAIR] / total[:, PAIR:]
            both = jnp.where(pair_lane, each[:piece_len], each[piece_len:])
            context[:, columns(pair, PAIR)] = both.astype(BF16)

        most, q = None, load_query(0)
        for slot in range(len(keys)):
            most = score_block(q, slot, columns(0, PAIR), scores_even, most)
        close(most, 0, max_even)

        def group(index, carry):
            for inner_pair in range(0, GROUP, 2):
                pair = index * GROUP + inner_pair
                after = jnp.minimum(pair + 2, pair_count - 1)
                step(pair, scores_even, max_even, pair + 1, scores_odd, max_odd)
                step(pair + 1, scores_odd, max_odd, after, scores_even, max_even)
            return carry

        lax.fori_loop(0, pair_count // GROUP, group, 0)

    def used(frame, slot):
        return slot < counts[0, frame]

    def named(frame, position):
        keys, values = [], []
        for key in range(key_count):
            there = jnp.int32(0)
            for slot in range(slot_count):
                same = (matches[0, frame, slot] == key * 3 + position) & used(frame, slot)
                there = there + jnp.where(same, 1, 0)
            block = position * key_count + key
            keys.append(jnp.where(there > 0, block, key_count))
            values.append(jnp.where(there > 0, block, 3 * key_count))
        return keys, values

    def partner(half, step, source=me):
        top = lax.rem(source // half_tiles, 2)
        other, bit = jnp.where(half == 0, 1 - top, top) * half_tiles, 1
        while bit < half_tiles:
            mine = lax.rem(source // bit, 2)
            moved = 1 - mine if step // bit % 2 else mine
            if 2 * bit == half_tiles:
                moved = jnp.where(half == 0, step // bit % 2, moved)
            other = other + moved * bit
            bit *= 2
        return other

    across = me + 2 - 4 * lax.rem(me // 2, 2)
    relayed = (me == 3) | (me == tiles - 4)
    relays = (me == 1) | (me == tiles - 2)

    def relay_slot(step):
        return step // 4 * 2 + step % 2

    def hand_over(frame, step, other):
        return pltpu.make_async_remote_copy(
            src_ref=stage.at[frame, other], dst_ref=relay.at[frame, relay_slot(step)],
            send_sem=send_sem.at[frame, other], recv_sem=relay_recv.at[frame, relay_slot(step)],
            device_id={"tile": across}, device_id_type=pl.DeviceIdType.MESH,
        )

    def pass_on(frame, step):
        return pltpu.make_async_remote_copy(
            src_ref=relay.at[frame, relay_slot(step)], dst_ref=out.at[frame, across],
            send_sem=relay_send.at[frame, relay_slot(step)], recv_sem=recv_sem.at[frame, across],
            device_id={"tile": partner(0, step, across)}, device_id_type=pl.DeviceIdType.MESH,
        )

    relay_steps = [step for step in range(half_tiles) if step // 2 % 2]

    def waits(step):
        return lax.rem(me // 2, 2) != step // 2 % 2

    def finish_piece(half, frame, hold=None):
        for chunk in range(chunk_count):
            at = slice(chunk * CHUNK, (chunk + 1) * CHUNK)
            update = jnp.dot(context[...], wo[:, at], preferred_element_type=F32)
            mixed = frames[half, frame, :, :, at].reshape(piece_len, CHUNK).astype(F32) + update
            if exchange:
                first = image_half(half) * half_tiles
                for other in range(half_tiles):
                    group = [
                        mixed[row * half_cols + other * cols : row * half_cols + (other + 1) * cols]
                        for row in range(rows)
                    ]
                    stage[frame, first + other, :, at] = jnp.concatenate(group, axis=0).astype(BF16)
            else:
                stage[frame, image_half(half), :, :, at] = mixed.reshape(rows, half_cols, CHUNK).astype(BF16)

        if exchange:
            order = sorted(range(half_tiles), key=lambda step: (2 * step // half_tiles, step // 2 % 2, -step))
            for step in order:
                other = partner(half, step)
                if hold is not None:
                    detour = relayed & (step in relay_steps) & (frame < relay_limit)

                    @pl.when(detour)
                    def _():
                        hand_over(frame, step, other).start()

                    @pl.when(jnp.logical_not(detour | (hold & waits(step) & (frame >= HOLD_FROM))))
                    def _():
                        send(frame, other, me).start()

                    continue
                if step in relay_steps and relay_count:
                    detour = relayed & (half == 0) & (frame < relay_limit)

                    @pl.when(detour)
                    def _():
                        hand_over(frame, step, other).start()

                    @pl.when(jnp.logical_not(detour))
                    def _():
                        send(frame, other, me).start()

                    continue
                if step:
                    send(frame, other, me).start()
                    continue

                @pl.when(half == 0)
                def _():
                    send(frame, other, me).start()

                @pl.when(half != 0)
                def _():
                    keep(frame).start()
        else:
            place_half(frame, half).start()

    def one_piece(piece, carry):
        half = piece // frame_count
        frame = lax.rem(piece, frame_count)
        keys, values = [], []
        for slot in range(slot_count):
            chosen = jnp.where(used(frame, slot), matches[0, frame, slot], matches[0, frame, 0])
            block = lax.rem(chosen, 3) * key_count + lax.div(chosen, 3)
            keys.append(block)
            values.append(jnp.where(used(frame, slot), block, 3 * key_count))

        @pl.when((piece == frame_count) & jnp.logical_not(has_far))
        def _():
            project_queries(1)

        attend(piece, keys, values)
        finish_piece(half, frame)
        if relay_count:

            @pl.when(relays & (piece >= 1) & (piece <= relay_limit))
            def _():
                for step in relay_steps:
                    hand_over(piece - 1, step, me).wait_recv()
                    pass_on(piece - 1, step).start()

        return carry

    def early_piece(piece, carry):
        own_keys, own_values = named(piece, 1)
        near_keys, near_values = named(piece, partners[0][1])
        attend(piece, own_keys + near_keys, own_values + near_values, early=True)

        @pl.when((piece == 0) & held)
        def _():
            start_halo()

        return carry

    def late_piece(piece, carry):
        keys, values = named(piece, partners[1][1])
        attend(piece, keys[-1:], values[-1:], late=True)
        finish_piece(jnp.int32(0), piece, slow & (side == 1))
        return carry

    def middle_piece(key, piece, carry):
        keys, values = named(piece, partners[1][1])
        attend(piece, keys[key : key + 1], values[key : key + 1], early=True, late=True)
        return carry

    def held_sends(frame, carry):
        for step in range(half_tiles):

            @pl.when(waits(step))
            def _():
                send(frame, partner(0, step), me).start()

        return carry

    lax.fori_loop(0, early_count, early_piece, 0)
    if exchange:

        @pl.when(jnp.logical_not(leads))
        def _():
            pl.semaphore_wait(open_sem, 1)


    @pl.when(has_far)
    def _():
        for key in range(key_count):
            halo(key).wait_recv()
            project_stills(1, partners[1][1], key, 1)
            if key < key_count - 1:
                lax.fori_loop(0, early_count, functools.partial(middle_piece, key), 0)

    lax.fori_loop(0, early_count, late_piece, 0)
    if exchange:
        lax.fori_loop(HOLD_FROM, jnp.where(slow & (side == 1), frame_count, HOLD_FROM), held_sends, 0)
    lax.fori_loop(early_count, 2 * frame_count, one_piece, 0)

    @pl.when(has_far)
    def _():
        for key in range(key_count):
            halo(key).wait_send()

    for key in range(key_count):
        for chunk in range(chunk_count):
            for copy in shared(key, chunk, partners[1][1]):
                copy.wait_send()

    if relay_count:

        @pl.when(relays)
        def _():
            for frame in range(relay_count):

                @pl.when(frame < relay_limit)
                def _():
                    for step in relay_steps:
                        pass_on(frame, step).wait_send()

    def finish(frame, carry):
        if exchange:

            def end(step, carry):
                other = lax.rem(me + step, tiles)
                send(frame, other, me).wait_send()
                send(frame, other, other).wait_recv()
                return carry

            lax.fori_loop(1, tiles, end, 0)
            keep(frame).wait()
        else:
            for half in range(2):
                place_half(frame, half).wait()
        return carry

    lax.fori_loop(0, frame_count, finish, 0)


def settle(src, out, held, in_sem, out_sem):
    frame_count, parts = in_sem.shape
    step = src.shape[1] // parts
    places = [(frame, pl.ds(part * step, step)) for frame in range(frame_count) for part in range(parts)]
    fetch = [
        pltpu.make_async_copy(src.at[at], held.at[at], in_sem.at[i // parts, i % parts])
        for i, at in enumerate(places)
    ]
    place = [
        pltpu.make_async_copy(held.at[at], out.at[at], out_sem.at[i // parts, i % parts])
        for i, at in enumerate(places)
    ]
    for copy in fetch:
        copy.start()
    for copy, back in zip(fetch, place):
        copy.wait()
        back.start()
    for back in place:
        back.wait()


def shards(tiles, frames, keyframes, matches, counts, w_query, w_key, w_value, w_out):
    frame_count, row_count, col_count, model_dim = frames.shape
    key_count = keyframes.shape[0]
    block_len = row_count * col_count
    half_cols = col_count // 2
    piece_len = row_count * half_cols
    slots = matches.shape[2]
    cols = col_count // tiles
    exchange = cols % 8 == 0 and tiles & (tiles - 1) == 0 and tiles >= 8
    if exchange:
        out_shape = (frame_count, tiles, row_count * cols, model_dim)
        stage_shape = out_shape
    else:
        out_shape = (frame_count, row_count, col_count, model_dim)
        stage_shape = (frame_count, 2, row_count, half_cols, model_dim)
    weight = pltpu.VMEM((model_dim, model_dim), BF16)
    products = (4 * frame_count + 12 * key_count) * block_len * model_dim * model_dim
    products += 4 * frame_count * slots * block_len * block_len * model_dim
    mixed = pl.pallas_call(
        functools.partial(kernel, tiles, exchange),
        out_shape=jax.ShapeDtypeStruct(out_shape, BF16),
        in_specs=[pl.BlockSpec(memory_space=pl.ANY)] * 8,
        out_specs=pl.BlockSpec(memory_space=pl.ANY),
        scratch_shapes=[
            pltpu.SMEM(matches.shape, jnp.int32),
            pltpu.SMEM(counts.shape, jnp.int32),
            pltpu.VMEM((2, frame_count, row_count, half_cols, model_dim), BF16),
            pltpu.VMEM((2, key_count * block_len, model_dim), BF16),
            weight, weight, weight, weight,
            pltpu.VMEM((2 * frame_count, 2 * piece_len, model_dim), BF16),
            pltpu.VMEM((3 * key_count, model_dim, block_len), BF16),
            pltpu.VMEM((3 * key_count + 1, block_len, model_dim), BF16),
            pltpu.VMEM((piece_len, model_dim), BF16),
            pltpu.VMEM(stage_shape, BF16),
            pltpu.VMEM((min(max(RELAYED), frame_count), 4) + stage_shape[2:], BF16),
            pltpu.VMEM((2 * piece_len, slots * block_len), F32),
            pltpu.VMEM((2 * piece_len, slots * block_len), F32),
            pltpu.VMEM((2 * piece_len, PAIR), F32),
            pltpu.VMEM((2 * piece_len, PAIR), F32),
            pltpu.VMEM((frame_count, HEADS // 2, 2 * piece_len, 2 * PAIR), F32),
            pltpu.VMEM((frame_count, HEADS // 2, 2 * piece_len, PAIR), F32),
            pltpu.SemaphoreType.REGULAR,
            pltpu.SemaphoreType.REGULAR,
            pltpu.SemaphoreType.REGULAR,
            pltpu.SemaphoreType.DMA((7,)),
            pltpu.SemaphoreType.DMA((2, model_dim // CHUNK)),
            pltpu.SemaphoreType.DMA((key_count,)),
            pltpu.SemaphoreType.DMA((key_count,)),
            pltpu.SemaphoreType.DMA((2, key_count, model_dim // CHUNK)),
            pltpu.SemaphoreType.DMA((2, key_count, model_dim // CHUNK)),
            pltpu.SemaphoreType.DMA((min(max(RELAYED), frame_count), 4)),
            pltpu.SemaphoreType.DMA((min(max(RELAYED), frame_count), 4)),
            pltpu.SemaphoreType.DMA((frame_count, tiles)),
            pltpu.SemaphoreType.DMA((frame_count, tiles)),
            pltpu.SemaphoreType.DMA((2, frame_count)),
        ],
        compiler_params=pltpu.CompilerParams(
            collective_id=0, has_side_effects=True, vmem_limit_bytes=60 * 1024 * 1024
        ),
        cost_estimate=pl.CostEstimate(
            flops=products, bytes_accessed=16 * 1024 * 1024,
            transcendentals=frame_count * slots * HEADS * block_len * block_len,
        ),
        name="attend_and_relay",
    )(
        matches, counts, frames,
        keyframes.reshape(key_count * block_len, model_dim),
        w_query, w_key, w_value, w_out,
    )
    if exchange:
        mixed = pl.pallas_call(
            settle,
            out_shape=jax.ShapeDtypeStruct(out_shape, BF16),
            in_specs=[pl.BlockSpec(memory_space=pl.ANY)],
            out_specs=pl.BlockSpec(memory_space=pl.ANY),
            scratch_shapes=[
                pltpu.VMEM(out_shape, BF16),
                pltpu.SemaphoreType.DMA((frame_count, 2)),
                pltpu.SemaphoreType.DMA((frame_count, 2)),
            ],
            name="settle",
        )(mixed)
        return mixed.reshape(frame_count, tiles * row_count, cols, model_dim)
    return lax.all_to_all(mixed, "tile", split_axis=2, concat_axis=1, tiled=True)


def solution(mesh):
    placed = (
        P("clip", "tile", None, None),
        P("clip", "tile", None, None),
        P("tile", "clip", None),
        P("tile", "clip"),
        P(),
        P(),
        P(),
        P(),
    )
    return jax.shard_map(
        functools.partial(shards, mesh.shape["tile"]),
        mesh=mesh, in_specs=placed, out_specs=P("clip", None, "tile", None), check_vma=False,
    )
```

```python
import functools

import jax
import jax.numpy as jnp
from jax import lax
from jax.experimental import pallas as pl
from jax.experimental.pallas import tpu as pltpu
from jax.sharding import PartitionSpec as P

HEADS = 16
PAIR = 128
CHUNK = 512
FAST_EARLY = 1
GATHER = 4
HOLD_FROM = 1
GROUP = 8
RELAYED = (2, 2)
F32 = jnp.float32
BF16 = jnp.bfloat16


def kernel(
    tiles, exchange,
    matches_in, counts_in, frames_in, keys_in, wq_in, wk_in, wv_in, wo_in,
    out,
    matches, counts, frames, stills, wq, wk, wv, wo, queries, key_table, value_table, context,
    stage, relay, scores_even, scores_odd, max_even, max_odd, early_total, early_max,
    gather_sem, lead_sem, open_sem, load_sem, weight_sem, halo_send, halo_recv, near_send, near_recv, relay_recv, relay_send, send_sem, recv_sem, own_sem,
):
    _, frame_count, rows, half_cols, model_dim = frames.shape
    piece_len = rows * half_cols
    block_len = 2 * piece_len
    key_count = stills.shape[1] // block_len
    slot_count = matches.shape[2]
    head_dim = model_dim // HEADS
    pair_count = model_dim // PAIR
    chunk_count = model_dim // CHUNK
    half_tiles = tiles // 2
    relay_count = relay.shape[0] if exchange and tiles == 16 else 0
    cols = half_cols // half_tiles
    me = lax.axis_index("tile")
    side = me // half_tiles
    relay_limit = jnp.where(side == 0, RELAYED[0], RELAYED[1])

    def image_half(half):
        return jnp.where(half == 0, 1 - side, side)

    def half_columns(half):
        return pl.ds(pl.multiple_of(image_half(half) * half_cols, half_cols), half_cols)

    loads = [
        pltpu.make_async_copy(src, dst, load_sem.at[i])
        for i, (src, dst) in enumerate(
            [
                (keys_in, stills.at[0]),
                (frames_in.at[:, :, half_columns(0)], frames.at[0]), (wq_in, wq),
                (frames_in.at[:, :, half_columns(1)], frames.at[1]), (wo_in, wo),
                (matches_in, matches), (counts_in, counts),
            ]
        )
    ]

    def weight_load(which, chunk):
        at = pl.ds(pl.multiple_of(chunk * CHUNK, CHUNK), CHUNK)
        src, dst = ((wk_in, wk), (wv_in, wv))[which]
        return pltpu.make_async_copy(src.at[:, at], dst.at[:, at], weight_sem.at[which, chunk])

    loads[0].start()
    for chunk in range(chunk_count):
        for which in range(2):
            weight_load(which, chunk).start()

    barrier = pltpu.get_barrier_semaphore()

    def signal(semaphore, other):
        pl.semaphore_signal(
            semaphore, inc=1, device_id={"tile": other}, device_id_type=pl.DeviceIdType.MESH
        )

    odd = lax.rem(me, 2)
    partners = ((me + 1 - 2 * odd, 2 - 2 * odd), (me - 1 + 2 * odd, 2 * odd))
    far = partners[1][0]
    has_far = (far >= 0) & (far < tiles)
    place = lax.rem(me, GATHER)
    inner = (place == 1) | (place == 2)
    slow = inner & (me != 1) & (me != tiles - 2)
    held = has_far & inner & (far != 1) & (far != tiles - 2)
    early_count = jnp.where(has_far, jnp.where(slow, frame_count, FAST_EARLY), 0)

    groups = tiles // GATHER
    leads = place == 0

    def greet(step, carry):
        signal(barrier, lax.rem(me + step * GATHER, tiles))
        return carry

    signal(barrier, partners[0][0])

    @pl.when(has_far)
    def _():
        signal(barrier, far)

    @pl.when(leads)
    def _():
        lax.fori_loop(1, groups, greet, 0)
        for step in range(2, GATHER):
            signal(barrier, me + step)

    value_table[3 * key_count] = jnp.zeros((block_len, model_dim), BF16)
    known = jnp.where(leads, groups - 1, jnp.where(place >= 2, 1, 0))
    pl.semaphore_wait(barrier, 1 + jnp.where(has_far, 1, 0) + known)

    def halo(key):
        part = pl.ds(key * block_len, block_len)
        return pltpu.make_async_remote_copy(
            src_ref=keys_in.at[part], dst_ref=stills.at[1, part],
            send_sem=halo_send.at[key], recv_sem=halo_recv.at[key],
            device_id={"tile": far}, device_id_type=pl.DeviceIdType.MESH,
        )

    def start_halo():
        for key in range(key_count):
            halo(key).start()

    def shared(key, chunk, position):
        block = position * key_count + key
        own = key_count + key
        narrow = pl.ds(pl.multiple_of(chunk * CHUNK, CHUNK), CHUNK)
        pieces = (
            (key_table.at[own, narrow], key_table.at[block, narrow]),
            (value_table.at[own, :, narrow], value_table.at[block, :, narrow]),
        )
        return [
            pltpu.make_async_remote_copy(
                src_ref=src, dst_ref=dst,
                send_sem=near_send.at[kind, key, chunk], recv_sem=near_recv.at[kind, key, chunk],
                device_id={"tile": partners[0][0]}, device_id_type=pl.DeviceIdType.MESH,
            )
            for kind, (src, dst) in enumerate(pieces)
        ]

    @pl.when(has_far & jnp.logical_not(held))
    def _():
        start_halo()

    if exchange:

        @pl.when(jnp.logical_not(leads))
        def _():
            signal(gather_sem, me - place)

    lane = lax.broadcasted_iota(jnp.int32, (piece_len, CHUNK), 1)
    even = lax.rem(lane, PAIR) < head_dim

    def project_queries(half):
        def step(chunk, carry):
            at = pl.ds(pl.multiple_of(chunk * CHUNK, CHUNK), CHUNK)
            tokens = frames[half].reshape(frame_count * piece_len, model_dim)
            q = jnp.dot(tokens, wq[:, at], preferred_element_type=F32)
            q = q * head_dim ** (-0.5)
            for frame in range(frame_count):
                part = q[frame * piece_len : (frame + 1) * piece_len]
                piece = half * frame_count + frame
                queries[piece, 0:piece_len, at] = jnp.where(even, part, 0.0).astype(BF16)
                queries[piece, piece_len : 2 * piece_len, at] = jnp.where(even, 0.0, part).astype(BF16)
            return carry

        lax.fori_loop(0, chunk_count, step, 0)

    def project_stills(source, slot, first, count, share=False):
        def step(chunk, carry):
            at = pl.ds(pl.multiple_of(chunk * CHUNK, CHUNK), CHUNK)
            if share:
                for which in range(2):
                    weight_load(which, chunk).wait()

                @pl.when(chunk == 0)
                def _():
                    for load in loads[1:]:
                        load.start()

            tokens = stills[source, first * block_len : (first + count) * block_len, :]
            k = jnp.dot(tokens, wk[:, at], preferred_element_type=F32).astype(BF16)
            v = jnp.dot(tokens, wv[:, at], preferred_element_type=F32).astype(BF16)
            for key in range(count):
                part = slice(key * block_len, (key + 1) * block_len)
                block = slot * key_count + first + key
                key_table[block, at, :] = k[part].T
                value_table[block, :, at] = v[part]
                if share:
                    for copy in shared(key, chunk, partners[1][1]):
                        copy.start()
            return carry

        lax.fori_loop(0, chunk_count, step, 0)

    loads[0].wait()
    project_stills(0, 1, 0, key_count, share=True)

    def tell(step, carry):
        signal(lead_sem, lax.rem(me + step * GATHER, tiles))
        return carry

    if exchange:

        @pl.when(leads)
        def _():
            pl.semaphore_wait(gather_sem, GATHER - 1)
            lax.fori_loop(1, groups, tell, 0)

    for load in loads[1:]:
        load.wait()

    def project_half(half, carry):
        project_queries(half)
        return carry

    def open_group():
        pl.semaphore_wait(lead_sem, groups - 1)
        for step in range(1, GATHER):
            signal(open_sem, me + step)

    lax.fori_loop(0, 1, project_half, 0)
    if exchange:

        @pl.when(leads & (side == 1))
        def _():
            open_group()

    lax.fori_loop(1, jnp.where(has_far, 2, 1), project_half, 0)
    if exchange:

        @pl.when(leads & (side == 0))
        def _():
            open_group()

    for key in range(key_count):
        for chunk in range(chunk_count):
            for copy in shared(key, chunk, partners[0][1]):
                copy.wait_recv()
    pair_lane = lax.broadcasted_iota(jnp.int32, (piece_len, PAIR), 1) < head_dim

    def send(frame, other, source):
        return pltpu.make_async_remote_copy(
            src_ref=stage.at[frame, other], dst_ref=out.at[frame, source],
            send_sem=send_sem.at[frame, other], recv_sem=recv_sem.at[frame, source],
            device_id={"tile": other}, device_id_type=pl.DeviceIdType.MESH,
        )

    def keep(frame):
        return pltpu.make_async_copy(stage.at[frame, me], out.at[frame, me], own_sem.at[0, frame])

    def place_half(frame, half):
        return pltpu.make_async_copy(
            stage.at[frame, image_half(half)], out.at[frame, :, half_columns(half)],
            own_sem.at[half, frame],
        )

    def attend(piece, keys, values, early=False, late=False):
        ones = [
            jnp.full((block_len, PAIR), jnp.where(block < 3 * key_count, 1.0, 0.0), F32).astype(BF16)
            for block in values
        ]

        def score_block(q, slot, at, scores, most):
            s = jnp.dot(q, key_table[keys[slot], at, :], preferred_element_type=F32)
            scores[:, slot * block_len : (slot + 1) * block_len] = s
            for part in range(block_len // PAIR):
                some = s[:, part * PAIR : (part + 1) * PAIR]
                most = some if most is None else jnp.maximum(most, some)
            return most

        def value_block(slot, at, scores, most, total):
            p = jnp.concatenate(
                [
                    jnp.exp(scores[:, part : part + PAIR] - most).astype(BF16)
                    for part in range(slot * block_len, (slot + 1) * block_len, PAIR)
                ],
                axis=1,
            )
            both = jnp.concatenate([value_table[values[slot], :, at], ones[slot]], axis=1)
            term = jnp.dot(p, both, preferred_element_type=F32)
            return term if total is None else total + term

        def close(most, pair, top):
            most = jnp.broadcast_to(jnp.max(most, axis=1, keepdims=True), top.shape)
            if late:
                most = jnp.maximum(most, early_max[piece, pair])
            top[...] = most

        def columns(pair, width):
            return pl.ds(pl.multiple_of(pair * width, width), width)

        def load_query(pair):
            return queries[piece, :, columns(pair, PAIR)]

        def step(pair, scores, top, next_pair, next_scores, next_top):
            most, total, next_most = top[...], None, None
            q = load_query(next_pair)
            if late:
                scale = jnp.exp(early_max[piece, pair] - most)
                total = early_total[piece, pair] * jnp.concatenate([scale, scale], axis=1)
            for slot in range(len(keys)):
                next_most = score_block(q, slot, columns(next_pair, PAIR), next_scores, next_most)
                total = value_block(slot, columns(pair, PAIR), scores, most, total)
            close(next_most, next_pair, next_top)
            if early:
                early_total[piece, pair] = total
                early_max[piece, pair] = most
                return None
            each = total[:, :PAIR] / total[:, PAIR:]
            both = jnp.where(pair_lane, each[:piece_len], each[piece_len:])
            context[:, columns(pair, PAIR)] = both.astype(BF16)

        most, q = None, load_query(0)
        for slot in range(len(keys)):
            most = score_block(q, slot, columns(0, PAIR), scores_even, most)
        close(most, 0, max_even)

        def group(index, carry):
            for inner_pair in range(0, GROUP, 2):
                pair = index * GROUP + inner_pair
                after = jnp.minimum(pair + 2, pair_count - 1)
                step(pair, scores_even, max_even, pair + 1, scores_odd, max_odd)
                step(pair + 1, scores_odd, max_odd, after, scores_even, max_even)
            return carry

        lax.fori_loop(0, pair_count // GROUP, group, 0)

    def used(frame, slot):
        return slot < counts[0, frame]

    def named(frame, position):
        keys, values = [], []
        for key in range(key_count):
            there = jnp.int32(0)
            for slot in range(slot_count):
                same = (matches[0, frame, slot] == key * 3 + position) & used(frame, slot)
                there = there + jnp.where(same, 1, 0)
            block = position * key_count + key
            keys.append(jnp.where(there > 0, block, key_count))
            values.append(jnp.where(there > 0, block, 3 * key_count))
        return keys, values

    def partner(half, step, source=me):
        top = lax.rem(source // half_tiles, 2)
        other, bit = jnp.where(half == 0, 1 - top, top) * half_tiles, 1
        while bit < half_tiles:
            mine = lax.rem(source // bit, 2)
            moved = 1 - mine if step // bit % 2 else mine
            if 2 * bit == half_tiles:
                moved = jnp.where(half == 0, step // bit % 2, moved)
            other = other + moved * bit
            bit *= 2
        return other

    across = me + 2 - 4 * lax.rem(me // 2, 2)
    relayed = (me == 3) | (me == tiles - 4)
    relays = (me == 1) | (me == tiles - 2)

    def relay_slot(step):
        return step // 4 * 2 + step % 2

    def hand_over(frame, step, other):
        return pltpu.make_async_remote_copy(
            src_ref=stage.at[frame, other], dst_ref=relay.at[frame, relay_slot(step)],
            send_sem=send_sem.at[frame, other], recv_sem=relay_recv.at[frame, relay_slot(step)],
            device_id={"tile": across}, device_id_type=pl.DeviceIdType.MESH,
        )

    def pass_on(frame, step):
        return pltpu.make_async_remote_copy(
            src_ref=relay.at[frame, relay_slot(step)], dst_ref=out.at[frame, across],
            send_sem=relay_send.at[frame, relay_slot(step)], recv_sem=recv_sem.at[frame, across],
            device_id={"tile": partner(0, step, across)}, device_id_type=pl.DeviceIdType.MESH,
        )

    relay_steps = [step for step in range(half_tiles) if step // 2 % 2]

    def waits(step):
        return lax.rem(me // 2, 2) != step // 2 % 2

    def finish_piece(half, frame, hold=None):
        for chunk in range(chunk_count):
            at = slice(chunk * CHUNK, (chunk + 1) * CHUNK)
            update = jnp.dot(context[...], wo[:, at], preferred_element_type=F32)
            mixed = frames[half, frame, :, :, at].reshape(piece_len, CHUNK).astype(F32) + update
            if exchange:
                first = image_half(half) * half_tiles
                for other in range(half_tiles):
                    group = [
                        mixed[row * half_cols + other * cols : row * half_cols + (other + 1) * cols]
                        for row in range(rows)
                    ]
                    stage[frame, first + other, :, at] = jnp.concatenate(group, axis=0).astype(BF16)
            else:
                stage[frame, image_half(half), :, :, at] = mixed.reshape(rows, half_cols, CHUNK).astype(BF16)

        if exchange:
            order = sorted(range(half_tiles), key=lambda step: (2 * step // half_tiles, step // 2 % 2, -step))
            for step in order:
                other = partner(half, step)
                if hold is not None:
                    detour = relayed & (step in relay_steps) & (frame < relay_limit)

                    @pl.when(detour)
                    def _():
                        hand_over(frame, step, other).start()

                    @pl.when(jnp.logical_not(detour | (hold & waits(step) & (frame >= HOLD_FROM))))
                    def _():
                        send(frame, other, me).start()

                    continue
                if step in relay_steps and relay_count:
                    detour = relayed & (half == 0) & (frame < relay_limit)

                    @pl.when(detour)
                    def _():
                        hand_over(frame, step, other).start()

                    @pl.when(jnp.logical_not(detour))
                    def _():
                        send(frame, other, me).start()

                    continue
                if step:
                    send(frame, other, me).start()
                    continue

                @pl.when(half == 0)
                def _():
                    send(frame, other, me).start()

                @pl.when(half != 0)
                def _():
                    keep(frame).start()
        else:
            place_half(frame, half).start()

    def one_piece(piece, carry):
        half = piece // frame_count
        frame = lax.rem(piece, frame_count)
        keys, values = [], []
        for slot in range(slot_count):
            chosen = jnp.where(used(frame, slot), matches[0, frame, slot], matches[0, frame, 0])
            block = lax.rem(chosen, 3) * key_count + lax.div(chosen, 3)
            keys.append(block)
            values.append(jnp.where(used(frame, slot), block, 3 * key_count))

        @pl.when((piece == frame_count) & jnp.logical_not(has_far))
        def _():
            project_queries(1)

        attend(piece, keys, values)
        finish_piece(half, frame)
        if relay_count:

            @pl.when(relays & (piece >= 1) & (piece <= relay_limit))
            def _():
                for step in relay_steps:
                    hand_over(piece - 1, step, me).wait_recv()
                    pass_on(piece - 1, step).start()

        return carry

    def early_piece(piece, carry):
        own_keys, own_values = named(piece, 1)
        near_keys, near_values = named(piece, partners[0][1])
        attend(piece, own_keys + near_keys, own_values + near_values, early=True)

        @pl.when((piece == 0) & held)
        def _():
            start_halo()

        return carry

    def late_piece(piece, carry):
        keys, values = named(piece, partners[1][1])
        attend(piece, keys[-1:], values[-1:], late=True)
        finish_piece(jnp.int32(0), piece, slow & (side == 1))
        return carry

    def middle_piece(key, piece, carry):
        keys, values = named(piece, partners[1][1])
        attend(piece, keys[key : key + 1], values[key : key + 1], early=True, late=True)
        return carry

    def held_sends(frame, carry):
        for step in range(half_tiles):

            @pl.when(waits(step))
            def _():
                send(frame, partner(0, step), me).start()

        return carry

    lax.fori_loop(0, early_count, early_piece, 0)
    if exchange:

        @pl.when(jnp.logical_not(leads))
        def _():
            pl.semaphore_wait(open_sem, 1)


    @pl.when(has_far)
    def _():
        for key in range(key_count):
            halo(key).wait_recv()
            project_stills(1, partners[1][1], key, 1)
            if key < key_count - 1:
                lax.fori_loop(0, early_count, functools.partial(middle_piece, key), 0)

    lax.fori_loop(0, early_count, late_piece, 0)
    if exchange:
        lax.fori_loop(HOLD_FROM, jnp.where(slow & (side == 1), frame_count, HOLD_FROM), held_sends, 0)
    lax.fori_loop(early_count, 2 * frame_count, one_piece, 0)

    @pl.when(has_far)
    def _():
        for key in range(key_count):
            halo(key).wait_send()

    for key in range(key_count):
        for chunk in range(chunk_count):
            for copy in shared(key, chunk, partners[1][1]):
                copy.wait_send()

    if relay_count:

        @pl.when(relays)
        def _():
            for frame in range(relay_count):

                @pl.when(frame < relay_limit)
                def _():
                    for step in relay_steps:
                        pass_on(frame, step).wait_send()

    def finish(frame, carry):
        if exchange:

            def end(step, carry):
                other = lax.rem(me + step, tiles)
                send(frame, other, me).wait_send()
                send(frame, other, other).wait_recv()
                return carry

            lax.fori_loop(1, tiles, end, 0)
            keep(frame).wait()
        else:
            for half in range(2):
                place_half(frame, half).wait()
        return carry

    lax.fori_loop(0, frame_count, finish, 0)


def settle(src, out, held, in_sem, out_sem):
    frame_count, parts = in_sem.shape
    step = src.shape[1] // parts
    places = [(frame, pl.ds(part * step, step)) for frame in range(frame_count) for part in range(parts)]
    fetch = [
        pltpu.make_async_copy(src.at[at], held.at[at], in_sem.at[i // parts, i % parts])
        for i, at in enumerate(places)
    ]
    place = [
        pltpu.make_async_copy(held.at[at], out.at[at], out_sem.at[i // parts, i % parts])
        for i, at in enumerate(places)
    ]
    for copy in fetch:
        copy.start()
    for copy, back in zip(fetch, place):
        copy.wait()
        back.start()
    for back in place:
        back.wait()


def shards(tiles, frames, keyframes, matches, counts, w_query, w_key, w_value, w_out):
    frame_count, row_count, col_count, model_dim = frames.shape
    key_count = keyframes.shape[0]
    block_len = row_count * col_count
    half_cols = col_count // 2
    piece_len = row_count * half_cols
    slots = matches.shape[2]
    cols = col_count // tiles
    exchange = cols % 8 == 0 and tiles & (tiles - 1) == 0 and tiles >= 8
    if exchange:
        out_shape = (frame_count, tiles, row_count * cols, model_dim)
        stage_shape = out_shape
    else:
        out_shape = (frame_count, row_count, col_count, model_dim)
        stage_shape = (frame_count, 2, row_count, half_cols, model_dim)
    weight = pltpu.VMEM((model_dim, model_dim), BF16)
    products = (4 * frame_count + 12 * key_count) * block_len * model_dim * model_dim
    products += 4 * frame_count * slots * block_len * block_len * model_dim
    mixed = pl.pallas_call(
        functools.partial(kernel, tiles, exchange),
        out_shape=jax.ShapeDtypeStruct(out_shape, BF16),
        in_specs=[pl.BlockSpec(memory_space=pl.ANY)] * 8,
        out_specs=pl.BlockSpec(memory_space=pl.ANY),
        scratch_shapes=[
            pltpu.SMEM(matches.shape, jnp.int32),
            pltpu.SMEM(counts.shape, jnp.int32),
            pltpu.VMEM((2, frame_count, row_count, half_cols, model_dim), BF16),
            pltpu.VMEM((2, key_count * block_len, model_dim), BF16),
            weight, weight, weight, weight,
            pltpu.VMEM((2 * frame_count, 2 * piece_len, model_dim), BF16),
            pltpu.VMEM((3 * key_count, model_dim, block_len), BF16),
            pltpu.VMEM((3 * key_count + 1, block_len, model_dim), BF16),
            pltpu.VMEM((piece_len, model_dim), BF16),
            pltpu.VMEM(stage_shape, BF16),
            pltpu.VMEM((min(max(RELAYED), frame_count), 4) + stage_shape[2:], BF16),
            pltpu.VMEM((2 * piece_len, slots * block_len), F32),
            pltpu.VMEM((2 * piece_len, slots * block_len), F32),
            pltpu.VMEM((2 * piece_len, PAIR), F32),
            pltpu.VMEM((2 * piece_len, PAIR), F32),
            pltpu.VMEM((frame_count, HEADS // 2, 2 * piece_len, 2 * PAIR), F32),
            pltpu.VMEM((frame_count, HEADS // 2, 2 * piece_len, PAIR), F32),
            pltpu.SemaphoreType.REGULAR,
            pltpu.SemaphoreType.REGULAR,
            pltpu.SemaphoreType.REGULAR,
            pltpu.SemaphoreType.DMA((7,)),
            pltpu.SemaphoreType.DMA((2, model_dim // CHUNK)),
            pltpu.SemaphoreType.DMA((key_count,)),
            pltpu.SemaphoreType.DMA((key_count,)),
            pltpu.SemaphoreType.DMA((2, key_count, model_dim // CHUNK)),
            pltpu.SemaphoreType.DMA((2, key_count, model_dim // CHUNK)),
            pltpu.SemaphoreType.DMA((min(max(RELAYED), frame_count), 4)),
            pltpu.SemaphoreType.DMA((min(max(RELAYED), frame_count), 4)),
            pltpu.SemaphoreType.DMA((frame_count, tiles)),
            pltpu.SemaphoreType.DMA((frame_count, tiles)),
            pltpu.SemaphoreType.DMA((2, frame_count)),
        ],
        compiler_params=pltpu.CompilerParams(
            collective_id=0, has_side_effects=True, vmem_limit_bytes=60 * 1024 * 1024
        ),
        cost_estimate=pl.CostEstimate(
            flops=products, bytes_accessed=16 * 1024 * 1024,
            transcendentals=frame_count * slots * HEADS * block_len * block_len,
        ),
        name="attend_and_relay",
    )(
        matches, counts, frames,
        keyframes.reshape(key_count * block_len, model_dim),
        w_query, w_key, w_value, w_out,
    )
    if exchange:
        mixed = pl.pallas_call(
            settle,
            out_shape=jax.ShapeDtypeStruct(out_shape, BF16),
            in_specs=[pl.BlockSpec(memory_space=pl.ANY)],
            out_specs=pl.BlockSpec(memory_space=pl.ANY),
            scratch_shapes=[
                pltpu.VMEM(out_shape, BF16),
                pltpu.SemaphoreType.DMA((frame_count, 1)),
                pltpu.SemaphoreType.DMA((frame_count, 1)),
            ],
            name="settle",
        )(mixed)
        return mixed.reshape(frame_count, tiles * row_count, cols, model_dim)
    return lax.all_to_all(mixed, "tile", split_axis=2, concat_axis=1, tiled=True)


def solution(mesh):
    placed = (
        P("clip", "tile", None, None),
        P("clip", "tile", None, None),
        P("tile", "clip", None),
        P("tile", "clip"),
        P(),
        P(),
        P(),
        P(),
    )
    return jax.shard_map(
        functools.partial(shards, mesh.shape["tile"]),
        mesh=mesh, in_specs=placed, out_specs=P("clip", None, "tile", None), check_vma=False,
    )
```
